128 devices in a mesh: alpha: 16 (over y, x), beta: 8 (over z, core).
Axes of the slice: x: 4, y: 4, z: 4, core: 2. Of those that a mesh axis runs over, the one named last changes fastest.
Arguments:
- coefficients: float32 [16384, 8192], P('alpha', 'beta'), may hold values from -6 to 6
- alpha_energy: float32 [16384], P('alpha'), may hold values from -5 to 5
- beta_energy: float32 [8192], P('beta'), may hold values from -5 to 5
- one_body: float32 [18, 18], replicated, may hold values from -3 to 3
- alpha_source: int32 [128, 3], replicated, may hold values from 0 to 127, as said below
- alpha_pair: int32 [128, 3], replicated, may hold values from 0 to 323
- alpha_links: int32 [128, 3, 128], replicated, may hold values from -128 to 128, as said below
- beta_source: int32 [64, 3], replicated, may hold values from 0 to 63, as said below
- beta_pair: int32 [64, 3], replicated, may hold values from 0 to 323
- beta_links: int32 [64, 3, 128], replicated, may hold values from -128 to 128, as said below
Outputs:
- sigma: float32 [16384, 8192], P('alpha', 'beta')
The draws below stay inside these ranges and needn't reach their ends.
Inputs may be any that keep to these rules, and one draw needn't show every extreme that they name: `alpha_source`: entry (g, k) names a block that feeds alpha block g. Among the entries of the 8 blocks of one aligned group, at most 2 name blocks of one aligned group of 8 source blocks, and some such pair of groups has exactly 2. `beta_source`: entry (g, k) names a block that feeds beta block g. Among the entries of the 8 blocks of one aligned group, at most 3 name blocks of one aligned group of 8 source blocks, and some such pair of groups has exactly 3. `alpha_links`: 0 where the excitation removes the target string; else the sign times one plus the string's position in the source block. `beta_links`: 0 where the excitation removes the target string; else the sign times one plus the string's position in the source block.
All inputs are finite; a program needn't handle non-finite values.
Results may differ from the reference program's by a relative error of at most 0.0003.
Values sent between devices are 32-bit elements; how exact they have to be, the bound alone decides.
A program may use at most 192 MiB of HBM per device.

```python
import jax
import jax.numpy as jnp
from jax import lax

NORB = 18
NPAIR = 324
SB = 128
ABLK = 8
BBLK = 8
NLA = 3
NLB = 3
NA_BLK = 128
NB_BLK = 64
NA = 16384
NB = 8192
CAP = 2
CAPB = 3


def source_table(base_key, blocks_dev, lists, devices, capacity):
    entries = blocks_dev * lists
    device_keys = jax.random.split(base_key, devices)

    def one_device(device_key):
        first_key, second_key = jax.random.split(device_key)
        order = jax.random.permutation(first_key, devices * capacity)[:entries]
        owners = order // capacity
        inner = jax.random.randint(second_key, (entries,), 0, blocks_dev)
        return owners * blocks_dev + inner
    return jax.vmap(one_device)(device_keys).reshape(devices * blocks_dev, lists).astype(jnp.int32)


def link_values(base_key, shape):
    first_key, second_key = jax.random.split(base_key)
    sign_draw = jax.random.randint(first_key, shape, -1, 2)
    anchor = jax.random.randint(second_key, shape, 0, SB)
    return (sign_draw * (anchor + 1)).astype(jnp.int32)


def draw_alpha_source(key, part):
    key = jax.random.fold_in(key, 1)
    return source_table(key, ABLK, NLA, NA_BLK // ABLK, CAP)


def draw_beta_source(key, part):
    key = jax.random.fold_in(key, 2)
    return source_table(key, BBLK, NLB, NB_BLK // BBLK, CAPB)


def draw_alpha_links(key, part):
    key = jax.random.fold_in(key, 3)
    return link_values(key, (NA_BLK, NLA, SB))


def draw_beta_links(key, part):
    key = jax.random.fold_in(key, 4)
    return link_values(key, (NB_BLK, NLB, SB))


def set_ends(drawn, own_key, smallest, high):
    extent = drawn.shape
    place = [jax.random.randint(jax.random.fold_in(own_key, axis), (), 0, extent[axis]) for axis in range(len(extent))]
    drawn = drawn.at[tuple(place)].set(smallest)
    longest = extent.index(max(extent))
    place[longest] = (place[longest] + 1) % extent[longest]
    return drawn.at[tuple(place)].set(high)


def steps_of(own_key, shape, cuts, smallest, largest):
    level = 1.0
    for axis_at, shards_of in cuts:
        heights = jax.random.uniform(jax.random.fold_in(jax.random.fold_in(own_key, 6), axis_at), (shards_of,), jnp.float32, smallest / len(cuts), largest / len(cuts))
        level = level * jnp.repeat(jnp.exp(heights), shape[axis_at] // shards_of).reshape((-1,) + (1,) * (len(shape) - 1 - axis_at))
    return level


def centred(key, shape, scale, most, pieces=(), kind=jnp.bfloat16):
    gain = steps_of(key, shape, pieces, -0.22, 0.18) if pieces else 1.0
    array = jax.random.normal(key, shape, jnp.float32) * scale * gain
    return jnp.minimum(jnp.maximum(array, -most), most).astype(kind)


def setup_inputs(seed: int = 0) -> dict:
    arg_keys = jax.random.split(jax.random.key(seed), 11)
    return {
        "coefficients": centred(arg_keys[0], (NA, NB), 1.0, 6.0, ((0, 16), (1, 8)), jnp.float32),
        "alpha_energy": centred(arg_keys[1], (NA,), 1.0, 5.0, ((0, 16),), jnp.float32),
        "beta_energy": centred(arg_keys[2], (NB,), 1.0, 5.0, ((0, 8),), jnp.float32),
        "one_body": centred(arg_keys[3], (NORB, NORB), 0.5, 3.0, (), jnp.float32),
        "alpha_source": draw_alpha_source(jax.random.fold_in(arg_keys[10], 71), 0),
        "alpha_pair": set_ends(jax.random.randint(arg_keys[5], (NA_BLK, NLA), 0, NPAIR), jax.random.fold_in(arg_keys[5], 1), 0, NPAIR - 1).astype(jnp.int32),
        "alpha_links": draw_alpha_links(jax.random.fold_in(arg_keys[10], 71), 0),
        "beta_source": draw_beta_source(jax.random.fold_in(arg_keys[10], 71), 0),
        "beta_pair": set_ends(jax.random.randint(arg_keys[8], (NB_BLK, NLB), 0, NPAIR), jax.random.fold_in(arg_keys[8], 1), 0, NPAIR - 1).astype(jnp.int32),
        "beta_links": draw_beta_links(jax.random.fold_in(arg_keys[10], 71), 0),
    }


def decode(links, pairs, one_body):
    flat_table = one_body.reshape(-1)
    hvalue = flat_table[pairs]
    weights = jnp.sign(links).astype(jnp.float32) * hvalue[..., None]
    anchor = jnp.maximum(jnp.abs(links) - 1, 0).astype(jnp.int32)
    return weights, anchor


def reference(coefficients, alpha_energy, beta_energy, one_body, alpha_source, alpha_pair, alpha_links, beta_source, beta_pair, beta_links):
    alpha_weights, alpha_anchor = decode(alpha_links, alpha_pair, one_body)
    alpha_index = (alpha_source[:, :, None] * SB + alpha_anchor).astype(jnp.int32)

    def alpha_block(inputs):
        index_rows, weights = inputs
        picked = coefficients[index_rows]
        return jnp.sum(picked * weights[..., None], axis=0)

    alpha_term = lax.map(alpha_block, (alpha_index, alpha_weights)).reshape(NA_BLK * SB, NB_BLK * SB)
    beta_weights, beta_anchor = decode(beta_links, beta_pair, one_body)
    beta_index = (beta_source[:, :, None] * SB + beta_anchor).astype(jnp.int32)

    def beta_block(inputs):
        index_cols, weights = inputs
        picked = coefficients[:, index_cols]
        return jnp.sum(picked * weights[None], axis=1)

    beta_blocks = lax.map(beta_block, (beta_index, beta_weights))
    beta_term = jnp.transpose(beta_blocks, (1, 0, 2)).reshape(NA_BLK * SB, NB_BLK * SB)
    return (alpha_energy[:, None] + beta_energy[None, :]) * coefficients + alpha_term + beta_term
```

```python
import jax
import jax.numpy as jnp
from jax import lax
from jax.experimental import pallas as pl
from jax.experimental.pallas import tpu as pltpu
from jax.sharding import PartitionSpec as P

MESH = pl.DeviceIdType.MESH
F32, BF16 = jnp.float32, jnp.bfloat16
SB = 128
NCH = 4
NZ = 8


def kernel(
    coef,
    asrc,
    apair,
    alinks,
    bsrc,
    bpair,
    blinks,
    table,
    out,
    gx,
    gy,
    gz,
    stage,
    stage_b,
    split,
    split_b,
    part,
    far,
    near,
    core_out,
    core_in,
    hot,
    hot_b,
    g_send,
    g_recv,
    z_send,
    z_recv,
    r_send,
    r_recv,
    c_send,
    c_recv,
    l_sem,
):
    a = lax.axis_index("alpha")
    b = lax.axis_index("beta")
    y, x, z, core = a // 4, a % 4, b // 2, b % 2

    def step(axis, d):
        s = 1 if d == 0 else 3
        if axis == "x":
            return (y * 4 + (x + s) % 4, b)
        if axis == "y":
            return (((y + s) % 4) * 4 + x, b)
        return (a, ((z + s) % 4) * 2 + core)

    partner = (a, z * 2 + 1 - core)

    def cols(h, c):
        return pl.ds(pl.multiple_of(h * 512 + c * SB, SB), SB)

    axes = ("x", "y")
    bufs = (gx, gy)

    def own(h, c, d):
        return pltpu.make_async_remote_copy(
            src_ref=coef.at[:, cols(h, c)],
            dst_ref=bufs[h].at[2 if d == 0 else 0, c],
            send_sem=g_send.at[h, 0, c, d],
            recv_sem=g_recv.at[h, 0, c, d],
            device_id=step(axes[h], d),
            device_id_type=MESH,
        )

    def relay(h, c, d):
        rows = pl.ds(d * 512, 512)
        return pltpu.make_async_remote_copy(
            src_ref=bufs[h].at[2 if d == 0 else 0, c, rows],
            dst_ref=bufs[h].at[1, c, rows],
            send_sem=g_send.at[h, 1, c, d],
            recv_sem=g_recv.at[h, 1, c, d],
            device_id=step(axes[h], d),
            device_id_type=MESH,
        )

    def own_z(c, d):
        rows = pl.ds(pl.multiple_of(c * SB, SB), SB)
        return pltpu.make_async_remote_copy(
            src_ref=coef.at[rows],
            dst_ref=gz.at[2 if d == 0 else 0, rows],
            send_sem=z_send.at[0, c, d],
            recv_sem=z_recv.at[0, c, d],
            device_id=step("z", d),
            device_id_type=MESH,
        )

    def relay_z(c, d):
        rows = pl.ds(pl.multiple_of(c * SB + d * 64, 64), 64)
        return pltpu.make_async_remote_copy(
            src_ref=gz.at[2 if d == 0 else 0, rows],
            dst_ref=gz.at[1, rows],
            send_sem=z_send.at[1, c, d],
            recv_sem=z_recv.at[1, c, d],
            device_id=step("z", d),
            device_id_type=MESH,
        )

    def send_far(h, c, d):
        return pltpu.make_async_remote_copy(
            src_ref=part.at[h, c, 1, pl.ds(d * 512, 512)],
            dst_ref=far.at[h, c, d],
            send_sem=r_send.at[h, 0, c, d],
            recv_sem=r_recv.at[h, 0, c, d],
            device_id=step(axes[1 - h], d),
            device_id_type=MESH,
        )

    def send_near(h, c, d):
        return pltpu.make_async_remote_copy(
            src_ref=part.at[h, c, 0 if d == 0 else 2],
            dst_ref=near.at[h, c, d],
            send_sem=r_send.at[h, 1, c, d],
            recv_sem=r_recv.at[h, 1, c, d],
            device_id=step(axes[1 - h], d),
            device_id_type=MESH,
        )

    def send_core(c):
        return pltpu.make_async_remote_copy(
            src_ref=core_out.at[c],
            dst_ref=core_in.at[c],
            send_sem=c_send.at[c],
            recv_sem=c_recv.at[c],
            device_id=partner,
            device_id_type=MESH,
        )

    def integral(pair):
        p = pair // 18
        return table[p, pair - p * 18]

    def reader(h, q):
        if h == 0:
            return ((y + q) % 4) * 4 + x
        return y * 4 + (x + q) % 4

    def signed_hot(row):
        s = lax.broadcasted_iota(jnp.int32, (SB, SB), 0)
        return jnp.where(jnp.abs(row) - 1 == s, jnp.where(row > 0, 1.0, -1.0), 0.0)

    def build_alpha(h):
        def body(n, _):
            g = reader(h, n // 8) * 8 + n % 8
            for k in range(3):
                row = alinks[k, pl.ds(g, 1), :]
                hot[h, n * 3 + k] = signed_hot(row).T.astype(BF16)
            return 0

        lax.fori_loop(0, 32, body, 0)

    def build_beta():
        def body(n, _):
            g = (z * 2 + (core + n // 8) % 2) * 8 + n % 8
            for k in range(3):
                row = blinks[k, pl.ds(g, 1), :]
                hot_b[n * 3 + k] = signed_hot(row).astype(BF16)
            return 0

        lax.fori_loop(0, 16, body, 0)

    def pieces(v):
        hi = v.astype(BF16)
        return hi, (v - hi.astype(F32)).astype(BF16)

    def compute_alpha(h, c):
        copies = [pltpu.make_async_copy(coef.at[:, cols(h, c)], stage.at[0], l_sem.at[0])]
        for q in range(3):
            copies.append(
                pltpu.make_async_copy(bufs[h].at[q, c], stage.at[q + 1], l_sem.at[q + 1])
            )
        for cp in copies:
            cp.start()
        for cp in copies:
            cp.wait()

        def split_body(n, _):
            rows = pl.ds(pl.multiple_of((n % 8) * SB, SB), SB)
            hi, lo = pieces(stage[n // 8, rows, :])
            split[n, 0:SB, :] = hi
            split[n, SB : 2 * SB, :] = lo
            return 0

        lax.fori_loop(0, 32, split_body, 0, unroll=2)

        def target(n):
            g = reader(h, n // 8) * 8 + n % 8
            acc = jnp.zeros((SB, SB), F32)
            for k in range(3):
                src = asrc[k, g]
                sy, sx = (src >> 5) & 3, (src >> 3) & 3
                if h == 0:
                    here, q = sy == y, (sx - x) & 3
                else:
                    here, q = sx == x, (sy - y) & 3
                weight = jnp.where(here, integral(apair[k, g]), 0.0)
                w = hot[h, n * 3 + k]
                acc += weight * jnp.dot(
                    jnp.concatenate([w, w], axis=1),
                    split[q * 8 + (src & 7)],
                    preferred_element_type=F32,
                )
            return acc

        def mine(n, _):
            rows = pl.ds(pl.multiple_of(n * SB, SB), SB)
            out[rows, cols(h, c)] += target(n)
            return 0

        lax.fori_loop(0, 8, mine, 0, unroll=4)

        def others(n, _):
            rows = pl.ds(pl.multiple_of((n % 8) * SB, SB), SB)
            part[h, c, n // 8 - 1, rows, :] = target(n)
            return 0

        lax.fori_loop(8, 32, others, 0, unroll=4)

    def compute_beta(c):
        rows = pl.ds(pl.multiple_of(c * SB, SB), SB)
        copies = [pltpu.make_async_copy(coef.at[rows], stage_b.at[0], l_sem.at[4])]
        for q in range(3):
            copies.append(
                pltpu.make_async_copy(gz.at[q, rows], stage_b.at[q + 1], l_sem.at[q + 5])
            )
        for cp in copies:
            cp.start()
        for cp in copies:
            cp.wait()

        def split_body(n, _):
            hi, lo = pieces(stage_b[n // 8, :, pl.ds(pl.multiple_of((n % 8) * SB, SB), SB)])
            split_b[n, :, 0:SB] = hi
            split_b[n, :, SB : 2 * SB] = lo
            return 0

        lax.fori_loop(0, 32, split_body, 0, unroll=2)

        def target(n):
            g = (z * 2 + (core + n // 8) % 2) * 8 + n % 8
            acc = jnp.zeros((SB, SB), F32)
            for k in range(3):
                src = bsrc[k, g]
                sz, sc = (src >> 4) & 3, (src >> 3) & 1
                weight = jnp.where(sc == core, integral(bpair[k, g]), 0.0)
                w = hot_b[n * 3 + k]
                acc += weight * jnp.dot(
                    split_b[((sz - z) & 3) * 8 + (src & 7)],
                    jnp.concatenate([w, w], axis=0),
                    preferred_element_type=F32,
                )
            return acc

        def mine(n, _):
            at = pl.ds(pl.multiple_of(n * SB, SB), SB)
            out[rows, at] += target(n)
            return 0

        lax.fori_loop(0, 8, mine, 0, unroll=4)

        def others(n, _):
            at = pl.ds(pl.multiple_of((n - 8) * SB, SB), SB)
            core_out[c, :, at] = target(n)
            return 0

        lax.fori_loop(8, 16, others, 0, unroll=4)

    def pass_on(h, c):
        for d in range(2):
            send_far(h, c, d).wait_recv()
            slot = 0 if d == 0 else 2

            def body(n, _):
                rows = pl.ds(pl.multiple_of(d * 512 + n * SB, SB), SB)
                part[h, c, slot, rows, :] += far[h, c, d, pl.ds(pl.multiple_of(n * SB, SB), SB), :]
                return 0

            lax.fori_loop(0, 4, body, 0)
            send_near(h, c, d).start()

    def finish(h, c):
        for d in range(2):
            send_near(h, c, d).wait_recv()

        def body(n, _):
            rows = pl.ds(pl.multiple_of(n * SB, SB), SB)
            out[rows, cols(h, c)] += near[h, c, 0, rows, :] + near[h, c, 1, rows, :]
            return 0

        lax.fori_loop(0, 8, body, 0)

    def finish_core(c):
        send_core(c).wait_recv()
        rows = pl.ds(pl.multiple_of(c * SB, SB), SB)
        out[rows, :] += core_in[c]

    barrier = pltpu.get_barrier_semaphore()
    for axis in ("x", "y", "z"):
        for d in range(2):
            pl.semaphore_signal(barrier, inc=1, device_id=step(axis, d), device_id_type=MESH)
    pl.semaphore_signal(barrier, inc=1, device_id=partner, device_id_type=MESH)
    pl.semaphore_wait(barrier, 7)

    for c in range(2):
        for d in range(2):
            own(0, c, d).start()
            own(1, c, d).start()
            own_z(c, d).start()

    out[...] = jnp.zeros_like(out)
    build_alpha(0)

    def move_on(c):
        for h in range(2):
            for d in range(2):
                own(h, c, d).wait_recv()
                relay(h, c, d).start()

        @pl.when(c < NCH - 2)
        def _():
            for h in range(2):
                for d in range(2):
                    own(h, c + 2, d).start()

    def move_on_z(c):
        for d in range(2):
            own_z(c, d).wait_recv()
            relay_z(c, d).start()

        @pl.when(c < NZ - 2)
        def _():
            for d in range(2):
                own_z(c + 2, d).start()

    move_on(0)
    move_on_z(0)
    build_alpha(1)
    build_beta()

    def loop(t, _):
        @pl.when(t < NCH - 1)
        def _():
            move_on(t + 1)

        @pl.when(t < NZ - 1)
        def _():
            move_on_z(t + 1)

        @pl.when(t < NCH)
        def _():
            for h in range(2):
                for d in range(2):
                    relay(h, t, d).wait_recv()
                compute_alpha(h, t)

        @pl.when(t == 2)
        def _():
            for c in range(2):
                for h in range(2):
                    for d in range(2):
                        send_far(h, c, d).start()

        @pl.when((t >= 2) & (t < NCH))
        def _():
            for h in range(2):
                for d in range(2):
                    send_far(h, t, d).start()

        @pl.when((t >= 3) & (t < 7))
        def _():
            for h in range(2):
                pass_on(h, t - 3)

        for d in range(2):
            relay_z(t, d).wait_recv()
        compute_beta(t)
        send_core(t).start()

        @pl.when(t >= 6)
        def _():
            for h in range(2):
                finish(h, t - 6)

        @pl.when(t >= 1)
        def _():
            finish_core(t - 1)

        return 0

    lax.fori_loop(0, NZ, loop, 0)
    finish_core(NZ - 1)

    def last(c, _):
        for h in range(2):
            finish(h, c)
        return 0

    lax.fori_loop(2, NCH, last, 0)

    def drain(c, _):
        for h in range(2):
            for d in range(2):
                own(h, c, d).wait_send()
                relay(h, c, d).wait_send()
                send_far(h, c, d).wait_send()
                send_near(h, c, d).wait_send()
        return 0

    lax.fori_loop(0, NCH, drain, 0)

    def drain_z(c, _):
        for d in range(2):
            own_z(c, d).wait_send()
            relay_z(c, d).wait_send()
        send_core(c).wait_send()
        return 0

    lax.fori_loop(0, NZ, drain_z, 0)


def couplings(coef, one_body, asrc, apair, alinks, bsrc, bpair, blinks):
    hbm = pl.BlockSpec(memory_space=pl.ANY)
    vmem = pl.BlockSpec(memory_space=pltpu.VMEM)
    smem = pl.BlockSpec(memory_space=pltpu.SMEM)
    dma = pltpu.SemaphoreType.DMA
    return pl.pallas_call(
        kernel,
        out_shape=[
            jax.ShapeDtypeStruct((1024, 1024), F32),
            jax.ShapeDtypeStruct((3, NCH, 1024, SB), F32),
            jax.ShapeDtypeStruct((3, NCH, 1024, SB), F32),
            jax.ShapeDtypeStruct((3, 1024, 1024), F32),
        ],
        in_specs=[hbm, smem, smem, vmem, smem, smem, vmem, smem],
        out_specs=[vmem, hbm, hbm, hbm],
        scratch_shapes=[
            pltpu.VMEM((4, 1024, SB), F32),
            pltpu.VMEM((4, SB, 1024), F32),
            pltpu.VMEM((32, 2 * SB, SB), BF16),
            pltpu.VMEM((32, SB, 2 * SB), BF16),
            pltpu.VMEM((2, NCH, 3, 1024, SB), F32),
            pltpu.VMEM((2, NCH, 2, 512, SB), F32),
            pltpu.VMEM((2, NCH, 2, 1024, SB), F32),
            pltpu.VMEM((NZ, SB, 1024), F32),
            pltpu.VMEM((NZ, SB, 1024), F32),
            pltpu.VMEM((2, 96, SB, SB), BF16),
            pltpu.VMEM((48, SB, SB), BF16),
            dma((2, 2, NCH, 2)),
            dma((2, 2, NCH, 2)),
            dma((2, NZ, 2)),
            dma((2, NZ, 2)),
            dma((2, 2, NCH, 2)),
            dma((2, 2, NCH, 2)),
            dma((NZ,)),
            dma((NZ,)),
            dma((8,)),
        ],
        compiler_params=pltpu.CompilerParams(
            collective_id=0, has_side_effects=True, vmem_limit_bytes=60 * 2**20
        ),
        name="couplings",
    )(coef, asrc, apair, alinks, bsrc, bpair, blinks, one_body)[0]


def on_device(
    coefficients,
    alpha_energy,
    beta_energy,
    one_body,
    alpha_source,
    alpha_pair,
    alpha_links,
    beta_source,
    beta_pair,
    beta_links,
):
    terms = couplings(
        coefficients,
        one_body,
        alpha_source.T,
        alpha_pair.T,
        alpha_links.transpose(1, 0, 2),
        beta_source.T,
        beta_pair.T,
        beta_links.transpose(1, 0, 2),
    )
    return (alpha_energy[:, None] + beta_energy[None, :]) * coefficients + terms


def solution(mesh):
    in_specs = (P("alpha", "beta"), P("alpha"), P("beta"), P(), P(), P(), P(), P(), P(), P())
    out_specs = P("alpha", "beta")
    return jax.shard_map(
        on_device, mesh=mesh, in_specs=in_specs, out_specs=out_specs, check_vma=False
    )
```

```python
import numpy as np

import jax
import jax.numpy as jnp
from jax import lax
from jax.experimental import pallas as pl
from jax.experimental.pallas import tpu as pltpu
from jax.sharding import PartitionSpec as P

MESH = pl.DeviceIdType.MESH
F32, BF16 = jnp.float32, jnp.bfloat16
SB = 128
NCH = 4
NZ = 8
SLOTS = 13

LINK = (1, 3, 4, 12)


def link_of(o, i):
    return (o + i) % 4


def spans(links):
    found = [0]
    for link in links:
        found = found + [v ^ LINK[link] for v in found]
    return found


def reader_masks(o):
    last, third = LINK[link_of(o, 3)], LINK[link_of(o, 2)]
    return (0, last, third, third ^ last)


HOT_SLOT = {m: i for i, m in enumerate(sorted({m for o in range(4) for m in reader_masks(o)}))}


def message_masks():
    shape = (4, 16, 16)
    two_readers, two_sources = np.zeros(shape, np.float32), np.zeros(shape, np.float32)
    three_sources, three_readers = np.zeros(shape, np.float32), np.zeros(shape, np.float32)
    for o in range(4):
        l1, l2, l3, l4 = (link_of(o, i) for i in range(4))
        for n in range(16):
            for v in spans((l3, l4)):
                two_readers[o, n, n ^ LINK[l2] ^ v] = 1
            for v in spans((l1,)):
                two_sources[o, n, n ^ v] = 1
            for v in spans((l1, l2)):
                three_sources[o, n, n ^ v] = 1
            for v in spans((l4,)):
                three_readers[o, n, n ^ LINK[l3] ^ v] = 1
    return two_readers, two_sources, three_sources, three_readers


def rows_of_device():
    pick = np.zeros((16, 2, 2, 4, 4, 16), np.float32)
    for n in range(16):
        for stage in range(2):
            for o in range(4):
                pick[n, stage, 0, o, o, n] = 1
                pick[n, stage, 1, o, o, n ^ LINK[link_of(o, stage + 1)]] = 1
    return pick.reshape(16, 2, 8, 64)


def message_tables(source, me):
    two_readers, two_sources, three_sources, three_readers = (
        jnp.asarray(m.reshape(64, 16)) for m in message_masks()
    )
    blocks = jnp.arange(128, dtype=jnp.int32)
    by_reader = source.reshape(16, 24)
    named = jnp.any(by_reader[:, :, None] == blocks, axis=1).astype(F32)
    devices = jnp.arange(16, dtype=jnp.int32)
    fed = jnp.any((source >> 3)[:, :, None] == devices, axis=1).astype(F32)
    two = (jnp.dot(two_readers, named) > 0.5) & (jnp.repeat(two_sources, 8, axis=1) > 0.5)
    three = (jnp.dot(three_sources, fed.T) > 0.5) & (jnp.repeat(three_readers, 8, axis=1) > 0.5)
    masks = jnp.stack([two, three]).astype(F32)
    most = jnp.max(jnp.sum(masks, axis=2))
    pick = lax.dynamic_index_in_dim(jnp.asarray(rows_of_device()), me, 0, keepdims=False)
    mine = jnp.einsum("trm,tmb->trb", pick, masks)
    before = jnp.asarray(np.triu(np.ones((128, 128), np.float32), 1))
    rank = jnp.einsum("trb,bc->trc", mine, before).astype(jnp.int32)
    here = mine > 0.5
    slots = jnp.arange(16, dtype=jnp.int32)
    chosen = here[:, :4, None, :] & (rank[:, :4, None, :] == slots[:, None])
    sent = jnp.sum(jnp.where(chosen, blocks, 0), axis=3)
    got = jnp.where(here[:, 4:], jnp.minimum(rank[:, 4:], SLOTS - 1), -1)
    return sent, got, most


def named_kernel(
    coef,
    asrc,
    apair,
    alinks_hbm,
    bsrc,
    bpair,
    blinks_hbm,
    table,
    sent,
    got,
    out_hbm,
    got1,
    got2,
    gz,
    gc,
    gf,
    got_b,
    out,
    alinks,
    blinks,
    stage,
    split,
    held,
    pack,
    part3,
    *rest,
):
    got3, rest = rest[:8], rest[8:]
    part4, got4, stage_b, split_b, part_b, hot, hot_b, s_sem, r_sem, zs_sem, zr_sem, l_sem = rest
    a = lax.axis_index("alpha")
    b = lax.axis_index("beta")
    y, x, z, core = a // 4, a % 4, b // 2, b % 2

    def over(place, link):
        py, px = place
        if link == 0:
            return (py, px + 1 - 2 * (px % 2))
        if link == 1:
            return (py, 3 - px)
        if link == 2:
            return (py + 1 - 2 * (py % 2), px)
        return (3 - py, px)

    def index(place):
        return place[0] * 4 + place[1]

    def peer(link):
        return (index(over((y, x), link)), b)

    def over_z(pair):
        return z + 1 - 2 * (z % 2) if pair == 0 else 3 - z

    partner = (a, z * 2 + 1 - core)

    def choose(o, values):
        return jnp.where(
            o == 0, values[0], jnp.where(o == 1, values[1], jnp.where(o == 2, values[2], values[3]))
        )

    def each(o, act):
        for k in range(4):

            @pl.when(o == k)
            def _(k=k):
                act(k)

    def columns(w, o):
        return pl.ds(pl.multiple_of((w * 4 + o) * SB, SB), SB)

    def block(n):
        return pl.ds(pl.multiple_of(n * SB, SB), SB)

    def send(i, w, o):
        ch = w * 4 + o
        src = (coef.at[:, :, columns(w, o)], pack.at[ch], part3.at[ch], part4.at[ch])[i]
        dst = got3[ch] if i == 2 else (got1, got2, None, got4)[i].at[ch]
        return pltpu.make_async_remote_copy(
            src_ref=src,
            dst_ref=dst,
            send_sem=s_sem.at[i, ch],
            recv_sem=r_sem.at[i, ch],
            device_id=peer(link_of(o, i)),
            device_id_type=MESH,
        )

    def blocks_b(h, c):
        return pl.ds(h * 4 + c * 2, 2)

    def send_z(h, c):
        return pltpu.make_async_remote_copy(
            src_ref=coef.at[blocks_b(h, c)],
            dst_ref=gz.at[blocks_b(h, c)],
            send_sem=zs_sem.at[0, h, c],
            recv_sem=zr_sem.at[0, h, c],
            device_id=(a, over_z(h) * 2 + core),
            device_id_type=MESH,
        )

    def send_c(h, c):
        return pltpu.make_async_remote_copy(
            src_ref=coef.at[blocks_b(h, c)],
            dst_ref=gc.at[blocks_b(h, c)],
            send_sem=zs_sem.at[1, h, c],
            recv_sem=zr_sem.at[1, h, c],
            device_id=partner,
            device_id_type=MESH,
        )

    def send_f(h, c):
        return pltpu.make_async_remote_copy(
            src_ref=gz.at[blocks_b(h, c)],
            dst_ref=gf.at[blocks_b(h, c)],
            send_sem=zs_sem.at[2, h, c],
            recv_sem=zr_sem.at[2, h, c],
            device_id=partner,
            device_id_type=MESH,
        )

    def send_b(h, c):
        return pltpu.make_async_remote_copy(
            src_ref=part_b.at[h, c],
            dst_ref=got_b.at[blocks_b(h, c)],
            send_sem=zs_sem.at[3, h, c],
            recv_sem=zr_sem.at[3, h, c],
            device_id=(a, over_z(1 - h) * 2 + core),
            device_id_type=MESH,
        )

    def integral(pair):
        p = pair // 18
        return table[p, pair - p * 18]

    def signed_hot(row):
        s = lax.broadcasted_iota(jnp.int32, (SB, SB), 0)
        return jnp.where(jnp.abs(row) - 1 == s, jnp.where(row > 0, 1.0, -1.0), 0.0)

    def pieces(v):
        hi = v.astype(BF16)
        return hi, (v - hi.astype(F32)).astype(BF16)

    def build_alpha():
        for mask, slot in HOT_SLOT.items():
            place = (y, x)
            for link in range(4):
                if mask & 3 == LINK[link] or mask & 12 == LINK[link]:
                    place = over(place, link)
            if mask & 3 == 2:
                place = over(over(place, 0), 1)
            if mask & 12 == 8:
                place = over(over(place, 2), 3)
            reader = index(place)

            def body(n, _, slot=slot, reader=reader):
                for k in range(3):
                    row = alinks[k, pl.ds(reader * 8 + n, 1), :]
                    hot[slot, n * 3 + k] = signed_hot(row).T.astype(BF16)
                return 0

            lax.fori_loop(0, 8, body, 0, unroll=4)

    def build_beta():
        for slot in range(3):
            reader = (z if slot == 0 else over_z(slot - 1)) * 2 + core

            def body(n, _, slot=slot, reader=reader):
                for k in range(3):
                    row = blinks[k, pl.ds(reader * 8 + n, 1), :]
                    hot_b[slot, n * 3 + k] = signed_hot(row).astype(BF16)
                return 0

            lax.fori_loop(0, 8, body, 0, unroll=4)

    def load(w, o, buf, second):
        copies = [
            pltpu.make_async_copy(
                coef.at[:, :, columns(w, o)], stage.at[buf, pl.ds(0, 8)], l_sem.at[buf, 0]
            ),
            pltpu.make_async_copy(
                got1.at[w * 4 + o], stage.at[buf, pl.ds(8, 8)], l_sem.at[buf, 1]
            ),
        ]
        if second:
            copies.append(
                pltpu.make_async_copy(
                    got2.at[w * 4 + o], stage.at[buf, pl.ds(16, SLOTS)], l_sem.at[buf, 2]
                )
            )
        return copies

    def start_load(w, o, second):
        for cp in load(w, o, o % 2, second):
            cp.start()

    def wait_load(w, o, second):
        for cp in load(w, o, o % 2, second):
            cp.wait()

    def ready(w, o, i):
        def first(k):
            if k == 0:
                send(i, w, 0).wait_recv()
                start_load(w, 0, i == 1)
            if k < 3:
                send(i, w, k + 1).wait_recv()
                start_load(w, k + 1, i == 1)
            wait_load(w, k, i == 1)

        each(o, first)

    def second_exchange(w):
        def body(o, _):
            ready(w, o, 0)
            buf = o % 2

            def hold(n, _):
                held[n] = stage[buf, n]
                return 0

            lax.fori_loop(0, 16, hold, 0, unroll=4)

            def fill(s, _):
                wanted = sent[0, o, s]
                at = jnp.where((wanted >> 3) == a, 0, 8) + (wanted & 7)
                pack[w * 4 + o, s] = held[at]
                return 0

            lax.fori_loop(0, SLOTS, fill, 0)
            each(o, lambda k: send(1, w, k).start())
            return 0

        lax.fori_loop(0, 4, body, 0)

    def third_exchange(w):
        def body(o, _):
            ready(w, o, 1)
            buf = o % 2
            ch = w * 4 + o
            m1 = choose(o, [LINK[link_of(k, 0)] for k in range(4)])
            m2 = choose(o, [LINK[link_of(k, 1)] for k in range(4)])
            m3 = choose(o, [LINK[link_of(k, 2)] for k in range(4)])
            hots = [
                choose(o, [HOT_SLOT[reader_masks(k)[role]] for k in range(4)]) for role in range(4)
            ]

            def split_body(n, _):
                hi, lo = pieces(stage[buf, n])
                split[n, 0:SB, :] = hi
                split[n, SB : 2 * SB, :] = lo
                return 0

            lax.fori_loop(0, 16 + SLOTS, split_body, 0, unroll=8)

            def target(g, slot):
                acc = jnp.zeros((SB, SB), F32)
                for k in range(3):
                    src = asrc[k, g]
                    apart = (src >> 3) ^ a
                    inner = src & 7
                    over_two = (apart == m2) | (apart == (m1 ^ m2))
                    here = over_two | (apart == 0) | (apart == m1)
                    arrived = 16 + jnp.maximum(got[0, o, src], 0)
                    at = jnp.where(over_two, arrived, jnp.where(apart == m1, 8 + inner, inner))
                    weight = jnp.where(here, integral(apair[k, g]), 0.0)
                    w_k = hot[slot, (g & 7) * 3 + k]
                    acc += weight * jnp.dot(
                        jnp.concatenate([w_k, w_k], axis=1), split[at], preferred_element_type=F32
                    )
                return acc

            def others(s, _):
                g = sent[1, o, s]
                slot = jnp.where(((g >> 3) ^ a) == m3, hots[2], hots[3])
                part3[ch, s] = target(g, slot)
                return 0

            lax.fori_loop(0, SLOTS, others, 0, unroll=SLOTS)
            each(o, lambda k: send(2, w, k).start())

            def mine(n, _):
                out[block(n), columns(w, o)] = target(a * 8 + n, hots[0])
                return 0

            lax.fori_loop(0, 8, mine, 0, unroll=8)
            last = choose(o, [peer(link_of(k, 3))[0] for k in range(4)])

            def across(n, _):
                part4[ch, n] = target(last * 8 + n, hots[1])
                return 0

            lax.fori_loop(0, 8, across, 0, unroll=8)
            return 0

        lax.fori_loop(0, 4, body, 0)

    def fourth_exchange(w):
        for o in range(4):
            ch = w * 4 + o
            send(2, w, o).wait_recv()
            last = peer(link_of(o, 3))[0]

            def came(g, o=o, ch=ch):
                at = got[1, o, g]
                return got3[ch][jnp.maximum(at, 0)] * jnp.where(at >= 0, 1.0, 0.0)

            def across(n, _, ch=ch, last=last, came=came):
                part4[ch, n] += came(last * 8 + n)
                return 0

            lax.fori_loop(0, 8, across, 0, unroll=2)
            send(3, w, o).start()

            def mine(n, _, o=o, came=came):
                out[block(n), columns(w, o)] += came(a * 8 + n)
                return 0

            lax.fori_loop(0, 8, mine, 0, unroll=2)

    def write(w):
        at = pl.ds(w * 512, 512)
        return pltpu.make_async_copy(out.at[:, at], out_hbm.at[:, at], l_sem.at[w, 3])

    def finish(w):
        def body(o, _):
            each(o, lambda k: send(3, w, k).wait_recv())

            def mine(n, _):
                out[block(n), columns(w, o)] += got4[w * 4 + o, n]
                return 0

            lax.fori_loop(0, 8, mine, 0, unroll=2)
            return 0

        lax.fori_loop(0, 4, body, 0)
        write(w).start()

    def compute_b(h, c):
        rows = pl.ds(h * 512 + c * 256, 256)
        send_c(h, c).wait_recv()
        send_f(h, c).wait_recv()
        sources = (coef, gc, gz, gf)
        copies = [
            pltpu.make_async_copy(sources[q].at[blocks_b(h, c)], stage_b.at[q % 2], l_sem.at[2 + q % 2, 0])
            for q in range(4)
        ]
        copies[0].start()
        copies[1].start()
        for q in range(4):
            copies[q].wait()

            def split_body(n, _, q=q):
                hi, lo = pieces(stage_b[q % 2, :, :, block(n)].reshape(256, SB))
                split_b[q * 8 + n, :, 0:SB] = hi
                split_b[q * 8 + n, :, SB : 2 * SB] = lo
                return 0

            lax.fori_loop(0, 8, split_body, 0, unroll=2)
            if q < 2:
                copies[q + 2].start()

        def target(reader, n, slot):
            g = reader * 8 + n
            acc = jnp.zeros((256, SB), F32)
            for k in range(3):
                src = bsrc[k, g]
                sz, sc = src >> 4, (src >> 3) & 1
                away = sz ^ z
                here = (away == 0) | (away == (1 if h == 0 else 3))
                at = jnp.where(away == 0, 0, 16) + jnp.where(sc == core, 0, 8) + (src & 7)
                weight = jnp.where(here, integral(bpair[k, g]), 0.0)
                w_k = hot_b[slot, n * 3 + k]
                acc += weight * jnp.dot(
                    split_b[at], jnp.concatenate([w_k, w_k], axis=0), preferred_element_type=F32
                )
            return acc

        def others(n, _):
            part_b[h, c, :, :, block(n)] = target(over_z(1 - h) * 2 + core, n, 2 - h).reshape(2, SB, SB)
            return 0

        lax.fori_loop(0, 8, others, 0, unroll=4)
        send_b(h, c).start()

        def mine(n, _):
            out[rows, block(n)] += target(b, n, 0)
            return 0

        lax.fori_loop(0, 8, mine, 0, unroll=4)

    def finish_b(h, c):
        send_b(h, c).wait_recv()
        cp = pltpu.make_async_copy(got_b.at[blocks_b(h, c)], stage_b.at[c], l_sem.at[2 + c, 1])
        cp.start()
        cp.wait()
        out[pl.ds(h * 512 + c * 256, 256), :] += stage_b[c].reshape(256, 1024)

    barrier = pltpu.get_barrier_semaphore()
    everyone = [peer(link) for link in range(4)]
    everyone += [(a, over_z(0) * 2 + core), (a, over_z(1) * 2 + core), partner]
    for device in everyone:
        pl.semaphore_signal(barrier, inc=1, device_id=device, device_id_type=MESH)
    pl.semaphore_wait(barrier, len(everyone))

    links = [
        pltpu.make_async_copy(alinks_hbm, alinks, l_sem.at[0, 4]),
        pltpu.make_async_copy(blinks_hbm, blinks, l_sem.at[1, 4]),
    ]
    for cp in links:
        cp.start()
    for w in range(2):
        for o in range(4):
            send(0, w, o).start()
    for c in range(2):
        for h in range(2):
            send_z(h, c).start()
            send_c(h, c).start()
    for cp in links:
        cp.wait()
    build_alpha()
    build_beta()
    second_exchange(0)
    second_exchange(1)
    for h in range(2):
        send_z(h, 0).wait_recv()
        send_f(h, 0).start()
    third_exchange(0)
    for h in range(2):
        send_z(h, 1).wait_recv()
        send_f(h, 1).start()
    third_exchange(1)
    compute_b(0, 0)
    compute_b(1, 0)
    fourth_exchange(0)
    compute_b(0, 1)
    compute_b(1, 1)
    fourth_exchange(1)
    for c in range(2):
        for h in range(2):
            finish_b(h, c)
    finish(0)
    finish(1)
    for w in range(2):
        write(w).wait()
        for o in range(4):
            for i in range(4):
                send(i, w, o).wait_send()
    for c in range(2):
        for h in range(2):
            for copy in (send_z, send_c, send_f, send_b):
                copy(h, c).wait_send()


def named_couplings(coef, one_body, asrc, apair, alinks, bsrc, bpair, blinks, sent, got):
    hbm = pl.BlockSpec(memory_space=pl.ANY)
    smem = pl.BlockSpec(memory_space=pltpu.SMEM)
    dma = pltpu.SemaphoreType.DMA
    whole = jax.ShapeDtypeStruct((8, SB, 1024), F32)
    return pl.pallas_call(
        named_kernel,
        out_shape=[
            jax.ShapeDtypeStruct((1024, 1024), F32),
            jax.ShapeDtypeStruct((8, 8, SB, SB), F32),
            jax.ShapeDtypeStruct((8, SLOTS, SB, SB), F32),
            whole,
            whole,
            whole,
            whole,
        ],
        in_specs=[hbm, smem, smem, hbm, smem, smem, hbm, smem, smem, smem],
        out_specs=[hbm] * 7,
        scratch_shapes=[
            pltpu.VMEM((1024, 1024), F32),
            pltpu.VMEM((3, 128, SB), jnp.int32),
            pltpu.VMEM((3, 64, SB), jnp.int32),
            pltpu.VMEM((2, 16 + SLOTS, SB, SB), F32),
            pltpu.VMEM((16 + SLOTS, 2 * SB, SB), BF16),
            pltpu.VMEM((16, SB, SB), F32),
            pltpu.VMEM((8, SLOTS, SB, SB), F32),
            pltpu.VMEM((8, SLOTS, SB, SB), F32),
            *[pltpu.VMEM((SLOTS, SB, SB), F32)] * 8,
            pltpu.VMEM((8, 8, SB, SB), F32),
            pltpu.VMEM((8, 8, SB, SB), F32),
            pltpu.VMEM((2, 2, SB, 1024), F32),
            pltpu.VMEM((32, 256, 2 * SB), BF16),
            pltpu.VMEM((2, 2, 2, SB, 1024), F32),
            pltpu.VMEM((len(HOT_SLOT), 24, SB, SB), BF16),
            pltpu.VMEM((3, 24, SB, SB), BF16),
            dma((4, 8)),
            dma((4, 8)),
            dma((4, 2, 2)),
            dma((4, 2, 2)),
            dma((4, 5)),
        ],
        compiler_params=pltpu.CompilerParams(
            collective_id=0, has_side_effects=True, vmem_limit_bytes=61 * 2**20
        ),
        name="named_couplings",
    )(
        coef.reshape(8, SB, 1024),
        asrc,
        apair,
        alinks,
        bsrc,
        bpair,
        blinks,
        one_body,
        sent,
        got,
    )[0]


def any_kernel(
    coef,
    asrc,
    apair,
    alinks,
    bsrc,
    bpair,
    blinks,
    table,
    out,
    gx,
    gy,
    gz,
    stage,
    stage_b,
    split,
    split_b,
    part,
    far,
    near,
    core_out,
    core_in,
    hot,
    hot_b,
    g_send,
    g_recv,
    z_send,
    z_recv,
    r_send,
    r_recv,
    c_send,
    c_recv,
    l_sem,
):
    a = lax.axis_index("alpha")
    b = lax.axis_index("beta")
    y, x, z, core = a // 4, a % 4, b // 2, b % 2

    def step(axis, d):
        s = 1 if d == 0 else 3
        if axis == "x":
            return (y * 4 + (x + s) % 4, b)
        if axis == "y":
            return (((y + s) % 4) * 4 + x, b)
        return (a, ((z + s) % 4) * 2 + core)

    partner = (a, z * 2 + 1 - core)

    def cols(h, c):
        return pl.ds(pl.multiple_of(h * 512 + c * SB, SB), SB)

    axes = ("x", "y")
    bufs = (gx, gy)

    def own(h, c, d):
        return pltpu.make_async_remote_copy(
            src_ref=coef.at[:, cols(h, c)],
            dst_ref=bufs[h].at[2 if d == 0 else 0, c],
            send_sem=g_send.at[h, 0, c, d],
            recv_sem=g_recv.at[h, 0, c, d],
            device_id=step(axes[h], d),
            device_id_type=MESH,
        )

    def relay(h, c, d):
        rows = pl.ds(d * 512, 512)
        return pltpu.make_async_remote_copy(
            src_ref=bufs[h].at[2 if d == 0 else 0, c, rows],
            dst_ref=bufs[h].at[1, c, rows],
            send_sem=g_send.at[h, 1, c, d],
            recv_sem=g_recv.at[h, 1, c, d],
            device_id=step(axes[h], d),
            device_id_type=MESH,
        )

    def own_z(c, d):
        rows = pl.ds(pl.multiple_of(c * SB, SB), SB)
        return pltpu.make_async_remote_copy(
            src_ref=coef.at[rows],
            dst_ref=gz.at[2 if d == 0 else 0, rows],
            send_sem=z_send.at[0, c, d],
            recv_sem=z_recv.at[0, c, d],
            device_id=step("z", d),
            device_id_type=MESH,
        )

    def relay_z(c, d):
        rows = pl.ds(pl.multiple_of(c * SB + d * 64, 64), 64)
        return pltpu.make_async_remote_copy(
            src_ref=gz.at[2 if d == 0 else 0, rows],
            dst_ref=gz.at[1, rows],
            send_sem=z_send.at[1, c, d],
            recv_sem=z_recv.at[1, c, d],
            device_id=step("z", d),
            device_id_type=MESH,
        )

    def send_far(h, c, d):
        return pltpu.make_async_remote_copy(
            src_ref=part.at[h, c, 1, pl.ds(d * 512, 512)],
            dst_ref=far.at[h, c, d],
            send_sem=r_send.at[h, 0, c, d],
            recv_sem=r_recv.at[h, 0, c, d],
            device_id=step(axes[1 - h], d),
            device_id_type=MESH,
        )

    def send_near(h, c, d):
        return pltpu.make_async_remote_copy(
            src_ref=part.at[h, c, 0 if d == 0 else 2],
            dst_ref=near.at[h, c, d],
            send_sem=r_send.at[h, 1, c, d],
            recv_sem=r_recv.at[h, 1, c, d],
            device_id=step(axes[1 - h], d),
            device_id_type=MESH,
        )

    def send_core(c):
        return pltpu.make_async_remote_copy(
            src_ref=core_out.at[c],
            dst_ref=core_in.at[c],
            send_sem=c_send.at[c],
            recv_sem=c_recv.at[c],
            device_id=partner,
            device_id_type=MESH,
        )

    def integral(pair):
        p = pair // 18
        return table[p, pair - p * 18]

    def reader(h, q):
        if h == 0:
            return ((y + q) % 4) * 4 + x
        return y * 4 + (x + q) % 4

    def signed_hot(row):
        s = lax.broadcasted_iota(jnp.int32, (SB, SB), 0)
        return jnp.where(jnp.abs(row) - 1 == s, jnp.where(row > 0, 1.0, -1.0), 0.0)

    def build_alpha(h):
        def body(n, _):
            g = reader(h, n // 8) * 8 + n % 8
            for k in range(3):
                row = alinks[k, pl.ds(g, 1), :]
                hot[h, n * 3 + k] = signed_hot(row).T.astype(BF16)
            return 0

        lax.fori_loop(0, 32, body, 0)

    def build_beta():
        def body(n, _):
            g = (z * 2 + (core + n // 8) % 2) * 8 + n % 8
            for k in range(3):
                row = blinks[k, pl.ds(g, 1), :]
                hot_b[n * 3 + k] = signed_hot(row).astype(BF16)
            return 0

        lax.fori_loop(0, 16, body, 0)

    def pieces(v):
        hi = v.astype(BF16)
        return hi, (v - hi.astype(F32)).astype(BF16)

    def compute_alpha(h, c):
        copies = [pltpu.make_async_copy(coef.at[:, cols(h, c)], stage.at[0], l_sem.at[0])]
        for q in range(3):
            copies.append(
                pltpu.make_async_copy(bufs[h].at[q, c], stage.at[q + 1], l_sem.at[q + 1])
            )
        for cp in copies:
            cp.start()
        for cp in copies:
            cp.wait()

        def split_body(n, _):
            rows = pl.ds(pl.multiple_of((n % 8) * SB, SB), SB)
            hi, lo = pieces(stage[n // 8, rows, :])
            split[n, 0:SB, :] = hi
            split[n, SB : 2 * SB, :] = lo
            return 0

        lax.fori_loop(0, 32, split_body, 0, unroll=2)

        def target(n):
            g = reader(h, n // 8) * 8 + n % 8
            acc = jnp.zeros((SB, SB), F32)
            for k in range(3):
                src = asrc[k, g]
                sy, sx = (src >> 5) & 3, (src >> 3) & 3
                if h == 0:
                    here, q = sy == y, (sx - x) & 3
                else:
                    here, q = sx == x, (sy - y) & 3
                weight = jnp.where(here, integral(apair[k, g]), 0.0)
                w = hot[h, n * 3 + k]
                acc += weight * jnp.dot(
                    jnp.concatenate([w, w], axis=1),
                    split[q * 8 + (src & 7)],
                    preferred_element_type=F32,
                )
            return acc

        def mine(n, _):
            rows = pl.ds(pl.multiple_of(n * SB, SB), SB)
            out[rows, cols(h, c)] += target(n)
            return 0

        lax.fori_loop(0, 8, mine, 0, unroll=4)

        def others(n, _):
            rows = pl.ds(pl.multiple_of((n % 8) * SB, SB), SB)
            part[h, c, n // 8 - 1, rows, :] = target(n)
            return 0

        lax.fori_loop(8, 32, others, 0, unroll=4)

    def compute_beta(c):
        rows = pl.ds(pl.multiple_of(c * SB, SB), SB)
        copies = [pltpu.make_async_copy(coef.at[rows], stage_b.at[0], l_sem.at[4])]
        for q in range(3):
            copies.append(
                pltpu.make_async_copy(gz.at[q, rows], stage_b.at[q + 1], l_sem.at[q + 5])
            )
        for cp in copies:
            cp.start()
        for cp in copies:
            cp.wait()

        def split_body(n, _):
            hi, lo = pieces(stage_b[n // 8, :, pl.ds(pl.multiple_of((n % 8) * SB, SB), SB)])
            split_b[n, :, 0:SB] = hi
            split_b[n, :, SB : 2 * SB] = lo
            return 0

        lax.fori_loop(0, 32, split_body, 0, unroll=2)

        def target(n):
            g = (z * 2 + (core + n // 8) % 2) * 8 + n % 8
            acc = jnp.zeros((SB, SB), F32)
            for k in range(3):
                src = bsrc[k, g]
                sz, sc = (src >> 4) & 3, (src >> 3) & 1
                weight = jnp.where(sc == core, integral(bpair[k, g]), 0.0)
                w = hot_b[n * 3 + k]
                acc += weight * jnp.dot(
                    split_b[((sz - z) & 3) * 8 + (src & 7)],
                    jnp.concatenate([w, w], axis=0),
                    preferred_element_type=F32,
                )
            return acc

        def mine(n, _):
            at = pl.ds(pl.multiple_of(n * SB, SB), SB)
            out[rows, at] += target(n)
            return 0

        lax.fori_loop(0, 8, mine, 0, unroll=4)

        def others(n, _):
            at = pl.ds(pl.multiple_of((n - 8) * SB, SB), SB)
            core_out[c, :, at] = target(n)
            return 0

        lax.fori_loop(8, 16, others, 0, unroll=4)

    def pass_on(h, c):
        for d in range(2):
            send_far(h, c, d).wait_recv()
            slot = 0 if d == 0 else 2

            def body(n, _):
                rows = pl.ds(pl.multiple_of(d * 512 + n * SB, SB), SB)
                part[h, c, slot, rows, :] += far[h, c, d, pl.ds(pl.multiple_of(n * SB, SB), SB), :]
                return 0

            lax.fori_loop(0, 4, body, 0)
            send_near(h, c, d).start()

    def finish(h, c):
        for d in range(2):
            send_near(h, c, d).wait_recv()

        def body(n, _):
            rows = pl.ds(pl.multiple_of(n * SB, SB), SB)
            out[rows, cols(h, c)] += near[h, c, 0, rows, :] + near[h, c, 1, rows, :]
            return 0

        lax.fori_loop(0, 8, body, 0)

    def finish_core(c):
        send_core(c).wait_recv()
        rows = pl.ds(pl.multiple_of(c * SB, SB), SB)
        out[rows, :] += core_in[c]

    barrier = pltpu.get_barrier_semaphore()
    for axis in ("x", "y", "z"):
        for d in range(2):
            pl.semaphore_signal(barrier, inc=1, device_id=step(axis, d), device_id_type=MESH)
    pl.semaphore_signal(barrier, inc=1, device_id=partner, device_id_type=MESH)
    pl.semaphore_wait(barrier, 7)

    for c in range(2):
        for d in range(2):
            own(0, c, d).start()
            own(1, c, d).start()
            own_z(c, d).start()

    out[...] = jnp.zeros_like(out)
    build_alpha(0)

    def move_on(c):
        for h in range(2):
            for d in range(2):
                own(h, c, d).wait_recv()
                relay(h, c, d).start()

        @pl.when(c < NCH - 2)
        def _():
            for h in range(2):
                for d in range(2):
                    own(h, c + 2, d).start()

    def move_on_z(c):
        for d in range(2):
            own_z(c, d).wait_recv()
            relay_z(c, d).start()

        @pl.when(c < NZ - 2)
        def _():
            for d in range(2):
                own_z(c + 2, d).start()

    move_on(0)
    move_on_z(0)
    build_alpha(1)
    build_beta()

    def loop(t, _):
        @pl.when(t < NCH - 1)
        def _():
            move_on(t + 1)

        @pl.when(t < NZ - 1)
        def _():
            move_on_z(t + 1)

        @pl.when(t < NCH)
        def _():
            for h in range(2):
                for d in range(2):
                    relay(h, t, d).wait_recv()
                compute_alpha(h, t)

        @pl.when(t == 2)
        def _():
            for c in range(2):
                for h in range(2):
                    for d in range(2):
                        send_far(h, c, d).start()

        @pl.when((t >= 2) & (t < NCH))
        def _():
            for h in range(2):
                for d in range(2):
                    send_far(h, t, d).start()

        @pl.when((t >= 3) & (t < 7))
        def _():
            for h in range(2):
                pass_on(h, t - 3)

        for d in range(2):
            relay_z(t, d).wait_recv()
        compute_beta(t)
        send_core(t).start()

        @pl.when(t >= 6)
        def _():
            for h in range(2):
                finish(h, t - 6)

        @pl.when(t >= 1)
        def _():
            finish_core(t - 1)

        return 0

    lax.fori_loop(0, NZ, loop, 0)
    finish_core(NZ - 1)

    def last(c, _):
        for h in range(2):
            finish(h, c)
        return 0

    lax.fori_loop(2, NCH, last, 0)

    def drain(c, _):
        for h in range(2):
            for d in range(2):
                own(h, c, d).wait_send()
                relay(h, c, d).wait_send()
                send_far(h, c, d).wait_send()
                send_near(h, c, d).wait_send()
        return 0

    lax.fori_loop(0, NCH, drain, 0)

    def drain_z(c, _):
        for d in range(2):
            own_z(c, d).wait_send()
            relay_z(c, d).wait_send()
        send_core(c).wait_send()
        return 0

    lax.fori_loop(0, NZ, drain_z, 0)


def any_couplings(coef, one_body, asrc, apair, alinks, bsrc, bpair, blinks):
    hbm = pl.BlockSpec(memory_space=pl.ANY)
    vmem = pl.BlockSpec(memory_space=pltpu.VMEM)
    smem = pl.BlockSpec(memory_space=pltpu.SMEM)
    dma = pltpu.SemaphoreType.DMA
    return pl.pallas_call(
        any_kernel,
        out_shape=[
            jax.ShapeDtypeStruct((1024, 1024), F32),
            jax.ShapeDtypeStruct((3, NCH, 1024, SB), F32),
            jax.ShapeDtypeStruct((3, NCH, 1024, SB), F32),
            jax.ShapeDtypeStruct((3, 1024, 1024), F32),
        ],
        in_specs=[hbm, smem, smem, vmem, smem, smem, vmem, smem],
        out_specs=[vmem, hbm, hbm, hbm],
        scratch_shapes=[
            pltpu.VMEM((4, 1024, SB), F32),
            pltpu.VMEM((4, SB, 1024), F32),
            pltpu.VMEM((32, 2 * SB, SB), BF16),
            pltpu.VMEM((32, SB, 2 * SB), BF16),
            pltpu.VMEM((2, NCH, 3, 1024, SB), F32),
            pltpu.VMEM((2, NCH, 2, 512, SB), F32),
            pltpu.VMEM((2, NCH, 2, 1024, SB), F32),
            pltpu.VMEM((NZ, SB, 1024), F32),
            pltpu.VMEM((NZ, SB, 1024), F32),
            pltpu.VMEM((2, 96, SB, SB), BF16),
            pltpu.VMEM((48, SB, SB), BF16),
            dma((2, 2, NCH, 2)),
            dma((2, 2, NCH, 2)),
            dma((2, NZ, 2)),
            dma((2, NZ, 2)),
            dma((2, 2, NCH, 2)),
            dma((2, 2, NCH, 2)),
            dma((NZ,)),
            dma((NZ,)),
            dma((8,)),
        ],
        compiler_params=pltpu.CompilerParams(
            collective_id=1, has_side_effects=True, vmem_limit_bytes=60 * 2**20
        ),
        name="any_couplings",
    )(coef, asrc, apair, alinks, bsrc, bpair, blinks, one_body)[0]


def on_device(
    coefficients,
    alpha_energy,
    beta_energy,
    one_body,
    alpha_source,
    alpha_pair,
    alpha_links,
    beta_source,
    beta_pair,
    beta_links,
):
    sent, got, most = message_tables(alpha_source, lax.axis_index("alpha"))
    tables = (
        alpha_source.T,
        alpha_pair.T,
        alpha_links.transpose(1, 0, 2),
        beta_source.T,
        beta_pair.T,
        beta_links.transpose(1, 0, 2),
    )
    terms = lax.cond(
        most <= SLOTS,
        lambda: named_couplings(coefficients, one_body, *tables, sent, got),
        lambda: any_couplings(coefficients, one_body, *tables),
    )
    return (alpha_energy[:, None] + beta_energy[None, :]) * coefficients + terms


def solution(mesh):
    in_specs = (P("alpha", "beta"), P("alpha"), P("beta"), P(), P(), P(), P(), P(), P(), P())
    out_specs = P("alpha", "beta")
    return jax.shard_map(
        on_device, mesh=mesh, in_specs=in_specs, out_specs=out_specs, check_vma=False
    )
```

```python
import jax
import jax.numpy as jnp
from jax import lax
from jax.experimental import pallas as pl
from jax.experimental.pallas import tpu as pltpu
from jax.sharding import PartitionSpec as P

MESH = pl.DeviceIdType.MESH
F32, BF16 = jnp.float32, jnp.bfloat16
SB = 128
NCH = 4
NZ = 8
SLOTS = 13

LINK = (1, 3, 4, 12)


def link_of(o, i):
    return (o + i) % 4


def spans(links):
    found = [0]
    for link in links:
        found = found + [v ^ LINK[link] for v in found]
    return found


def reader_masks(o):
    last, third = LINK[link_of(o, 3)], LINK[link_of(o, 2)]
    return (0, last, third, third ^ last)


HOT_SLOT = {m: i for i, m in enumerate(sorted({m for o in range(4) for m in reader_masks(o)}))}


def table_kernel(source, slots, fits):
    me = lax.axis_index("alpha")

    def iota(shape, axis):
        return lax.broadcasted_iota(jnp.int32, shape, axis)

    def mask_of(order, i):
        link = (order + i) % 4
        return jnp.where(link == 0, 1, jnp.where(link == 1, 3, jnp.where(link == 2, 4, 12)))

    def ones(mask):
        return jnp.where(mask, 1.0, 0.0).astype(BF16)

    def dot(left, right, axis=0):
        return lax.dot_general(left, right, (((1,), (axis,)), ((), ())), preferred_element_type=F32)

    row, lane = iota((64, 128), 0), iota((64, 128), 1)
    order, sender = row // 16, row % 16
    m1, m2, m3, m4 = (mask_of(order, i) for i in range(4))
    apart = (lane >> 3) ^ sender
    reader = apart ^ m2
    two_readers = (reader == 0) | (reader == m3) | (reader == m4) | (reader == (m3 ^ m4))
    two_sources = (apart == 0) | (apart == m1)
    device = lane ^ sender
    three_sources = (device == 0) | (device == m1) | (device == m2) | (device == (m1 ^ m2))
    three_readers = (apart == m3) | (apart == (m3 ^ m4))
    which = iota((128, 128), 0)
    named, fed = which < 0, which < 0
    for k in range(3):
        line = source[k : k + 1, :]
        named = named | (line == which)
        fed = fed | ((line >> 3) == which)
    two = two_sources & (dot(ones(two_readers), ones(named), 1) > 0.5)
    three = three_readers & (dot(ones(three_sources), ones(fed)) > 0.5)
    before = ones(which < iota((128, 128), 1))
    row, lane = iota((8, 64), 0), iota((8, 64), 1)
    order = row % 4
    at = iota((8, 128), 1)
    most = jnp.int32(0)
    for stage, messages in enumerate((two, three)):
        node = jnp.where(row < 4, me, me ^ mask_of(order, stage + 1))
        mine = dot(ones(lane == order * 16 + node), ones(messages))
        rank = dot(mine.astype(BF16), before).astype(jnp.int32)
        here = mine > 0.5
        chosen = jnp.zeros((8, 128), jnp.int32)
        for s in range(SLOTS):
            block = jnp.sum(jnp.where(here & (rank == s), at, 0), axis=1, keepdims=True)
            chosen = jnp.where(at == s, block, chosen)
        got = jnp.where(here, jnp.minimum(rank, SLOTS - 1), -1)
        slots[stage] = jnp.where(iota((8, 128), 0) < 4, chosen, got)
        count = jnp.sum(jnp.where(messages, 1, 0), axis=1, keepdims=True)
        most = jnp.maximum(most, jnp.max(count))
    fits[0, 0] = jnp.where(most <= SLOTS, 1, 0)


def message_tables(source):
    vmem = pl.BlockSpec(memory_space=pltpu.VMEM)
    return pl.pallas_call(
        table_kernel,
        out_shape=[
            jax.ShapeDtypeStruct((2, 8, 128), jnp.int32),
            jax.ShapeDtypeStruct((1, 1), jnp.int32),
        ],
        in_specs=[vmem],
        out_specs=[vmem, pl.BlockSpec(memory_space=pltpu.SMEM)],
        name="message_tables",
    )(source)


def named_kernel(
    coef,
    asrc,
    apair,
    alinks_hbm,
    bsrc,
    bpair,
    blinks_hbm,
    table,
    slots,
    energy_a,
    energy_b,
    out_hbm,
    got1,
    got2,
    gz,
    gc,
    gf,
    got_b,
    out,
    alinks,
    blinks,
    stage,
    split,
    held,
    pack,
    part3,
    *rest,
):
    got3, rest = rest[:8], rest[8:]
    part4, got4, stage_b, split_b, part_b, hot, hot_b, rows_a, *rest = rest
    at_own, weight_own, at_sent, weight_sent, hot_sent, s_sem, r_sem, zs_sem, zr_sem, l_sem = rest
    a = lax.axis_index("alpha")
    b = lax.axis_index("beta")
    y, x, z, core = a // 4, a % 4, b // 2, b % 2

    def over(place, link):
        py, px = place
        if link == 0:
            return (py, px + 1 - 2 * (px % 2))
        if link == 1:
            return (py, 3 - px)
        if link == 2:
            return (py + 1 - 2 * (py % 2), px)
        return (3 - py, px)

    def index(place):
        return place[0] * 4 + place[1]

    def peer(link):
        return (index(over((y, x), link)), b)

    def over_z(pair):
        return z + 1 - 2 * (z % 2) if pair == 0 else 3 - z

    partner = (a, z * 2 + 1 - core)

    def choose(o, values):
        return jnp.where(
            o == 0, values[0], jnp.where(o == 1, values[1], jnp.where(o == 2, values[2], values[3]))
        )

    def each(o, act):
        for k in range(4):

            @pl.when(o == k)
            def _(k=k):
                act(k)

    def columns(w, o):
        return pl.ds(pl.multiple_of((w * 4 + o) * SB, SB), SB)

    def block(n):
        return pl.ds(pl.multiple_of(n * SB, SB), SB)

    def send(i, w, o):
        ch = w * 4 + o
        src = (coef.at[:, :, columns(w, o)], pack.at[ch], part3.at[ch], part4.at[ch])[i]
        dst = got3[ch] if i == 2 else (got1, got2, None, got4)[i].at[ch]
        return pltpu.make_async_remote_copy(
            src_ref=src,
            dst_ref=dst,
            send_sem=s_sem.at[i, ch],
            recv_sem=r_sem.at[i, ch],
            device_id=peer(link_of(o, i)),
            device_id_type=MESH,
        )

    def blocks_b(h, c):
        return pl.ds(h * 4 + c * 2, 2)

    def send_z(h, c):
        return pltpu.make_async_remote_copy(
            src_ref=coef.at[blocks_b(h, c)],
            dst_ref=gz.at[blocks_b(h, c)],
            send_sem=zs_sem.at[0, h, c],
            recv_sem=zr_sem.at[0, h, c],
            device_id=(a, over_z(h) * 2 + core),
            device_id_type=MESH,
        )

    def send_c(h, c):
        return pltpu.make_async_remote_copy(
            src_ref=coef.at[blocks_b(h, c)],
            dst_ref=gc.at[blocks_b(h, c)],
            send_sem=zs_sem.at[1, h, c],
            recv_sem=zr_sem.at[1, h, c],
            device_id=partner,
            device_id_type=MESH,
        )

    def send_f(h, c):
        return pltpu.make_async_remote_copy(
            src_ref=gz.at[blocks_b(h, c)],
            dst_ref=gf.at[blocks_b(h, c)],
            send_sem=zs_sem.at[2, h, c],
            recv_sem=zr_sem.at[2, h, c],
            device_id=partner,
            device_id_type=MESH,
        )

    def send_b(h, c):
        return pltpu.make_async_remote_copy(
            src_ref=part_b.at[h, c],
            dst_ref=got_b.at[blocks_b(h, c)],
            send_sem=zs_sem.at[3, h, c],
            recv_sem=zr_sem.at[3, h, c],
            device_id=(a, over_z(1 - h) * 2 + core),
            device_id_type=MESH,
        )

    def integral(pair):
        p = pair // 18
        return table[p, pair - p * 18]

    def signed_hot(row):
        s = lax.broadcasted_iota(jnp.int32, (SB, SB), 0)
        return jnp.where(jnp.abs(row) - 1 == s, jnp.where(row > 0, 1.0, -1.0), 0.0)

    def pieces(v):
        hi = v.astype(BF16)
        return hi, (v - hi.astype(F32)).astype(BF16)

    def build_alpha():
        for mask, slot in HOT_SLOT.items():
            place = (y, x)
            for link in range(4):
                if mask & 3 == LINK[link] or mask & 12 == LINK[link]:
                    place = over(place, link)
            if mask & 3 == 2:
                place = over(over(place, 0), 1)
            if mask & 12 == 8:
                place = over(over(place, 2), 3)
            reader = index(place)

            def body(n, _, slot=slot, reader=reader):
                for k in range(3):
                    row = alinks[k, pl.ds(reader * 8 + n, 1), :]
                    hot[slot, k * 8 + n] = signed_hot(row).T.astype(BF16)
                return 0

            lax.fori_loop(0, 8, body, 0, unroll=4)

    def plan():
        def body(o, _):
            m1 = choose(o, [LINK[link_of(k, 0)] for k in range(4)])
            m2 = choose(o, [LINK[link_of(k, 1)] for k in range(4)])
            m3 = choose(o, [LINK[link_of(k, 2)] for k in range(4)])
            last = choose(o, [peer(link_of(k, 3))[0] for k in range(4)])
            hots = [
                choose(o, [HOT_SLOT[reader_masks(k)[role]] for k in range(4)])
                for role in range(2, 4)
            ]

            def entry(g, k):
                src = asrc[k, g]
                apart = (src >> 3) ^ a
                inner = src & 7
                over_two = (apart == m2) | (apart == (m1 ^ m2))
                here = over_two | (apart == 0) | (apart == m1)
                arrived = 16 + jnp.maximum(slots[0, 4 + o, src], 0)
                at = jnp.where(over_two, arrived, jnp.where(apart == m1, 8 + inner, inner))
                return at, jnp.where(here, integral(apair[k, g]), 0.0)

            def own_entries(n, _):
                for role, reader in enumerate((a, last)):
                    for k in range(3):
                        at, weight = entry(reader * 8 + n, k)
                        at_own[o, role * 24 + n * 3 + k] = at
                        weight_own[o, role * 24 + n * 3 + k] = weight
                return 0

            lax.fori_loop(0, 8, own_entries, 0)

            def sent_entries(s, _):
                g = slots[1, o, s]
                hot_sent[o, s] = jnp.where(((g >> 3) ^ a) == m3, hots[0], hots[1])
                hot_sent[o, SLOTS + s] = g & 7
                for k in range(3):
                    at, weight = entry(g, k)
                    at_sent[o, s * 3 + k] = at
                    weight_sent[o, s * 3 + k] = weight
                return 0

            lax.fori_loop(0, SLOTS, sent_entries, 0)
            return 0

        lax.fori_loop(0, 4, body, 0)

    def build_beta():
        for slot in range(3):
            reader = (z if slot == 0 else over_z(slot - 1)) * 2 + core

            def body(n, _, slot=slot, reader=reader):
                for k in range(3):
                    row = blinks[k, pl.ds(reader * 8 + n, 1), :]
                    hot_b[slot, n * 3 + k] = signed_hot(row).astype(BF16)
                return 0

            lax.fori_loop(0, 8, body, 0, unroll=4)

    def load(w, o, buf, second):
        copies = [
            pltpu.make_async_copy(
                coef.at[:, :, columns(w, o)], stage.at[buf, pl.ds(0, 8)], l_sem.at[buf, 0]
            ),
            pltpu.make_async_copy(
                got1.at[w * 4 + o], stage.at[buf, pl.ds(8, 8)], l_sem.at[buf, 1]
            ),
        ]
        if second:
            copies.append(
                pltpu.make_async_copy(
                    got2.at[w * 4 + o], stage.at[buf, pl.ds(16, SLOTS)], l_sem.at[buf, 2]
                )
            )
        return copies

    def start_load(w, o, second):
        for cp in load(w, o, o % 2, second):
            cp.start()

    def wait_load(w, o, second):
        for cp in load(w, o, o % 2, second):
            cp.wait()

    def ready(w, o, i):
        def first(k):
            if k == 0:
                send(i, w, 0).wait_recv()
                start_load(w, 0, i == 1)
            if k < 3:
                send(i, w, k + 1).wait_recv()
                start_load(w, k + 1, i == 1)
            wait_load(w, k, i == 1)

        each(o, first)

    def second_exchange(w):
        def body(o, _):
            ready(w, o, 0)
            buf = o % 2

            def hold(n, _):
                held[n] = stage[buf, n]
                return 0

            lax.fori_loop(0, 16, hold, 0, unroll=4)

            def fill(s, _):
                wanted = slots[0, o, s]
                at = jnp.where((wanted >> 3) == a, 0, 8) + (wanted & 7)
                pack[w * 4 + o, s] = held[at]
                return 0

            lax.fori_loop(0, SLOTS, fill, 0)
            each(o, lambda k: send(1, w, k).start())
            return 0

        lax.fori_loop(0, 4, body, 0)

    def third_exchange(w):
        def body(o, _):
            ready(w, o, 1)
            buf = o % 2
            ch = w * 4 + o
            hots = [
                choose(o, [HOT_SLOT[reader_masks(k)[role]] for k in range(4)]) for role in range(2)
            ]

            def split_body(n, _):
                hi, lo = pieces(stage[buf, n])
                split[n, 0:SB, :] = hi
                split[n, SB : 2 * SB, :] = lo
                return 0

            lax.fori_loop(0, 16 + SLOTS, split_body, 0, unroll=8)

            def product(at, w_k):
                return jnp.dot(
                    jnp.concatenate([w_k, w_k], axis=1), split[at], preferred_element_type=F32
                )

            def others(s, _):
                acc = jnp.zeros((SB, SB), F32)
                for k in range(3):
                    w_k = hot[hot_sent[o, s], k * 8 + hot_sent[o, SLOTS + s]]
                    acc += weight_sent[o, s * 3 + k] * product(at_sent[o, s * 3 + k], w_k)
                part3[ch, s] = acc
                return 0

            lax.fori_loop(0, SLOTS, others, 0, unroll=SLOTS)
            each(o, lambda k: send(2, w, k).start())

            def target(role, n):
                acc = jnp.zeros((SB, SB), F32)
                for k in range(3):
                    e = role * 24 + n * 3 + k
                    acc += weight_own[o, e] * product(at_own[o, e], hot[hots[role], k * 8 + n])
                return acc

            def mine(n, _):
                energy = rows_a[n] + energy_b[:, columns(w, o)]
                out[block(n), columns(w, o)] += energy * stage[buf, n] + target(0, n)
                return 0

            lax.fori_loop(0, 8, mine, 0, unroll=8)

            def across(n, _):
                part4[ch, n] = target(1, n)
                return 0

            lax.fori_loop(0, 8, across, 0, unroll=8)
            return 0

        lax.fori_loop(0, 4, body, 0)

    def fourth_exchange(w):
        for o in range(4):
            ch = w * 4 + o
            send(2, w, o).wait_recv()
            last = peer(link_of(o, 3))[0]

            def came(g, o=o, ch=ch):
                at = slots[1, 4 + o, g]
                return got3[ch][jnp.maximum(at, 0)] * jnp.where(at >= 0, 1.0, 0.0)

            def across(n, _, ch=ch, last=last, came=came):
                part4[ch, n] += came(last * 8 + n)
                return 0

            lax.fori_loop(0, 8, across, 0, unroll=2)
            send(3, w, o).start()

            def mine(n, _, o=o, came=came):
                out[block(n), columns(w, o)] += came(a * 8 + n)
                return 0

            lax.fori_loop(0, 8, mine, 0, unroll=2)

    def write(w):
        at = pl.ds(w * 512, 512)
        return pltpu.make_async_copy(out.at[:, at], out_hbm.at[:, at], l_sem.at[w, 3])

    def finish(w):
        def body(o, _):
            each(o, lambda k: send(3, w, k).wait_recv())

            def mine(n, _):
                out[block(n), columns(w, o)] += got4[w * 4 + o, n]
                return 0

            lax.fori_loop(0, 8, mine, 0, unroll=2)
            return 0

        lax.fori_loop(0, 4, body, 0)
        write(w).start()

    def compute_b(h, c):
        rows = pl.ds(h * 512 + c * 256, 256)
        send_c(h, c).wait_recv()
        send_f(h, c).wait_recv()
        sources = (coef, gc, gz, gf)
        copies = [
            pltpu.make_async_copy(sources[q].at[blocks_b(h, c)], stage_b.at[q % 2], l_sem.at[2 + q % 2, 0])
            for q in range(4)
        ]
        copies[0].start()
        copies[1].start()
        for q in range(4):
            copies[q].wait()

            def split_body(n, _, q=q):
                hi, lo = pieces(stage_b[q % 2, :, :, block(n)].reshape(256, SB))
                split_b[q * 8 + n, :, 0:SB] = hi
                split_b[q * 8 + n, :, SB : 2 * SB] = lo
                return 0

            lax.fori_loop(0, 8, split_body, 0, unroll=2)
            if q < 2:
                copies[q + 2].start()

        def target(reader, n, slot):
            g = reader * 8 + n
            acc = jnp.zeros((256, SB), F32)
            for k in range(3):
                src = bsrc[k, g]
                sz, sc = src >> 4, (src >> 3) & 1
                away = sz ^ z
                here = (away == 0) | (away == (1 if h == 0 else 3))
                at = jnp.where(away == 0, 0, 16) + jnp.where(sc == core, 0, 8) + (src & 7)
                weight = jnp.where(here, integral(bpair[k, g]), 0.0)
                w_k = hot_b[slot, n * 3 + k]
                acc += weight * jnp.dot(
                    split_b[at], jnp.concatenate([w_k, w_k], axis=0), preferred_element_type=F32
                )
            return acc

        def others(n, _):
            part_b[h, c, :, :, block(n)] = target(over_z(1 - h) * 2 + core, n, 2 - h).reshape(2, SB, SB)
            return 0

        lax.fori_loop(0, 8, others, 0, unroll=4)
        send_b(h, c).start()

        def mine(n, _):
            out[rows, block(n)] += target(b, n, 0)
            return 0

        lax.fori_loop(0, 8, mine, 0, unroll=4)

    def finish_b(h, c):
        send_b(h, c).wait_recv()
        cp = pltpu.make_async_copy(got_b.at[blocks_b(h, c)], stage_b.at[c], l_sem.at[2 + c, 1])
        cp.start()
        cp.wait()
        out[pl.ds(h * 512 + c * 256, 256), :] += stage_b[c].reshape(256, 1024)

    barrier = pltpu.get_barrier_semaphore()
    everyone = [peer(link) for link in range(4)]
    everyone += [(a, over_z(0) * 2 + core), (a, over_z(1) * 2 + core), partner]
    for device in everyone:
        pl.semaphore_signal(barrier, inc=1, device_id=device, device_id_type=MESH)
    pl.semaphore_wait(barrier, len(everyone))

    links = [
        pltpu.make_async_copy(alinks_hbm, alinks, l_sem.at[0, 4]),
        pltpu.make_async_copy(blinks_hbm, blinks, l_sem.at[1, 4]),
    ]
    for cp in links:
        cp.start()
    for w in range(2):
        for o in range(4):
            send(0, w, o).start()
    for c in range(2):
        for h in range(2):
            send_z(h, c).start()
            send_c(h, c).start()
    for cp in links:
        cp.wait()
    build_alpha()
    for n in range(8):
        rows_a[n] = jnp.broadcast_to(energy_a[n : n + 1, :], (SB, SB)).T
    out[...] = jnp.zeros_like(out)
    plan()
    second_exchange(0)
    build_beta()
    second_exchange(1)
    for h in range(2):
        send_z(h, 0).wait_recv()
        send_f(h, 0).start()
    for h in range(2):
        compute_b(h, 0)
    third_exchange(0)
    for h in range(2):
        send_z(h, 1).wait_recv()
        send_f(h, 1).start()
    third_exchange(1)
    for h in range(2):
        compute_b(h, 1)
    fourth_exchange(0)
    for h in range(2):
        finish_b(h, 0)
    fourth_exchange(1)
    for h in range(2):
        finish_b(h, 1)
    finish(0)
    finish(1)
    for w in range(2):
        write(w).wait()
        for o in range(4):
            for i in range(4):
                send(i, w, o).wait_send()
    for c in range(2):
        for h in range(2):
            for copy in (send_z, send_c, send_f, send_b):
                copy(h, c).wait_send()


def named_sigma(coef, energy_a, energy_b, one_body, asrc, apair, alinks, bsrc, bpair, blinks, slots):
    hbm = pl.BlockSpec(memory_space=pl.ANY)
    smem = pl.BlockSpec(memory_space=pltpu.SMEM)
    vmem = pl.BlockSpec(memory_space=pltpu.VMEM)
    dma = pltpu.SemaphoreType.DMA
    whole = jax.ShapeDtypeStruct((8, SB, 1024), F32)
    return pl.pallas_call(
        named_kernel,
        out_shape=[
            jax.ShapeDtypeStruct((1024, 1024), F32),
            jax.ShapeDtypeStruct((8, 8, SB, SB), F32),
            jax.ShapeDtypeStruct((8, SLOTS, SB, SB), F32),
            whole,
            whole,
            whole,
            whole,
        ],
        in_specs=[hbm, smem, smem, hbm, smem, smem, hbm, smem, smem, vmem, vmem],
        out_specs=[hbm] * 7,
        scratch_shapes=[
            pltpu.VMEM((1024, 1024), F32),
            pltpu.VMEM((3, 128, SB), jnp.int32),
            pltpu.VMEM((3, 64, SB), jnp.int32),
            pltpu.VMEM((2, 16 + SLOTS, SB, SB), F32),
            pltpu.VMEM((16 + SLOTS, 2 * SB, SB), BF16),
            pltpu.VMEM((16, SB, SB), F32),
            pltpu.VMEM((8, SLOTS, SB, SB), F32),
            pltpu.VMEM((8, SLOTS, SB, SB), F32),
            *[pltpu.VMEM((SLOTS, SB, SB), F32)] * 8,
            pltpu.VMEM((8, 8, SB, SB), F32),
            pltpu.VMEM((8, 8, SB, SB), F32),
            pltpu.VMEM((2, 2, SB, 1024), F32),
            pltpu.VMEM((32, 256, 2 * SB), BF16),
            pltpu.VMEM((2, 2, 2, SB, 1024), F32),
            pltpu.VMEM((len(HOT_SLOT), 24, SB, SB), BF16),
            pltpu.VMEM((3, 24, SB, SB), BF16),
            pltpu.VMEM((8, SB, SB), F32),
            pltpu.SMEM((4, 48), jnp.int32),
            pltpu.SMEM((4, 48), F32),
            pltpu.SMEM((4, 3 * SLOTS), jnp.int32),
            pltpu.SMEM((4, 3 * SLOTS), F32),
            pltpu.SMEM((4, 2 * SLOTS), jnp.int32),
            dma((4, 8)),
            dma((4, 8)),
            dma((4, 2, 2)),
            dma((4, 2, 2)),
            dma((4, 5)),
        ],
        compiler_params=pltpu.CompilerParams(
            collective_id=0, has_side_effects=True, vmem_limit_bytes=61 * 2**20
        ),
        name="named_sigma",
    )(
        coef.reshape(8, SB, 1024),
        asrc,
        apair,
        alinks,
        bsrc,
        bpair,
        blinks,
        one_body,
        slots,
        energy_a.reshape(8, SB),
        energy_b.reshape(1, 1024),
    )[0]


def any_kernel(
    coef,
    asrc,
    apair,
    alinks,
    bsrc,
    bpair,
    blinks,
    table,
    out,
    gx,
    gy,
    gz,
    stage,
    stage_b,
    split,
    split_b,
    part,
    far,
    near,
    core_out,
    core_in,
    hot,
    hot_b,
    g_send,
    g_recv,
    z_send,
    z_recv,
    r_send,
    r_recv,
    c_send,
    c_recv,
    l_sem,
):
    a = lax.axis_index("alpha")
    b = lax.axis_index("beta")
    y, x, z, core = a // 4, a % 4, b // 2, b % 2

    def step(axis, d):
        s = 1 if d == 0 else 3
        if axis == "x":
            return (y * 4 + (x + s) % 4, b)
        if axis == "y":
            return (((y + s) % 4) * 4 + x, b)
        return (a, ((z + s) % 4) * 2 + core)

    partner = (a, z * 2 + 1 - core)

    def cols(h, c):
        return pl.ds(pl.multiple_of(h * 512 + c * SB, SB), SB)

    axes = ("x", "y")
    bufs = (gx, gy)

    def own(h, c, d):
        return pltpu.make_async_remote_copy(
            src_ref=coef.at[:, cols(h, c)],
            dst_ref=bufs[h].at[2 if d == 0 else 0, c],
            send_sem=g_send.at[h, 0, c, d],
            recv_sem=g_recv.at[h, 0, c, d],
            device_id=step(axes[h], d),
            device_id_type=MESH,
        )

    def relay(h, c, d):
        rows = pl.ds(d * 512, 512)
        return pltpu.make_async_remote_copy(
            src_ref=bufs[h].at[2 if d == 0 else 0, c, rows],
            dst_ref=bufs[h].at[1, c, rows],
            send_sem=g_send.at[h, 1, c, d],
            recv_sem=g_recv.at[h, 1, c, d],
            device_id=step(axes[h], d),
            device_id_type=MESH,
        )

    def own_z(c, d):
        rows = pl.ds(pl.multiple_of(c * SB, SB), SB)
        return pltpu.make_async_remote_copy(
            src_ref=coef.at[rows],
            dst_ref=gz.at[2 if d == 0 else 0, rows],
            send_sem=z_send.at[0, c, d],
            recv_sem=z_recv.at[0, c, d],
            device_id=step("z", d),
            device_id_type=MESH,
        )

    def relay_z(c, d):
        rows = pl.ds(pl.multiple_of(c * SB + d * 64, 64), 64)
        return pltpu.make_async_remote_copy(
            src_ref=gz.at[2 if d == 0 else 0, rows],
            dst_ref=gz.at[1, rows],
            send_sem=z_send.at[1, c, d],
            recv_sem=z_recv.at[1, c, d],
            device_id=step("z", d),
            device_id_type=MESH,
        )

    def send_far(h, c, d):
        return pltpu.make_async_remote_copy(
            src_ref=part.at[h, c, 1, pl.ds(d * 512, 512)],
            dst_ref=far.at[h, c, d],
            send_sem=r_send.at[h, 0, c, d],
            recv_sem=r_recv.at[h, 0, c, d],
            device_id=step(axes[1 - h], d),
            device_id_type=MESH,
        )

    def send_near(h, c, d):
        return pltpu.make_async_remote_copy(
            src_ref=part.at[h, c, 0 if d == 0 else 2],
            dst_ref=near.at[h, c, d],
            send_sem=r_send.at[h, 1, c, d],
            recv_sem=r_recv.at[h, 1, c, d],
            device_id=step(axes[1 - h], d),
            device_id_type=MESH,
        )

    def send_core(c):
        return pltpu.make_async_remote_copy(
            src_ref=core_out.at[c],
            dst_ref=core_in.at[c],
            send_sem=c_send.at[c],
            recv_sem=c_recv.at[c],
            device_id=partner,
            device_id_type=MESH,
        )

    def integral(pair):
        p = pair // 18
        return table[p, pair - p * 18]

    def reader(h, q):
        if h == 0:
            return ((y + q) % 4) * 4 + x
        return y * 4 + (x + q) % 4

    def signed_hot(row):
        s = lax.broadcasted_iota(jnp.int32, (SB, SB), 0)
        return jnp.where(jnp.abs(row) - 1 == s, jnp.where(row > 0, 1.0, -1.0), 0.0)

    def build_alpha(h):
        def body(n, _):
            g = reader(h, n // 8) * 8 + n % 8
            for k in range(3):
                row = alinks[k, pl.ds(g, 1), :]
                hot[h, n * 3 + k] = signed_hot(row).T.astype(BF16)
            return 0

        lax.fori_loop(0, 32, body, 0)

    def build_beta():
        def body(n, _):
            g = (z * 2 + (core + n // 8) % 2) * 8 + n % 8
            for k in range(3):
                row = blinks[k, pl.ds(g, 1), :]
                hot_b[n * 3 + k] = signed_hot(row).astype(BF16)
            return 0

        lax.fori_loop(0, 16, body, 0)

    def pieces(v):
        hi = v.astype(BF16)
        return hi, (v - hi.astype(F32)).astype(BF16)

    def compute_alpha(h, c):
        copies = [pltpu.make_async_copy(coef.at[:, cols(h, c)], stage.at[0], l_sem.at[0])]
        for q in range(3):
            copies.append(
                pltpu.make_async_copy(bufs[h].at[q, c], stage.at[q + 1], l_sem.at[q + 1])
            )
        for cp in copies:
            cp.start()
        for cp in copies:
            cp.wait()

        def split_body(n, _):
            rows = pl.ds(pl.multiple_of((n % 8) * SB, SB), SB)
            hi, lo = pieces(stage[n // 8, rows, :])
            split[n, 0:SB, :] = hi
            split[n, SB : 2 * SB, :] = lo
            return 0

        lax.fori_loop(0, 32, split_body, 0, unroll=2)

        def target(n):
            g = reader(h, n // 8) * 8 + n % 8
            acc = jnp.zeros((SB, SB), F32)
            for k in range(3):
                src = asrc[k, g]
                sy, sx = (src >> 5) & 3, (src >> 3) & 3
                if h == 0:
                    here, q = sy == y, (sx - x) & 3
                else:
                    here, q = sx == x, (sy - y) & 3
                weight = jnp.where(here, integral(apair[k, g]), 0.0)
                w = hot[h, n * 3 + k]
                acc += weight * jnp.dot(
                    jnp.concatenate([w, w], axis=1),
                    split[q * 8 + (src & 7)],
                    preferred_element_type=F32,
                )
            return acc

        def mine(n, _):
            rows = pl.ds(pl.multiple_of(n * SB, SB), SB)
            out[rows, cols(h, c)] += target(n)
            return 0

        lax.fori_loop(0, 8, mine, 0, unroll=4)

        def others(n, _):
            rows = pl.ds(pl.multiple_of((n % 8) * SB, SB), SB)
            part[h, c, n // 8 - 1, rows, :] = target(n)
            return 0

        lax.fori_loop(8, 32, others, 0, unroll=4)

    def compute_beta(c):
        rows = pl.ds(pl.multiple_of(c * SB, SB), SB)
        copies = [pltpu.make_async_copy(coef.at[rows], stage_b.at[0], l_sem.at[4])]
        for q in range(3):
            copies.append(
                pltpu.make_async_copy(gz.at[q, rows], stage_b.at[q + 1], l_sem.at[q + 5])
            )
        for cp in copies:
            cp.start()
        for cp in copies:
            cp.wait()

        def split_body(n, _):
            hi, lo = pieces(stage_b[n // 8, :, pl.ds(pl.multiple_of((n % 8) * SB, SB), SB)])
            split_b[n, :, 0:SB] = hi
            split_b[n, :, SB : 2 * SB] = lo
            return 0

        lax.fori_loop(0, 32, split_body, 0, unroll=2)

        def target(n):
            g = (z * 2 + (core + n // 8) % 2) * 8 + n % 8
            acc = jnp.zeros((SB, SB), F32)
            for k in range(3):
                src = bsrc[k, g]
                sz, sc = (src >> 4) & 3, (src >> 3) & 1
                weight = jnp.where(sc == core, integral(bpair[k, g]), 0.0)
                w = hot_b[n * 3 + k]
                acc += weight * jnp.dot(
                    split_b[((sz - z) & 3) * 8 + (src & 7)],
                    jnp.concatenate([w, w], axis=0),
                    preferred_element_type=F32,
                )
            return acc

        def mine(n, _):
            at = pl.ds(pl.multiple_of(n * SB, SB), SB)
            out[rows, at] += target(n)
            return 0

        lax.fori_loop(0, 8, mine, 0, unroll=4)

        def others(n, _):
            at = pl.ds(pl.multiple_of((n - 8) * SB, SB), SB)
            core_out[c, :, at] = target(n)
            return 0

        lax.fori_loop(8, 16, others, 0, unroll=4)

    def pass_on(h, c):
        for d in range(2):
            send_far(h, c, d).wait_recv()
            slot = 0 if d == 0 else 2

            def body(n, _):
                rows = pl.ds(pl.multiple_of(d * 512 + n * SB, SB), SB)
                part[h, c, slot, rows, :] += far[h, c, d, pl.ds(pl.multiple_of(n * SB, SB), SB), :]
                return 0

            lax.fori_loop(0, 4, body, 0)
            send_near(h, c, d).start()

    def finish(h, c):
        for d in range(2):
            send_near(h, c, d).wait_recv()

        def body(n, _):
            rows = pl.ds(pl.multiple_of(n * SB, SB), SB)
            out[rows, cols(h, c)] += near[h, c, 0, rows, :] + near[h, c, 1, rows, :]
            return 0

        lax.fori_loop(0, 8, body, 0)

    def finish_core(c):
        send_core(c).wait_recv()
        rows = pl.ds(pl.multiple_of(c * SB, SB), SB)
        out[rows, :] += core_in[c]

    barrier = pltpu.get_barrier_semaphore()
    for axis in ("x", "y", "z"):
        for d in range(2):
            pl.semaphore_signal(barrier, inc=1, device_id=step(axis, d), device_id_type=MESH)
    pl.semaphore_signal(barrier, inc=1, device_id=partner, device_id_type=MESH)
    pl.semaphore_wait(barrier, 7)

    for c in range(2):
        for d in range(2):
            own(0, c, d).start()
            own(1, c, d).start()
            own_z(c, d).start()

    out[...] = jnp.zeros_like(out)
    build_alpha(0)

    def move_on(c):
        for h in range(2):
            for d in range(2):
                own(h, c, d).wait_recv()
                relay(h, c, d).start()

        @pl.when(c < NCH - 2)
        def _():
            for h in range(2):
                for d in range(2):
                    own(h, c + 2, d).start()

    def move_on_z(c):
        for d in range(2):
            own_z(c, d).wait_recv()
            relay_z(c, d).start()

        @pl.when(c < NZ - 2)
        def _():
            for d in range(2):
                own_z(c + 2, d).start()

    move_on(0)
    move_on_z(0)
    build_alpha(1)
    build_beta()

    def loop(t, _):
        @pl.when(t < NCH - 1)
        def _():
            move_on(t + 1)

        @pl.when(t < NZ - 1)
        def _():
            move_on_z(t + 1)

        @pl.when(t < NCH)
        def _():
            for h in range(2):
                for d in range(2):
                    relay(h, t, d).wait_recv()
                compute_alpha(h, t)

        @pl.when(t == 2)
        def _():
            for c in range(2):
                for h in range(2):
                    for d in range(2):
                        send_far(h, c, d).start()

        @pl.when((t >= 2) & (t < NCH))
        def _():
            for h in range(2):
                for d in range(2):
                    send_far(h, t, d).start()

        @pl.when((t >= 3) & (t < 7))
        def _():
            for h in range(2):
                pass_on(h, t - 3)

        for d in range(2):
            relay_z(t, d).wait_recv()
        compute_beta(t)
        send_core(t).start()

        @pl.when(t >= 6)
        def _():
            for h in range(2):
                finish(h, t - 6)

        @pl.when(t >= 1)
        def _():
            finish_core(t - 1)

        return 0

    lax.fori_loop(0, NZ, loop, 0)
    finish_core(NZ - 1)

    def last(c, _):
        for h in range(2):
            finish(h, c)
        return 0

    lax.fori_loop(2, NCH, last, 0)

    def drain(c, _):
        for h in range(2):
            for d in range(2):
                own(h, c, d).wait_send()
                relay(h, c, d).wait_send()
                send_far(h, c, d).wait_send()
                send_near(h, c, d).wait_send()
        return 0

    lax.fori_loop(0, NCH, drain, 0)

    def drain_z(c, _):
        for d in range(2):
            own_z(c, d).wait_send()
            relay_z(c, d).wait_send()
        send_core(c).wait_send()
        return 0

    lax.fori_loop(0, NZ, drain_z, 0)


def any_couplings(coef, one_body, asrc, apair, alinks, bsrc, bpair, blinks):
    hbm = pl.BlockSpec(memory_space=pl.ANY)
    vmem = pl.BlockSpec(memory_space=pltpu.VMEM)
    smem = pl.BlockSpec(memory_space=pltpu.SMEM)
    dma = pltpu.SemaphoreType.DMA
    return pl.pallas_call(
        any_kernel,
        out_shape=[
            jax.ShapeDtypeStruct((1024, 1024), F32),
            jax.ShapeDtypeStruct((3, NCH, 1024, SB), F32),
            jax.ShapeDtypeStruct((3, NCH, 1024, SB), F32),
            jax.ShapeDtypeStruct((3, 1024, 1024), F32),
        ],
        in_specs=[hbm, smem, smem, vmem, smem, smem, vmem, smem],
        out_specs=[vmem, hbm, hbm, hbm],
        scratch_shapes=[
            pltpu.VMEM((4, 1024, SB), F32),
            pltpu.VMEM((4, SB, 1024), F32),
            pltpu.VMEM((32, 2 * SB, SB), BF16),
            pltpu.VMEM((32, SB, 2 * SB), BF16),
            pltpu.VMEM((2, NCH, 3, 1024, SB), F32),
            pltpu.VMEM((2, NCH, 2, 512, SB), F32),
            pltpu.VMEM((2, NCH, 2, 1024, SB), F32),
            pltpu.VMEM((NZ, SB, 1024), F32),
            pltpu.VMEM((NZ, SB, 1024), F32),
            pltpu.VMEM((2, 96, SB, SB), BF16),
            pltpu.VMEM((48, SB, SB), BF16),
            dma((2, 2, NCH, 2)),
            dma((2, 2, NCH, 2)),
            dma((2, NZ, 2)),
            dma((2, NZ, 2)),
            dma((2, 2, NCH, 2)),
            dma((2, 2, NCH, 2)),
            dma((NZ,)),
            dma((NZ,)),
            dma((8,)),
        ],
        compiler_params=pltpu.CompilerParams(
            collective_id=1, has_side_effects=True, vmem_limit_bytes=60 * 2**20
        ),
        name="any_couplings",
    )(coef, asrc, apair, alinks, bsrc, bpair, blinks, one_body)[0]


def on_device(
    coefficients,
    alpha_energy,
    beta_energy,
    one_body,
    alpha_source,
    alpha_pair,
    alpha_links,
    beta_source,
    beta_pair,
    beta_links,
):
    tables = (
        alpha_source.T,
        alpha_pair.T,
        alpha_links.transpose(1, 0, 2),
        beta_source.T,
        beta_pair.T,
        beta_links.transpose(1, 0, 2),
    )
    slots, fits = message_tables(tables[0])

    def with_slots():
        return named_sigma(coefficients, alpha_energy, beta_energy, one_body, *tables, slots)

    def without_slots():
        terms = any_couplings(coefficients, one_body, *tables)
        return (alpha_energy[:, None] + beta_energy[None, :]) * coefficients + terms

    return lax.cond(fits[0, 0] == 1, with_slots, without_slots)


def solution(mesh):
    in_specs = (P("alpha", "beta"), P("alpha"), P("beta"), P(), P(), P(), P(), P(), P(), P())
    out_specs = P("alpha", "beta")
    return jax.shard_map(
        on_device, mesh=mesh, in_specs=in_specs, out_specs=out_specs, check_vma=False
    )
```

```python
import jax
import jax.numpy as jnp
from jax import lax
from jax.experimental import pallas as pl
from jax.experimental.pallas import tpu as pltpu
from jax.sharding import PartitionSpec as P

MESH = pl.DeviceIdType.MESH
F32, BF16 = jnp.float32, jnp.bfloat16
SB = 128
NCH = 4
NZ = 8
SLOTS = 13

LINK = (1, 3, 4, 12)


def link_of(o, i):
    return (o + i) % 4


def spans(links):
    found = [0]
    for link in links:
        found = found + [v ^ LINK[link] for v in found]
    return found


def reader_masks(o):
    last, third = LINK[link_of(o, 3)], LINK[link_of(o, 2)]
    return (0, last, third, third ^ last)


HOT_SLOT = {m: i for i, m in enumerate(sorted({m for o in range(4) for m in reader_masks(o)}))}


def table_kernel(source, slots, fits):
    me = lax.axis_index("alpha")

    def iota(shape, axis):
        return lax.broadcasted_iota(jnp.int32, shape, axis)

    def mask_of(order, i):
        link = (order + i) % 4
        return jnp.where(link == 0, 1, jnp.where(link == 1, 3, jnp.where(link == 2, 4, 12)))

    def ones(mask):
        return jnp.where(mask, 1.0, 0.0).astype(BF16)

    def dot(left, right, axis=0):
        return lax.dot_general(left, right, (((1,), (axis,)), ((), ())), preferred_element_type=F32)

    row, lane = iota((64, 128), 0), iota((64, 128), 1)
    order, sender = row // 16, row % 16
    m1, m2, m3, m4 = (mask_of(order, i) for i in range(4))
    apart = (lane >> 3) ^ sender
    reader = apart ^ m2
    two_readers = (reader == 0) | (reader == m3) | (reader == m4) | (reader == (m3 ^ m4))
    two_sources = (apart == 0) | (apart == m1)
    device = lane ^ sender
    three_sources = (device == 0) | (device == m1) | (device == m2) | (device == (m1 ^ m2))
    three_readers = (apart == m3) | (apart == (m3 ^ m4))
    which = iota((128, 128), 0)
    named, fed = which < 0, which < 0
    for k in range(3):
        line = source[k : k + 1, :]
        named = named | (line == which)
        fed = fed | ((line >> 3) == which)
    two = two_sources & (dot(ones(two_readers), ones(named), 1) > 0.5)
    three = three_readers & (dot(ones(three_sources), ones(fed)) > 0.5)
    before = ones(which < iota((128, 128), 1))
    row, lane = iota((8, 64), 0), iota((8, 64), 1)
    order = row % 4
    at = iota((8, 128), 1)
    most = jnp.int32(0)
    for stage, messages in enumerate((two, three)):
        node = jnp.where(row < 4, me, me ^ mask_of(order, stage + 1))
        mine = dot(ones(lane == order * 16 + node), ones(messages))
        rank = dot(mine.astype(BF16), before).astype(jnp.int32)
        here = mine > 0.5
        chosen = jnp.zeros((8, 128), jnp.int32)
        for s in range(SLOTS):
            block = jnp.sum(jnp.where(here & (rank == s), at, 0), axis=1, keepdims=True)
            chosen = jnp.where(at == s, block, chosen)
        got = jnp.where(here, jnp.minimum(rank, SLOTS - 1), -1)
        slots[stage] = jnp.where(iota((8, 128), 0) < 4, chosen, got)
        count = jnp.sum(jnp.where(messages, 1, 0), axis=1, keepdims=True)
        most = jnp.maximum(most, jnp.max(count))
    fits[0, 0] = jnp.where(most <= SLOTS, 1, 0)


def message_tables(source):
    vmem = pl.BlockSpec(memory_space=pltpu.VMEM)
    return pl.pallas_call(
        table_kernel,
        out_shape=[
            jax.ShapeDtypeStruct((2, 8, 128), jnp.int32),
            jax.ShapeDtypeStruct((1, 1), jnp.int32),
        ],
        in_specs=[vmem],
        out_specs=[vmem, pl.BlockSpec(memory_space=pltpu.SMEM)],
        name="message_tables",
    )(source)


def named_kernel(
    coef,
    asrc,
    apair,
    alinks_hbm,
    bsrc,
    bpair,
    blinks_hbm,
    table,
    slots,
    energy_a,
    energy_b,
    out_hbm,
    tail,
    got1,
    got2,
    gz,
    gc,
    gf,
    got_b,
    out,
    alinks,
    blinks,
    stage,
    split,
    held,
    pack,
    part3,
    *rest,
):
    got3, rest = rest[:8], rest[8:]
    part4, got4, stage_b, split_b, part_b, hot, hot_b, rows_a, *rest = rest
    at_own, weight_own, at_sent, weight_sent, hot_sent, s_sem, r_sem, zs_sem, zr_sem, l_sem = rest
    a = lax.axis_index("alpha")
    b = lax.axis_index("beta")
    y, x, z, core = a // 4, a % 4, b // 2, b % 2

    def over(place, link):
        py, px = place
        if link == 0:
            return (py, px + 1 - 2 * (px % 2))
        if link == 1:
            return (py, 3 - px)
        if link == 2:
            return (py + 1 - 2 * (py % 2), px)
        return (3 - py, px)

    def index(place):
        return place[0] * 4 + place[1]

    def peer(link):
        return (index(over((y, x), link)), b)

    def over_z(pair):
        return z + 1 - 2 * (z % 2) if pair == 0 else 3 - z

    partner = (a, z * 2 + 1 - core)

    def choose(o, values):
        return jnp.where(
            o == 0, values[0], jnp.where(o == 1, values[1], jnp.where(o == 2, values[2], values[3]))
        )

    def each(o, act):
        for k in range(4):

            @pl.when(o == k)
            def _(k=k):
                act(k)

    def columns(w, o):
        return pl.ds(pl.multiple_of((w * 4 + o) * SB, SB), SB)

    def block(n):
        return pl.ds(pl.multiple_of(n * SB, SB), SB)

    def send(i, w, o):
        ch = w * 4 + o
        src = (coef.at[:, :, columns(w, o)], pack.at[ch], part3.at[ch], part4.at[ch])[i]
        if i == 2:
            dst = got3[ch]
        elif i == 3:
            dst = (got4, tail)[w].at[o]
        else:
            dst = (got1, got2)[i].at[ch]
        return pltpu.make_async_remote_copy(
            src_ref=src,
            dst_ref=dst,
            send_sem=s_sem.at[i, ch],
            recv_sem=r_sem.at[i, ch],
            device_id=peer(link_of(o, i)),
            device_id_type=MESH,
        )

    def blocks_b(h, c):
        return pl.ds(h * 4 + c * 2, 2)

    def send_z(h, c):
        return pltpu.make_async_remote_copy(
            src_ref=coef.at[blocks_b(h, c)],
            dst_ref=gz.at[blocks_b(h, c)],
            send_sem=zs_sem.at[0, h, c],
            recv_sem=zr_sem.at[0, h, c],
            device_id=(a, over_z(h) * 2 + core),
            device_id_type=MESH,
        )

    def send_c(h, c):
        return pltpu.make_async_remote_copy(
            src_ref=coef.at[blocks_b(h, c)],
            dst_ref=gc.at[blocks_b(h, c)],
            send_sem=zs_sem.at[1, h, c],
            recv_sem=zr_sem.at[1, h, c],
            device_id=partner,
            device_id_type=MESH,
        )

    def send_f(h, c):
        return pltpu.make_async_remote_copy(
            src_ref=gz.at[blocks_b(h, c)],
            dst_ref=gf.at[blocks_b(h, c)],
            send_sem=zs_sem.at[2, h, c],
            recv_sem=zr_sem.at[2, h, c],
            device_id=partner,
            device_id_type=MESH,
        )

    def send_b(h, c):
        return pltpu.make_async_remote_copy(
            src_ref=part_b.at[h],
            dst_ref=got_b.at[blocks_b(h, c)],
            send_sem=zs_sem.at[3, h, c],
            recv_sem=zr_sem.at[3, h, c],
            device_id=(a, over_z(1 - h) * 2 + core),
            device_id_type=MESH,
        )

    def integral(pair):
        p = pair // 18
        return table[p, pair - p * 18]

    def signed_hot(row):
        s = lax.broadcasted_iota(jnp.int32, (SB, SB), 0)
        return jnp.where(jnp.abs(row) - 1 == s, jnp.where(row > 0, 1.0, -1.0), 0.0)

    def pieces(v):
        hi = v.astype(BF16)
        return hi, (v - hi.astype(F32)).astype(BF16)

    def build_alpha():
        for mask, slot in HOT_SLOT.items():
            place = (y, x)
            for link in range(4):
                if mask & 3 == LINK[link] or mask & 12 == LINK[link]:
                    place = over(place, link)
            if mask & 3 == 2:
                place = over(over(place, 0), 1)
            if mask & 12 == 8:
                place = over(over(place, 2), 3)
            reader = index(place)

            def body(n, _, slot=slot, reader=reader):
                for k in range(3):
                    row = alinks[k, pl.ds(reader * 8 + n, 1), :]
                    hot[slot, k * 8 + n] = signed_hot(row).T.astype(BF16)
                return 0

            lax.fori_loop(0, 8, body, 0, unroll=4)

    def plan():
        def body(o, _):
            m1 = choose(o, [LINK[link_of(k, 0)] for k in range(4)])
            m2 = choose(o, [LINK[link_of(k, 1)] for k in range(4)])
            m3 = choose(o, [LINK[link_of(k, 2)] for k in range(4)])
            last = choose(o, [peer(link_of(k, 3))[0] for k in range(4)])
            hots = [
                choose(o, [HOT_SLOT[reader_masks(k)[role]] for k in range(4)])
                for role in range(2, 4)
            ]

            def entry(g, k):
                src = asrc[k, g]
                apart = (src >> 3) ^ a
                inner = src & 7
                over_two = (apart == m2) | (apart == (m1 ^ m2))
                here = over_two | (apart == 0) | (apart == m1)
                arrived = 16 + jnp.maximum(slots[0, 4 + o, src], 0)
                at = jnp.where(over_two, arrived, jnp.where(apart == m1, 8 + inner, inner))
                return at, jnp.where(here, integral(apair[k, g]), 0.0)

            def own_entries(n, _):
                for role, reader in enumerate((a, last)):
                    for k in range(3):
                        at, weight = entry(reader * 8 + n, k)
                        at_own[o, role * 24 + n * 3 + k] = at
                        weight_own[o, role * 24 + n * 3 + k] = weight
                return 0

            lax.fori_loop(0, 8, own_entries, 0)

            def sent_entries(s, _):
                g = slots[1, o, s]
                hot_sent[o, s] = jnp.where(((g >> 3) ^ a) == m3, hots[0], hots[1])
                hot_sent[o, SLOTS + s] = g & 7
                for k in range(3):
                    at, weight = entry(g, k)
                    at_sent[o, s * 3 + k] = at
                    weight_sent[o, s * 3 + k] = weight
                return 0

            lax.fori_loop(0, SLOTS, sent_entries, 0)
            return 0

        lax.fori_loop(0, 4, body, 0)

    def build_beta():
        for slot in range(3):
            reader = (z if slot == 0 else over_z(slot - 1)) * 2 + core

            def body(n, _, slot=slot, reader=reader):
                for k in range(3):
                    row = blinks[k, pl.ds(reader * 8 + n, 1), :]
                    hot_b[slot, n * 3 + k] = signed_hot(row).astype(BF16)
                return 0

            lax.fori_loop(0, 8, body, 0, unroll=4)

    def load(w, o, buf, second):
        copies = [
            pltpu.make_async_copy(
                coef.at[:, :, columns(w, o)], stage.at[buf, pl.ds(0, 8)], l_sem.at[buf, 0]
            ),
            pltpu.make_async_copy(
                got1.at[w * 4 + o], stage.at[buf, pl.ds(8, 8)], l_sem.at[buf, 1]
            ),
        ]
        if second:
            copies.append(
                pltpu.make_async_copy(
                    got2.at[w * 4 + o], stage.at[buf, pl.ds(16, SLOTS)], l_sem.at[buf, 2]
                )
            )
        return copies

    def start_load(w, o, second):
        for cp in load(w, o, o % 2, second):
            cp.start()

    def wait_load(w, o, second):
        for cp in load(w, o, o % 2, second):
            cp.wait()

    def ready(w, o, i):
        def first(k):
            if k == 0:
                send(i, w, 0).wait_recv()
                start_load(w, 0, i == 1)
            if k < 3:
                send(i, w, k + 1).wait_recv()
                start_load(w, k + 1, i == 1)
            wait_load(w, k, i == 1)

        each(o, first)

    def second_exchange(w):
        def body(o, _):
            ready(w, o, 0)
            buf = o % 2

            def hold(n, _):
                held[n] = stage[buf, n]
                return 0

            lax.fori_loop(0, 16, hold, 0, unroll=4)

            def fill(s, _):
                wanted = slots[0, o, s]
                at = jnp.where((wanted >> 3) == a, 0, 8) + (wanted & 7)
                pack[w * 4 + o, s] = held[at]
                return 0

            lax.fori_loop(0, SLOTS, fill, 0)
            each(o, lambda k: send(1, w, k).start())
            return 0

        lax.fori_loop(0, 4, body, 0)

    def third_exchange(w):
        def body(o, _):
            ready(w, o, 1)
            buf = o % 2
            ch = w * 4 + o
            hots = [
                choose(o, [HOT_SLOT[reader_masks(k)[role]] for k in range(4)]) for role in range(2)
            ]

            def split_body(n, _):
                hi, lo = pieces(stage[buf, n])
                split[n, 0:SB, :] = hi
                split[n, SB : 2 * SB, :] = lo
                return 0

            lax.fori_loop(0, 16 + SLOTS, split_body, 0, unroll=8)

            def product(at, w_k):
                return jnp.dot(
                    jnp.concatenate([w_k, w_k], axis=1), split[at], preferred_element_type=F32
                )

            def others(s, _):
                acc = jnp.zeros((SB, SB), F32)
                for k in range(3):
                    w_k = hot[hot_sent[o, s], k * 8 + hot_sent[o, SLOTS + s]]
                    acc += weight_sent[o, s * 3 + k] * product(at_sent[o, s * 3 + k], w_k)
                part3[ch, s] = acc
                return 0

            lax.fori_loop(0, SLOTS, others, 0, unroll=SLOTS)
            each(o, lambda k: send(2, w, k).start())

            def target(role, n):
                acc = jnp.zeros((SB, SB), F32)
                for k in range(3):
                    e = role * 24 + n * 3 + k
                    acc += weight_own[o, e] * product(at_own[o, e], hot[hots[role], k * 8 + n])
                return acc

            def mine(n, _):
                energy = rows_a[n] + energy_b[:, columns(w, o)]
                out[block(n), columns(w, o)] += energy * stage[buf, n] + target(0, n)
                return 0

            lax.fori_loop(0, 8, mine, 0, unroll=8)

            def across(n, _):
                part4[ch, n] = target(1, n)
                return 0

            lax.fori_loop(0, 8, across, 0, unroll=8)
            return 0

        lax.fori_loop(0, 4, body, 0)

    def fourth_exchange(w):
        for o in range(4):
            ch = w * 4 + o
            send(2, w, o).wait_recv()
            last = peer(link_of(o, 3))[0]

            def came(g, o=o, ch=ch):
                at = slots[1, 4 + o, g]
                return got3[ch][jnp.maximum(at, 0)] * jnp.where(at >= 0, 1.0, 0.0)

            def across(n, _, ch=ch, last=last, came=came):
                part4[ch, n] += came(last * 8 + n)
                return 0

            lax.fori_loop(0, 8, across, 0, unroll=2)
            send(3, w, o).start()

            def mine(n, _, o=o, came=came):
                out[block(n), columns(w, o)] += came(a * 8 + n)
                return 0

            lax.fori_loop(0, 8, mine, 0, unroll=2)

    def write(w):
        at = pl.ds(w * 512, 512)
        return pltpu.make_async_copy(out.at[:, at], out_hbm.at[:, at], l_sem.at[w, 3])

    def finish():
        for o in range(4):
            send(3, 0, o).wait_recv()

            def mine(n, _, o=o):
                out[block(n), columns(0, o)] += got4[o, n]
                return 0

            lax.fori_loop(0, 8, mine, 0, unroll=2)

    def compute_b(h, c):
        rows = pl.ds(h * 512 + c * 256, 256)
        send_c(h, c).wait_recv()
        send_f(h, c).wait_recv()
        sources = (coef, gc, gz, gf)
        copies = [
            pltpu.make_async_copy(sources[q].at[blocks_b(h, c)], stage_b.at[q % 2], l_sem.at[2 + q % 2, 0])
            for q in range(4)
        ]
        copies[0].start()
        copies[1].start()
        for q in range(4):
            copies[q].wait()

            def split_body(n, _, q=q):
                hi, lo = pieces(stage_b[q % 2, :, :, block(n)].reshape(256, SB))
                split_b[q * 8 + n, :, 0:SB] = hi
                split_b[q * 8 + n, :, SB : 2 * SB] = lo
                return 0

            lax.fori_loop(0, 8, split_body, 0, unroll=2)
            if q < 2:
                copies[q + 2].start()

        def target(reader, n, slot):
            g = reader * 8 + n
            acc = jnp.zeros((256, SB), F32)
            for k in range(3):
                src = bsrc[k, g]
                sz, sc = src >> 4, (src >> 3) & 1
                away = sz ^ z
                here = (away == 0) | (away == (1 if h == 0 else 3))
                at = jnp.where(away == 0, 0, 16) + jnp.where(sc == core, 0, 8) + (src & 7)
                weight = jnp.where(here, integral(bpair[k, g]), 0.0)
                w_k = hot_b[slot, n * 3 + k]
                acc += weight * jnp.dot(
                    split_b[at], jnp.concatenate([w_k, w_k], axis=0), preferred_element_type=F32
                )
            return acc

        def others(n, _):
            part_b[h, :, :, block(n)] = target(over_z(1 - h) * 2 + core, n, 2 - h).reshape(2, SB, SB)
            return 0

        if c == 1:
            send_b(h, 0).wait_send()
        lax.fori_loop(0, 8, others, 0, unroll=4)
        send_b(h, c).start()

        def mine(n, _):
            out[rows, block(n)] += target(b, n, 0)
            return 0

        lax.fori_loop(0, 8, mine, 0, unroll=4)

    def finish_b(h, c):
        send_b(h, c).wait_recv()
        cp = pltpu.make_async_copy(got_b.at[blocks_b(h, c)], stage_b.at[c], l_sem.at[2 + c, 1])
        cp.start()
        cp.wait()
        out[pl.ds(h * 512 + c * 256, 256), :] += stage_b[c].reshape(256, 1024)

    barrier = pltpu.get_barrier_semaphore()
    everyone = [peer(link) for link in range(4)]
    everyone += [(a, over_z(0) * 2 + core), (a, over_z(1) * 2 + core), partner]
    for device in everyone:
        pl.semaphore_signal(barrier, inc=1, device_id=device, device_id_type=MESH)
    pl.semaphore_wait(barrier, len(everyone))

    links = [
        pltpu.make_async_copy(alinks_hbm, alinks, l_sem.at[0, 4]),
        pltpu.make_async_copy(blinks_hbm, blinks, l_sem.at[1, 4]),
    ]
    for cp in links:
        cp.start()
    for w in range(2):
        for o in range(4):
            send(0, w, o).start()
    for c in range(2):
        for h in range(2):
            send_z(h, c).start()
            send_c(h, c).start()
    for cp in links:
        cp.wait()
    build_alpha()
    for n in range(8):
        rows_a[n] = jnp.broadcast_to(energy_a[n : n + 1, :], (SB, SB)).T
    out[...] = jnp.zeros_like(out)
    plan()
    second_exchange(0)
    build_beta()
    second_exchange(1)
    for h in range(2):
        send_z(h, 0).wait_recv()
        send_f(h, 0).start()
    for h in range(2):
        compute_b(h, 0)
    third_exchange(0)
    for h in range(2):
        send_z(h, 1).wait_recv()
        send_f(h, 1).start()
    third_exchange(1)
    for h in range(2):
        compute_b(h, 1)
    fourth_exchange(0)
    for h in range(2):
        finish_b(h, 0)
    fourth_exchange(1)
    for h in range(2):
        finish_b(h, 1)
    write(1).start()
    finish()
    write(0).start()
    for o in range(4):
        send(3, 1, o).wait_recv()
    for w in range(2):
        write(w).wait()
        for o in range(4):
            for i in range(4):
                send(i, w, o).wait_send()
    for c in range(2):
        for h in range(2):
            for copy in (send_z, send_c, send_f):
                copy(h, c).wait_send()
            if c == 1:
                send_b(h, c).wait_send()


def named_sigma(coef, energy_a, energy_b, one_body, asrc, apair, alinks, bsrc, bpair, blinks, slots):
    hbm = pl.BlockSpec(memory_space=pl.ANY)
    smem = pl.BlockSpec(memory_space=pltpu.SMEM)
    vmem = pl.BlockSpec(memory_space=pltpu.VMEM)
    dma = pltpu.SemaphoreType.DMA
    whole = jax.ShapeDtypeStruct((8, SB, 1024), F32)
    return pl.pallas_call(
        named_kernel,
        out_shape=[
            jax.ShapeDtypeStruct((1024, 1024), F32),
            jax.ShapeDtypeStruct((4, 8, SB, SB), F32),
            jax.ShapeDtypeStruct((8, 8, SB, SB), F32),
            jax.ShapeDtypeStruct((8, SLOTS, SB, SB), F32),
            whole,
            whole,
            whole,
            whole,
        ],
        in_specs=[hbm, smem, smem, hbm, smem, smem, hbm, smem, smem, vmem, vmem],
        out_specs=[hbm] * 8,
        scratch_shapes=[
            pltpu.VMEM((1024, 1024), F32),
            pltpu.VMEM((3, 128, SB), jnp.int32),
            pltpu.VMEM((3, 64, SB), jnp.int32),
            pltpu.VMEM((2, 16 + SLOTS, SB, SB), F32),
            pltpu.VMEM((16 + SLOTS, 2 * SB, SB), BF16),
            pltpu.VMEM((16, SB, SB), F32),
            pltpu.VMEM((8, SLOTS, SB, SB), F32),
            pltpu.VMEM((8, SLOTS, SB, SB), F32),
            *[pltpu.VMEM((SLOTS, SB, SB), F32)] * 8,
            pltpu.VMEM((8, 8, SB, SB), F32),
            pltpu.VMEM((4, 8, SB, SB), F32),
            pltpu.VMEM((2, 2, SB, 1024), F32),
            pltpu.VMEM((32, 256, 2 * SB), BF16),
            pltpu.VMEM((2, 2, SB, 1024), F32),
            pltpu.VMEM((len(HOT_SLOT), 24, SB, SB), BF16),
            pltpu.VMEM((3, 24, SB, SB), BF16),
            pltpu.VMEM((8, SB, SB), F32),
            pltpu.SMEM((4, 48), jnp.int32),
            pltpu.SMEM((4, 48), F32),
            pltpu.SMEM((4, 3 * SLOTS), jnp.int32),
            pltpu.SMEM((4, 3 * SLOTS), F32),
            pltpu.SMEM((4, 2 * SLOTS), jnp.int32),
            dma((4, 8)),
            dma((4, 8)),
            dma((4, 2, 2)),
            dma((4, 2, 2)),
            dma((4, 5)),
        ],
        compiler_params=pltpu.CompilerParams(
            collective_id=0, has_side_effects=True, vmem_limit_bytes=109 * 2**19
        ),
        name="named_sigma",
    )(
        coef.reshape(8, SB, 1024),
        asrc,
        apair,
        alinks,
        bsrc,
        bpair,
        blinks,
        one_body,
        slots,
        energy_a.reshape(8, SB),
        energy_b.reshape(1, 1024),
    )[:2]


def finish_kernel(part, tail, sigma, half, sems):
    first = pl.ds(0, 512)
    copies = [pltpu.make_async_copy(part.at[:, first], sigma.at[:, first], sems.at[4])]
    copies[0].start()
    for o in range(4):
        at = pl.ds(512 + o * SB, SB)
        for n in range(8):
            rows = pl.ds(n * SB, SB)
            half[o, rows, :] = part[rows, at] + tail[o, n]
        copies.append(pltpu.make_async_copy(half.at[o], sigma.at[:, at], sems.at[o]))
        copies[-1].start()
    for copy in copies:
        copy.wait()


def finish_sigma(part, tail):
    vmem = pl.BlockSpec(memory_space=pltpu.VMEM)
    return pl.pallas_call(
        finish_kernel,
        out_shape=jax.ShapeDtypeStruct((1024, 1024), F32),
        in_specs=[vmem, vmem],
        out_specs=pl.BlockSpec(memory_space=pl.ANY),
        scratch_shapes=[pltpu.VMEM((4, 1024, SB), F32), pltpu.SemaphoreType.DMA((5,))],
        compiler_params=pltpu.CompilerParams(vmem_limit_bytes=16 * 2**20),
        name="finish_sigma",
    )(part, tail)


def any_kernel(
    coef,
    asrc,
    apair,
    alinks,
    bsrc,
    bpair,
    blinks,
    table,
    out,
    gx,
    gy,
    gz,
    stage,
    stage_b,
    split,
    split_b,
    part,
    far,
    near,
    core_out,
    core_in,
    hot,
    hot_b,
    g_send,
    g_recv,
    z_send,
    z_recv,
    r_send,
    r_recv,
    c_send,
    c_recv,
    l_sem,
):
    a = lax.axis_index("alpha")
    b = lax.axis_index("beta")
    y, x, z, core = a // 4, a % 4, b // 2, b % 2

    def step(axis, d):
        s = 1 if d == 0 else 3
        if axis == "x":
            return (y * 4 + (x + s) % 4, b)
        if axis == "y":
            return (((y + s) % 4) * 4 + x, b)
        return (a, ((z + s) % 4) * 2 + core)

    partner = (a, z * 2 + 1 - core)

    def cols(h, c):
        return pl.ds(pl.multiple_of(h * 512 + c * SB, SB), SB)

    axes = ("x", "y")
    bufs = (gx, gy)

    def own(h, c, d):
        return pltpu.make_async_remote_copy(
            src_ref=coef.at[:, cols(h, c)],
            dst_ref=bufs[h].at[2 if d == 0 else 0, c],
            send_sem=g_send.at[h, 0, c, d],
            recv_sem=g_recv.at[h, 0, c, d],
            device_id=step(axes[h], d),
            device_id_type=MESH,
        )

    def relay(h, c, d):
        rows = pl.ds(d * 512, 512)
        return pltpu.make_async_remote_copy(
            src_ref=bufs[h].at[2 if d == 0 else 0, c, rows],
            dst_ref=bufs[h].at[1, c, rows],
            send_sem=g_send.at[h, 1, c, d],
            recv_sem=g_recv.at[h, 1, c, d],
            device_id=step(axes[h], d),
            device_id_type=MESH,
        )

    def own_z(c, d):
        rows = pl.ds(pl.multiple_of(c * SB, SB), SB)
        return pltpu.make_async_remote_copy(
            src_ref=coef.at[rows],
            dst_ref=gz.at[2 if d == 0 else 0, rows],
            send_sem=z_send.at[0, c, d],
            recv_sem=z_recv.at[0, c, d],
            device_id=step("z", d),
            device_id_type=MESH,
        )

    def relay_z(c, d):
        rows = pl.ds(pl.multiple_of(c * SB + d * 64, 64), 64)
        return pltpu.make_async_remote_copy(
            src_ref=gz.at[2 if d == 0 else 0, rows],
            dst_ref=gz.at[1, rows],
            send_sem=z_send.at[1, c, d],
            recv_sem=z_recv.at[1, c, d],
            device_id=step("z", d),
            device_id_type=MESH,
        )

    def send_far(h, c, d):
        return pltpu.make_async_remote_copy(
            src_ref=part.at[h, c, 1, pl.ds(d * 512, 512)],
            dst_ref=far.at[h, c, d],
            send_sem=r_send.at[h, 0, c, d],
            recv_sem=r_recv.at[h, 0, c, d],
            device_id=step(axes[1 - h], d),
            device_id_type=MESH,
        )

    def send_near(h, c, d):
        return pltpu.make_async_remote_copy(
            src_ref=part.at[h, c, 0 if d == 0 else 2],
            dst_ref=near.at[h, c, d],
            send_sem=r_send.at[h, 1, c, d],
            recv_sem=r_recv.at[h, 1, c, d],
            device_id=step(axes[1 - h], d),
            device_id_type=MESH,
        )

    def send_core(c):
        return pltpu.make_async_remote_copy(
            src_ref=core_out.at[c],
            dst_ref=core_in.at[c],
            send_sem=c_send.at[c],
            recv_sem=c_recv.at[c],
            device_id=partner,
            device_id_type=MESH,
        )

    def integral(pair):
        p = pair // 18
        return table[p, pair - p * 18]

    def reader(h, q):
        if h == 0:
            return ((y + q) % 4) * 4 + x
        return y * 4 + (x + q) % 4

    def signed_hot(row):
        s = lax.broadcasted_iota(jnp.int32, (SB, SB), 0)
        return jnp.where(jnp.abs(row) - 1 == s, jnp.where(row > 0, 1.0, -1.0), 0.0)

    def build_alpha(h):
        def body(n, _):
            g = reader(h, n // 8) * 8 + n % 8
            for k in range(3):
                row = alinks[k, pl.ds(g, 1), :]
                hot[h, n * 3 + k] = signed_hot(row).T.astype(BF16)
            return 0

        lax.fori_loop(0, 32, body, 0)

    def build_beta():
        def body(n, _):
            g = (z * 2 + (core + n // 8) % 2) * 8 + n % 8
            for k in range(3):
                row = blinks[k, pl.ds(g, 1), :]
                hot_b[n * 3 + k] = signed_hot(row).astype(BF16)
            return 0

        lax.fori_loop(0, 16, body, 0)

    def pieces(v):
        hi = v.astype(BF16)
        return hi, (v - hi.astype(F32)).astype(BF16)

    def compute_alpha(h, c):
        copies = [pltpu.make_async_copy(coef.at[:, cols(h, c)], stage.at[0], l_sem.at[0])]
        for q in range(3):
            copies.append(
                pltpu.make_async_copy(bufs[h].at[q, c], stage.at[q + 1], l_sem.at[q + 1])
            )
        for cp in copies:
            cp.start()
        for cp in copies:
            cp.wait()

        def split_body(n, _):
            rows = pl.ds(pl.multiple_of((n % 8) * SB, SB), SB)
            hi, lo = pieces(stage[n // 8, rows, :])
            split[n, 0:SB, :] = hi
            split[n, SB : 2 * SB, :] = lo
            return 0

        lax.fori_loop(0, 32, split_body, 0, unroll=2)

        def target(n):
            g = reader(h, n // 8) * 8 + n % 8
            acc = jnp.zeros((SB, SB), F32)
            for k in range(3):
                src = asrc[k, g]
                sy, sx = (src >> 5) & 3, (src >> 3) & 3
                if h == 0:
                    here, q = sy == y, (sx - x) & 3
                else:
                    here, q = sx == x, (sy - y) & 3
                weight = jnp.where(here, integral(apair[k, g]), 0.0)
                w = hot[h, n * 3 + k]
                acc += weight * jnp.dot(
                    jnp.concatenate([w, w], axis=1),
                    split[q * 8 + (src & 7)],
                    preferred_element_type=F32,
                )
            return acc

        def mine(n, _):
            rows = pl.ds(pl.multiple_of(n * SB, SB), SB)
            out[rows, cols(h, c)] += target(n)
            return 0

        lax.fori_loop(0, 8, mine, 0, unroll=4)

        def others(n, _):
            rows = pl.ds(pl.multiple_of((n % 8) * SB, SB), SB)
            part[h, c, n // 8 - 1, rows, :] = target(n)
            return 0

        lax.fori_loop(8, 32, others, 0, unroll=4)

    def compute_beta(c):
        rows = pl.ds(pl.multiple_of(c * SB, SB), SB)
        copies = [pltpu.make_async_copy(coef.at[rows], stage_b.at[0], l_sem.at[4])]
        for q in range(3):
            copies.append(
                pltpu.make_async_copy(gz.at[q, rows], stage_b.at[q + 1], l_sem.at[q + 5])
            )
        for cp in copies:
            cp.start()
        for cp in copies:
            cp.wait()

        def split_body(n, _):
            hi, lo = pieces(stage_b[n // 8, :, pl.ds(pl.multiple_of((n % 8) * SB, SB), SB)])
            split_b[n, :, 0:SB] = hi
            split_b[n, :, SB : 2 * SB] = lo
            return 0

        lax.fori_loop(0, 32, split_body, 0, unroll=2)

        def target(n):
            g = (z * 2 + (core + n // 8) % 2) * 8 + n % 8
            acc = jnp.zeros((SB, SB), F32)
            for k in range(3):
                src = bsrc[k, g]
                sz, sc = (src >> 4) & 3, (src >> 3) & 1
                weight = jnp.where(sc == core, integral(bpair[k, g]), 0.0)
                w = hot_b[n * 3 + k]
                acc += weight * jnp.dot(
                    split_b[((sz - z) & 3) * 8 + (src & 7)],
                    jnp.concatenate([w, w], axis=0),
                    preferred_element_type=F32,
                )
            return acc

        def mine(n, _):
            at = pl.ds(pl.multiple_of(n * SB, SB), SB)
            out[rows, at] += target(n)
            return 0

        lax.fori_loop(0, 8, mine, 0, unroll=4)

        def others(n, _):
            at = pl.ds(pl.multiple_of((n - 8) * SB, SB), SB)
            core_out[c, :, at] = target(n)
            return 0

        lax.fori_loop(8, 16, others, 0, unroll=4)

    def pass_on(h, c):
        for d in range(2):
            send_far(h, c, d).wait_recv()
            slot = 0 if d == 0 else 2

            def body(n, _):
                rows = pl.ds(pl.multiple_of(d * 512 + n * SB, SB), SB)
                part[h, c, slot, rows, :] += far[h, c, d, pl.ds(pl.multiple_of(n * SB, SB), SB), :]
                return 0

            lax.fori_loop(0, 4, body, 0)
            send_near(h, c, d).start()

    def finish(h, c):
        for d in range(2):
            send_near(h, c, d).wait_recv()

        def body(n, _):
            rows = pl.ds(pl.multiple_of(n * SB, SB), SB)
            out[rows, cols(h, c)] += near[h, c, 0, rows, :] + near[h, c, 1, rows, :]
            return 0

        lax.fori_loop(0, 8, body, 0)

    def finish_core(c):
        send_core(c).wait_recv()
        rows = pl.ds(pl.multiple_of(c * SB, SB), SB)
        out[rows, :] += core_in[c]

    barrier = pltpu.get_barrier_semaphore()
    for axis in ("x", "y", "z"):
        for d in range(2):
            pl.semaphore_signal(barrier, inc=1, device_id=step(axis, d), device_id_type=MESH)
    pl.semaphore_signal(barrier, inc=1, device_id=partner, device_id_type=MESH)
    pl.semaphore_wait(barrier, 7)

    for c in range(2):
        for d in range(2):
            own(0, c, d).start()
            own(1, c, d).start()
            own_z(c, d).start()

    out[...] = jnp.zeros_like(out)
    build_alpha(0)

    def move_on(c):
        for h in range(2):
            for d in range(2):
                own(h, c, d).wait_recv()
                relay(h, c, d).start()

        @pl.when(c < NCH - 2)
        def _():
            for h in range(2):
                for d in range(2):
                    own(h, c + 2, d).start()

    def move_on_z(c):
        for d in range(2):
            own_z(c, d).wait_recv()
            relay_z(c, d).start()

        @pl.when(c < NZ - 2)
        def _():
            for d in range(2):
                own_z(c + 2, d).start()

    move_on(0)
    move_on_z(0)
    build_alpha(1)
    build_beta()

    def loop(t, _):
        @pl.when(t < NCH - 1)
        def _():
            move_on(t + 1)

        @pl.when(t < NZ - 1)
        def _():
            move_on_z(t + 1)

        @pl.when(t < NCH)
        def _():
            for h in range(2):
                for d in range(2):
                    relay(h, t, d).wait_recv()
                compute_alpha(h, t)

        @pl.when(t == 2)
        def _():
            for c in range(2):
                for h in range(2):
                    for d in range(2):
                        send_far(h, c, d).start()

        @pl.when((t >= 2) & (t < NCH))
        def _():
            for h in range(2):
                for d in range(2):
                    send_far(h, t, d).start()

        @pl.when((t >= 3) & (t < 7))
        def _():
            for h in range(2):
                pass_on(h, t - 3)

        for d in range(2):
            relay_z(t, d).wait_recv()
        compute_beta(t)
        send_core(t).start()

        @pl.when(t >= 6)
        def _():
            for h in range(2):
                finish(h, t - 6)

        @pl.when(t >= 1)
        def _():
            finish_core(t - 1)

        return 0

    lax.fori_loop(0, NZ, loop, 0)
    finish_core(NZ - 1)

    def last(c, _):
        for h in range(2):
            finish(h, c)
        return 0

    lax.fori_loop(2, NCH, last, 0)

    def drain(c, _):
        for h in range(2):
            for d in range(2):
                own(h, c, d).wait_send()
                relay(h, c, d).wait_send()
                send_far(h, c, d).wait_send()
                send_near(h, c, d).wait_send()
        return 0

    lax.fori_loop(0, NCH, drain, 0)

    def drain_z(c, _):
        for d in range(2):
            own_z(c, d).wait_send()
            relay_z(c, d).wait_send()
        send_core(c).wait_send()
        return 0

    lax.fori_loop(0, NZ, drain_z, 0)


def any_couplings(coef, one_body, asrc, apair, alinks, bsrc, bpair, blinks):
    hbm = pl.BlockSpec(memory_space=pl.ANY)
    vmem = pl.BlockSpec(memory_space=pltpu.VMEM)
    smem = pl.BlockSpec(memory_space=pltpu.SMEM)
    dma = pltpu.SemaphoreType.DMA
    return pl.pallas_call(
        any_kernel,
        out_shape=[
            jax.ShapeDtypeStruct((1024, 1024), F32),
            jax.ShapeDtypeStruct((3, NCH, 1024, SB), F32),
            jax.ShapeDtypeStruct((3, NCH, 1024, SB), F32),
            jax.ShapeDtypeStruct((3, 1024, 1024), F32),
        ],
        in_specs=[hbm, smem, smem, vmem, smem, smem, vmem, smem],
        out_specs=[vmem, hbm, hbm, hbm],
        scratch_shapes=[
            pltpu.VMEM((4, 1024, SB), F32),
            pltpu.VMEM((4, SB, 1024), F32),
            pltpu.VMEM((32, 2 * SB, SB), BF16),
            pltpu.VMEM((32, SB, 2 * SB), BF16),
            pltpu.VMEM((2, NCH, 3, 1024, SB), F32),
            pltpu.VMEM((2, NCH, 2, 512, SB), F32),
            pltpu.VMEM((2, NCH, 2, 1024, SB), F32),
            pltpu.VMEM((NZ, SB, 1024), F32),
            pltpu.VMEM((NZ, SB, 1024), F32),
            pltpu.VMEM((2, 96, SB, SB), BF16),
            pltpu.VMEM((48, SB, SB), BF16),
            dma((2, 2, NCH, 2)),
            dma((2, 2, NCH, 2)),
            dma((2, NZ, 2)),
            dma((2, NZ, 2)),
            dma((2, 2, NCH, 2)),
            dma((2, 2, NCH, 2)),
            dma((NZ,)),
            dma((NZ,)),
            dma((8,)),
        ],
        compiler_params=pltpu.CompilerParams(
            collective_id=1, has_side_effects=True, vmem_limit_bytes=109 * 2**19
        ),
        name="any_couplings",
    )(coef, asrc, apair, alinks, bsrc, bpair, blinks, one_body)[0]


def on_device(
    coefficients,
    alpha_energy,
    beta_energy,
    one_body,
    alpha_source,
    alpha_pair,
    alpha_links,
    beta_source,
    beta_pair,
    beta_links,
):
    tables = (
        alpha_source.T,
        alpha_pair.T,
        alpha_links.transpose(1, 0, 2),
        beta_source.T,
        beta_pair.T,
        beta_links.transpose(1, 0, 2),
    )
    slots, fits = message_tables(tables[0])

    def with_slots():
        return named_sigma(coefficients, alpha_energy, beta_energy, one_body, *tables, slots)

    def without_slots():
        terms = any_couplings(coefficients, one_body, *tables)
        diagonal = (alpha_energy[:, None] + beta_energy[None, :]) * coefficients
        return diagonal + terms, jnp.zeros((4, 8, SB, SB), F32)

    return finish_sigma(*lax.cond(fits[0, 0] == 1, lambda: tuple(with_slots()), without_slots))


def solution(mesh):
    in_specs = (P("alpha", "beta"), P("alpha"), P("beta"), P(), P(), P(), P(), P(), P(), P())
    out_specs = P("alpha", "beta")
    return jax.shard_map(
        on_device, mesh=mesh, in_specs=in_specs, out_specs=out_specs, check_vma=False
    )
```

```python
import functools

import jax
import jax.numpy as jnp
from jax import lax
from jax.experimental import pallas as pl
from jax.experimental.pallas import tpu as pltpu
from jax.sharding import PartitionSpec as P

MESH = pl.DeviceIdType.MESH
F32, BF16 = jnp.float32, jnp.bfloat16
SB = 128
NCH = 4
NZ = 8
ROOMS = (12, 13)

LINK = (1, 3, 4, 12)


def link_of(o, i):
    return (o + i) % 4


def spans(links):
    found = [0]
    for link in links:
        found = found + [v ^ LINK[link] for v in found]
    return found


def reader_masks(o):
    last, third = LINK[link_of(o, 3)], LINK[link_of(o, 2)]
    return (0, last, third, third ^ last)


HOT_SLOT = {m: i for i, m in enumerate(sorted({m for o in range(4) for m in reader_masks(o)}))}


def table_kernel(source, slots, choice):
    me = lax.axis_index("alpha")

    def iota(shape, axis):
        return lax.broadcasted_iota(jnp.int32, shape, axis)

    def mask_of(order, i):
        link = (order + i) % 4
        return jnp.where(link == 0, 1, jnp.where(link == 1, 3, jnp.where(link == 2, 4, 12)))

    def ones(mask):
        return jnp.where(mask, 1.0, 0.0).astype(BF16)

    def dot(left, right, axis=0):
        return lax.dot_general(left, right, (((1,), (axis,)), ((), ())), preferred_element_type=F32)

    row, lane = iota((64, 128), 0), iota((64, 128), 1)
    order, sender = row // 16, row % 16
    m1, m2, m3, m4 = (mask_of(order, i) for i in range(4))
    apart = (lane >> 3) ^ sender
    reader = apart ^ m2
    two_readers = (reader == 0) | (reader == m3) | (reader == m4) | (reader == (m3 ^ m4))
    two_sources = (apart == 0) | (apart == m1)
    device = lane ^ sender
    three_sources = (device == 0) | (device == m1) | (device == m2) | (device == (m1 ^ m2))
    three_readers = (apart == m3) | (apart == (m3 ^ m4))
    which = iota((128, 128), 0)
    named, fed = which < 0, which < 0
    for k in range(3):
        line = source[k : k + 1, :]
        named = named | (line == which)
        fed = fed | ((line >> 3) == which)
    two = two_sources & (dot(ones(two_readers), ones(named), 1) > 0.5)
    three = three_readers & (dot(ones(three_sources), ones(fed)) > 0.5)
    before = ones(which < iota((128, 128), 1))
    row, lane = iota((8, 64), 0), iota((8, 64), 1)
    order = row % 4
    at = iota((8, 128), 1)
    most = jnp.int32(0)
    for stage, messages in enumerate((two, three)):
        node = jnp.where(row < 4, me, me ^ mask_of(order, stage + 1))
        mine = dot(ones(lane == order * 16 + node), ones(messages))
        rank = dot(mine.astype(BF16), before).astype(jnp.int32)
        here = mine > 0.5
        chosen = jnp.zeros((8, 128), jnp.int32)
        for s in range(ROOMS[-1]):
            block = jnp.sum(jnp.where(here & (rank == s), at, 0), axis=1, keepdims=True)
            chosen = jnp.where(at == s, block, chosen)
        got = jnp.where(here, jnp.minimum(rank, ROOMS[-1] - 1), -1)
        slots[stage] = jnp.where(iota((8, 128), 0) < 4, chosen, got)
        count = jnp.sum(jnp.where(messages, 1, 0), axis=1, keepdims=True)
        most = jnp.maximum(most, jnp.max(count))
    choice[0, 0] = sum(jnp.where(most > room, 1, 0) for room in ROOMS)


def message_tables(source):
    vmem = pl.BlockSpec(memory_space=pltpu.VMEM)
    return pl.pallas_call(
        table_kernel,
        out_shape=[
            jax.ShapeDtypeStruct((2, 8, 128), jnp.int32),
            jax.ShapeDtypeStruct((1, 1), jnp.int32),
        ],
        in_specs=[vmem],
        out_specs=[vmem, pl.BlockSpec(memory_space=pltpu.SMEM)],
        name="message_tables",
    )(source)


def named_kernel(
    room,
    coef,
    asrc,
    apair,
    alinks_hbm,
    bsrc,
    bpair,
    blinks_hbm,
    table,
    slots,
    energy_a,
    energy_b,
    out_hbm,
    tail,
    got1,
    got2,
    gz,
    gc,
    gf,
    got_b,
    out,
    alinks,
    blinks,
    stage,
    split,
    held,
    pack,
    part3,
    *rest,
):
    got3, rest = rest[:8], rest[8:]
    part4, got4, stage_b, split_b, part_b, hot, hot_b, rows_a, *rest = rest
    at_own, weight_own, at_sent, weight_sent, hot_sent, s_sem, r_sem, zs_sem, zr_sem, l_sem = rest
    a = lax.axis_index("alpha")
    b = lax.axis_index("beta")
    y, x, z, core = a // 4, a % 4, b // 2, b % 2

    def over(place, link):
        py, px = place
        if link == 0:
            return (py, px + 1 - 2 * (px % 2))
        if link == 1:
            return (py, 3 - px)
        if link == 2:
            return (py + 1 - 2 * (py % 2), px)
        return (3 - py, px)

    def index(place):
        return place[0] * 4 + place[1]

    def peer(link):
        return (index(over((y, x), link)), b)

    def over_z(pair):
        return z + 1 - 2 * (z % 2) if pair == 0 else 3 - z

    partner = (a, z * 2 + 1 - core)

    def choose(o, values):
        return jnp.where(
            o == 0, values[0], jnp.where(o == 1, values[1], jnp.where(o == 2, values[2], values[3]))
        )

    def each(o, act):
        for k in range(4):

            @pl.when(o == k)
            def _(k=k):
                act(k)

    def columns(w, o):
        return pl.ds(pl.multiple_of((w * 4 + o) * SB, SB), SB)

    def block(n):
        return pl.ds(pl.multiple_of(n * SB, SB), SB)

    def send(i, w, o):
        ch = w * 4 + o
        src = (coef.at[:, :, columns(w, o)], pack.at[ch], part3.at[ch], part4.at[ch])[i]
        if i == 2:
            dst = got3[ch]
        elif i == 3:
            dst = (got4, tail)[w].at[o]
        else:
            dst = (got1, got2)[i].at[ch]
        return pltpu.make_async_remote_copy(
            src_ref=src,
            dst_ref=dst,
            send_sem=s_sem.at[i, ch],
            recv_sem=r_sem.at[i, ch],
            device_id=peer(link_of(o, i)),
            device_id_type=MESH,
        )

    def blocks_b(h, c):
        return pl.ds(h * 4 + c * 2, 2)

    def send_z(h, c):
        return pltpu.make_async_remote_copy(
            src_ref=coef.at[blocks_b(h, c)],
            dst_ref=gz.at[blocks_b(h, c)],
            send_sem=zs_sem.at[0, h, c],
            recv_sem=zr_sem.at[0, h, c],
            device_id=(a, over_z(h) * 2 + core),
            device_id_type=MESH,
        )

    def send_c(h, c):
        return pltpu.make_async_remote_copy(
            src_ref=coef.at[blocks_b(h, c)],
            dst_ref=gc.at[blocks_b(h, c)],
            send_sem=zs_sem.at[1, h, c],
            recv_sem=zr_sem.at[1, h, c],
            device_id=partner,
            device_id_type=MESH,
        )

    def send_f(h, c):
        return pltpu.make_async_remote_copy(
            src_ref=gz.at[blocks_b(h, c)],
            dst_ref=gf.at[blocks_b(h, c)],
            send_sem=zs_sem.at[2, h, c],
            recv_sem=zr_sem.at[2, h, c],
            device_id=partner,
            device_id_type=MESH,
        )

    def send_b(h, c):
        return pltpu.make_async_remote_copy(
            src_ref=part_b.at[h],
            dst_ref=got_b.at[blocks_b(h, c)],
            send_sem=zs_sem.at[3, h, c],
            recv_sem=zr_sem.at[3, h, c],
            device_id=(a, over_z(1 - h) * 2 + core),
            device_id_type=MESH,
        )

    def integral(pair):
        p = pair // 18
        return table[p, pair - p * 18]

    def signed_hot(row):
        s = lax.broadcasted_iota(jnp.int32, (SB, SB), 0)
        return jnp.where(jnp.abs(row) - 1 == s, jnp.where(row > 0, 1.0, -1.0), 0.0)

    def pieces(v):
        hi = v.astype(BF16)
        return hi, (v - hi.astype(F32)).astype(BF16)

    def build_alpha():
        for mask, slot in HOT_SLOT.items():
            place = (y, x)
            for link in range(4):
                if mask & 3 == LINK[link] or mask & 12 == LINK[link]:
                    place = over(place, link)
            if mask & 3 == 2:
                place = over(over(place, 0), 1)
            if mask & 12 == 8:
                place = over(over(place, 2), 3)
            reader = index(place)

            def body(n, _, slot=slot, reader=reader):
                for k in range(3):
                    row = alinks[k, pl.ds(reader * 8 + n, 1), :]
                    hot[slot, k * 8 + n] = signed_hot(row).T.astype(BF16)
                return 0

            lax.fori_loop(0, 8, body, 0, unroll=4)

    def plan():
        def body(o, _):
            m1 = choose(o, [LINK[link_of(k, 0)] for k in range(4)])
            m2 = choose(o, [LINK[link_of(k, 1)] for k in range(4)])
            m3 = choose(o, [LINK[link_of(k, 2)] for k in range(4)])
            last = choose(o, [peer(link_of(k, 3))[0] for k in range(4)])
            hots = [
                choose(o, [HOT_SLOT[reader_masks(k)[role]] for k in range(4)])
                for role in range(2, 4)
            ]

            def entry(g, k):
                src = asrc[k, g]
                apart = (src >> 3) ^ a
                inner = src & 7
                over_two = (apart == m2) | (apart == (m1 ^ m2))
                here = over_two | (apart == 0) | (apart == m1)
                arrived = 16 + jnp.maximum(slots[0, 4 + o, src], 0)
                at = jnp.where(over_two, arrived, jnp.where(apart == m1, 8 + inner, inner))
                return at, jnp.where(here, integral(apair[k, g]), 0.0)

            def own_entries(n, _):
                for role, reader in enumerate((a, last)):
                    for k in range(3):
                        at, weight = entry(reader * 8 + n, k)
                        at_own[o, role * 24 + n * 3 + k] = at
                        weight_own[o, role * 24 + n * 3 + k] = weight
                return 0

            lax.fori_loop(0, 8, own_entries, 0)

            def sent_entries(s, _):
                g = slots[1, o, s]
                hot_sent[o, s] = jnp.where(((g >> 3) ^ a) == m3, hots[0], hots[1])
                hot_sent[o, room + s] = g & 7
                for k in range(3):
                    at, weight = entry(g, k)
                    at_sent[o, s * 3 + k] = at
                    weight_sent[o, s * 3 + k] = weight
                return 0

            lax.fori_loop(0, room, sent_entries, 0)
            return 0

        lax.fori_loop(0, 4, body, 0)

    def build_beta():
        for slot in range(3):
            reader = (z if slot == 0 else over_z(slot - 1)) * 2 + core

            def body(n, _, slot=slot, reader=reader):
                for k in range(3):
                    row = blinks[k, pl.ds(reader * 8 + n, 1), :]
                    hot_b[slot, n * 3 + k] = signed_hot(row).astype(BF16)
                return 0

            lax.fori_loop(0, 8, body, 0, unroll=4)

    def load(w, o, buf, second):
        copies = [
            pltpu.make_async_copy(
                coef.at[:, :, columns(w, o)], stage.at[buf, pl.ds(0, 8)], l_sem.at[buf, 0]
            ),
            pltpu.make_async_copy(
                got1.at[w * 4 + o], stage.at[buf, pl.ds(8, 8)], l_sem.at[buf, 1]
            ),
        ]
        if second:
            copies.append(
                pltpu.make_async_copy(
                    got2.at[w * 4 + o], stage.at[buf, pl.ds(16, room)], l_sem.at[buf, 2]
                )
            )
        return copies

    def start_load(w, o, second):
        for cp in load(w, o, o % 2, second):
            cp.start()

    def wait_load(w, o, second):
        for cp in load(w, o, o % 2, second):
            cp.wait()

    def ready(w, o, i):
        def first(k):
            if k == 0:
                send(i, w, 0).wait_recv()
                start_load(w, 0, i == 1)
            if k < 3:
                send(i, w, k + 1).wait_recv()
                start_load(w, k + 1, i == 1)
            wait_load(w, k, i == 1)

        each(o, first)

    def second_exchange(w):
        def body(o, _):
            ready(w, o, 0)
            buf = o % 2

            def hold(n, _):
                held[n] = stage[buf, n]
                return 0

            lax.fori_loop(0, 16, hold, 0, unroll=4)

            def fill(s, _):
                wanted = slots[0, o, s]
                at = jnp.where((wanted >> 3) == a, 0, 8) + (wanted & 7)
                pack[w * 4 + o, s] = held[at]
                return 0

            lax.fori_loop(0, room, fill, 0)
            each(o, lambda k: send(1, w, k).start())
            return 0

        lax.fori_loop(0, 4, body, 0)

    def third_exchange(w):
        def body(o, _):
            ready(w, o, 1)
            buf = o % 2
            ch = w * 4 + o
            hots = [
                choose(o, [HOT_SLOT[reader_masks(k)[role]] for k in range(4)]) for role in range(2)
            ]

            def split_body(n, _):
                hi, lo = pieces(stage[buf, n])
                split[n, 0:SB, :] = hi
                split[n, SB : 2 * SB, :] = lo
                return 0

            lax.fori_loop(0, 16 + room, split_body, 0, unroll=8)

            def product(at, w_k):
                return jnp.dot(
                    jnp.concatenate([w_k, w_k], axis=1), split[at], preferred_element_type=F32
                )

            def others(s, _):
                acc = jnp.zeros((SB, SB), F32)
                for k in range(3):
                    w_k = hot[hot_sent[o, s], k * 8 + hot_sent[o, room + s]]
                    acc += weight_sent[o, s * 3 + k] * product(at_sent[o, s * 3 + k], w_k)
                part3[ch, s] = acc
                return 0

            lax.fori_loop(0, room, others, 0, unroll=room)
            each(o, lambda k: send(2, w, k).start())

            def target(role, n):
                acc = jnp.zeros((SB, SB), F32)
                for k in range(3):
                    e = role * 24 + n * 3 + k
                    acc += weight_own[o, e] * product(at_own[o, e], hot[hots[role], k * 8 + n])
                return acc

            def mine(n, _):
                energy = rows_a[n] + energy_b[:, columns(w, o)]
                out[block(n), columns(w, o)] += energy * stage[buf, n] + target(0, n)
                return 0

            lax.fori_loop(0, 8, mine, 0, unroll=8)

            def across(n, _):
                part4[ch, n] = target(1, n)
                return 0

            lax.fori_loop(0, 8, across, 0, unroll=8)
            return 0

        lax.fori_loop(0, 4, body, 0)

    def fourth_exchange(w):
        for o in range(4):
            ch = w * 4 + o
            send(2, w, o).wait_recv()
            last = peer(link_of(o, 3))[0]

            def came(g, o=o, ch=ch):
                at = slots[1, 4 + o, g]
                return got3[ch][jnp.maximum(at, 0)] * jnp.where(at >= 0, 1.0, 0.0)

            def across(n, _, ch=ch, last=last, came=came):
                part4[ch, n] += came(last * 8 + n)
                return 0

            lax.fori_loop(0, 8, across, 0, unroll=2)
            send(3, w, o).start()

            def mine(n, _, o=o, came=came):
                out[block(n), columns(w, o)] += came(a * 8 + n)
                return 0

            lax.fori_loop(0, 8, mine, 0, unroll=2)

    def write(w):
        at = pl.ds(w * 512, 512)
        return pltpu.make_async_copy(out.at[:, at], out_hbm.at[:, at], l_sem.at[w, 3])

    def finish():
        for o in range(4):
            send(3, 0, o).wait_recv()

            def mine(n, _, o=o):
                out[block(n), columns(0, o)] += got4[o, n]
                return 0

            lax.fori_loop(0, 8, mine, 0, unroll=2)

    def compute_b(h, c):
        rows = pl.ds(h * 512 + c * 256, 256)
        send_c(h, c).wait_recv()
        send_f(h, c).wait_recv()
        sources = (coef, gc, gz, gf)
        copies = [
            pltpu.make_async_copy(sources[q].at[blocks_b(h, c)], stage_b.at[q % 2], l_sem.at[2 + q % 2, 0])
            for q in range(4)
        ]
        copies[0].start()
        copies[1].start()
        for q in range(4):
            copies[q].wait()

            def split_body(n, _, q=q):
                hi, lo = pieces(stage_b[q % 2, :, :, block(n)].reshape(256, SB))
                split_b[q * 8 + n, :, 0:SB] = hi
                split_b[q * 8 + n, :, SB : 2 * SB] = lo
                return 0

            lax.fori_loop(0, 8, split_body, 0, unroll=2)
            if q < 2:
                copies[q + 2].start()

        def target(reader, n, slot):
            g = reader * 8 + n
            acc = jnp.zeros((256, SB), F32)
            for k in range(3):
                src = bsrc[k, g]
                sz, sc = src >> 4, (src >> 3) & 1
                away = sz ^ z
                here = (away == 0) | (away == (1 if h == 0 else 3))
                at = jnp.where(away == 0, 0, 16) + jnp.where(sc == core, 0, 8) + (src & 7)
                weight = jnp.where(here, integral(bpair[k, g]), 0.0)
                w_k = hot_b[slot, n * 3 + k]
                acc += weight * jnp.dot(
                    split_b[at], jnp.concatenate([w_k, w_k], axis=0), preferred_element_type=F32
                )
            return acc

        def others(n, _):
            part_b[h, :, :, block(n)] = target(over_z(1 - h) * 2 + core, n, 2 - h).reshape(2, SB, SB)
            return 0

        if c == 1:
            send_b(h, 0).wait_send()
        lax.fori_loop(0, 8, others, 0, unroll=4)
        send_b(h, c).start()

        def mine(n, _):
            out[rows, block(n)] += target(b, n, 0)
            return 0

        lax.fori_loop(0, 8, mine, 0, unroll=4)

    def finish_b(h, c):
        send_b(h, c).wait_recv()
        cp = pltpu.make_async_copy(got_b.at[blocks_b(h, c)], stage_b.at[c], l_sem.at[2 + c, 1])
        cp.start()
        cp.wait()
        out[pl.ds(h * 512 + c * 256, 256), :] += stage_b[c].reshape(256, 1024)

    barrier = pltpu.get_barrier_semaphore()
    everyone = [peer(link) for link in range(4)]
    everyone += [(a, over_z(0) * 2 + core), (a, over_z(1) * 2 + core), partner]
    for device in everyone:
        pl.semaphore_signal(barrier, inc=1, device_id=device, device_id_type=MESH)
    pl.semaphore_wait(barrier, len(everyone))

    links = [
        pltpu.make_async_copy(alinks_hbm, alinks, l_sem.at[0, 4]),
        pltpu.make_async_copy(blinks_hbm, blinks, l_sem.at[1, 4]),
    ]
    for cp in links:
        cp.start()
    for w in range(2):
        for o in range(4):
            send(0, w, o).start()
    for c in range(2):
        for h in range(2):
            send_z(h, c).start()
            send_c(h, c).start()
    for cp in links:
        cp.wait()
    build_alpha()
    for n in range(8):
        rows_a[n] = jnp.broadcast_to(energy_a[n : n + 1, :], (SB, SB)).T
    out[...] = jnp.zeros_like(out)
    plan()
    second_exchange(0)
    build_beta()
    second_exchange(1)
    for h in range(2):
        send_z(h, 0).wait_recv()
        send_f(h, 0).start()
    for h in range(2):
        compute_b(h, 0)
    third_exchange(0)
    for h in range(2):
        send_z(h, 1).wait_recv()
        send_f(h, 1).start()
    third_exchange(1)
    for h in range(2):
        compute_b(h, 1)
    fourth_exchange(0)
    for h in range(2):
        finish_b(h, 0)
    fourth_exchange(1)
    for h in range(2):
        finish_b(h, 1)
    write(1).start()
    finish()
    write(0).start()
    for o in range(4):
        send(3, 1, o).wait_recv()
    for w in range(2):
        write(w).wait()
        for o in range(4):
            for i in range(4):
                send(i, w, o).wait_send()
    for c in range(2):
        for h in range(2):
            for copy in (send_z, send_c, send_f):
                copy(h, c).wait_send()
            if c == 1:
                send_b(h, c).wait_send()


def named_sigma(
    room, coef, energy_a, energy_b, one_body, asrc, apair, alinks, bsrc, bpair, blinks, slots
):
    hbm = pl.BlockSpec(memory_space=pl.ANY)
    smem = pl.BlockSpec(memory_space=pltpu.SMEM)
    vmem = pl.BlockSpec(memory_space=pltpu.VMEM)
    dma = pltpu.SemaphoreType.DMA
    whole = jax.ShapeDtypeStruct((8, SB, 1024), F32)
    return pl.pallas_call(
        functools.partial(named_kernel, room),
        out_shape=[
            jax.ShapeDtypeStruct((1024, 1024), F32),
            jax.ShapeDtypeStruct((4, 8, SB, SB), F32),
            jax.ShapeDtypeStruct((8, 8, SB, SB), F32),
            jax.ShapeDtypeStruct((8, room, SB, SB), F32),
            whole,
            whole,
            whole,
            whole,
        ],
        in_specs=[hbm, smem, smem, hbm, smem, smem, hbm, smem, smem, vmem, vmem],
        out_specs=[hbm] * 8,
        scratch_shapes=[
            pltpu.VMEM((1024, 1024), F32),
            pltpu.VMEM((3, 128, SB), jnp.int32),
            pltpu.VMEM((3, 64, SB), jnp.int32),
            pltpu.VMEM((2, 16 + room, SB, SB), F32),
            pltpu.VMEM((16 + room, 2 * SB, SB), BF16),
            pltpu.VMEM((16, SB, SB), F32),
            pltpu.VMEM((8, room, SB, SB), F32),
            pltpu.VMEM((8, room, SB, SB), F32),
            *[pltpu.VMEM((room, SB, SB), F32)] * 8,
            pltpu.VMEM((8, 8, SB, SB), F32),
            pltpu.VMEM((4, 8, SB, SB), F32),
            pltpu.VMEM((2, 2, SB, 1024), F32),
            pltpu.VMEM((32, 256, 2 * SB), BF16),
            pltpu.VMEM((2, 2, SB, 1024), F32),
            pltpu.VMEM((len(HOT_SLOT), 24, SB, SB), BF16),
            pltpu.VMEM((3, 24, SB, SB), BF16),
            pltpu.VMEM((8, SB, SB), F32),
            pltpu.SMEM((4, 48), jnp.int32),
            pltpu.SMEM((4, 48), F32),
            pltpu.SMEM((4, 3 * room), jnp.int32),
            pltpu.SMEM((4, 3 * room), F32),
            pltpu.SMEM((4, 2 * room), jnp.int32),
            dma((4, 8)),
            dma((4, 8)),
            dma((4, 2, 2)),
            dma((4, 2, 2)),
            dma((4, 5)),
        ],
        compiler_params=pltpu.CompilerParams(
            collective_id=ROOMS.index(room), has_side_effects=True, vmem_limit_bytes=109 * 2**19
        ),
        name=f"named_sigma_{room}",
    )(
        coef.reshape(8, SB, 1024),
        asrc,
        apair,
        alinks,
        bsrc,
        bpair,
        blinks,
        one_body,
        slots,
        energy_a.reshape(8, SB),
        energy_b.reshape(1, 1024),
    )[:2]


def finish_kernel(part, tail, sigma, half, sems):
    first = pl.ds(0, 512)
    copies = [pltpu.make_async_copy(part.at[:, first], sigma.at[:, first], sems.at[4])]
    copies[0].start()
    for o in range(4):
        at = pl.ds(512 + o * SB, SB)
        for n in range(8):
            rows = pl.ds(n * SB, SB)
            half[o, rows, :] = part[rows, at] + tail[o, n]
        copies.append(pltpu.make_async_copy(half.at[o], sigma.at[:, at], sems.at[o]))
        copies[-1].start()
    for copy in copies:
        copy.wait()


def finish_sigma(part, tail):
    vmem = pl.BlockSpec(memory_space=pltpu.VMEM)
    return pl.pallas_call(
        finish_kernel,
        out_shape=jax.ShapeDtypeStruct((1024, 1024), F32),
        in_specs=[vmem, vmem],
        out_specs=pl.BlockSpec(memory_space=pl.ANY),
        scratch_shapes=[pltpu.VMEM((4, 1024, SB), F32), pltpu.SemaphoreType.DMA((5,))],
        compiler_params=pltpu.CompilerParams(vmem_limit_bytes=16 * 2**20),
        name="finish_sigma",
    )(part, tail)


def any_kernel(
    coef,
    asrc,
    apair,
    alinks,
    bsrc,
    bpair,
    blinks,
    table,
    out,
    gx,
    gy,
    gz,
    stage,
    stage_b,
    split,
    split_b,
    part,
    far,
    near,
    core_out,
    core_in,
    hot,
    hot_b,
    g_send,
    g_recv,
    z_send,
    z_recv,
    r_send,
    r_recv,
    c_send,
    c_recv,
    l_sem,
):
    a = lax.axis_index("alpha")
    b = lax.axis_index("beta")
    y, x, z, core = a // 4, a % 4, b // 2, b % 2

    def step(axis, d):
        s = 1 if d == 0 else 3
        if axis == "x":
            return (y * 4 + (x + s) % 4, b)
        if axis == "y":
            return (((y + s) % 4) * 4 + x, b)
        return (a, ((z + s) % 4) * 2 + core)

    partner = (a, z * 2 + 1 - core)

    def cols(h, c):
        return pl.ds(pl.multiple_of(h * 512 + c * SB, SB), SB)

    axes = ("x", "y")
    bufs = (gx, gy)

    def own(h, c, d):
        return pltpu.make_async_remote_copy(
            src_ref=coef.at[:, cols(h, c)],
            dst_ref=bufs[h].at[2 if d == 0 else 0, c],
            send_sem=g_send.at[h, 0, c, d],
            recv_sem=g_recv.at[h, 0, c, d],
            device_id=step(axes[h], d),
            device_id_type=MESH,
        )

    def relay(h, c, d):
        rows = pl.ds(d * 512, 512)
        return pltpu.make_async_remote_copy(
            src_ref=bufs[h].at[2 if d == 0 else 0, c, rows],
            dst_ref=bufs[h].at[1, c, rows],
            send_sem=g_send.at[h, 1, c, d],
            recv_sem=g_recv.at[h, 1, c, d],
            device_id=step(axes[h], d),
            device_id_type=MESH,
        )

    def own_z(c, d):
        rows = pl.ds(pl.multiple_of(c * SB, SB), SB)
        return pltpu.make_async_remote_copy(
            src_ref=coef.at[rows],
            dst_ref=gz.at[2 if d == 0 else 0, rows],
            send_sem=z_send.at[0, c, d],
            recv_sem=z_recv.at[0, c, d],
            device_id=step("z", d),
            device_id_type=MESH,
        )

    def relay_z(c, d):
        rows = pl.ds(pl.multiple_of(c * SB + d * 64, 64), 64)
        return pltpu.make_async_remote_copy(
            src_ref=gz.at[2 if d == 0 else 0, rows],
            dst_ref=gz.at[1, rows],
            send_sem=z_send.at[1, c, d],
            recv_sem=z_recv.at[1, c, d],
            device_id=step("z", d),
            device_id_type=MESH,
        )

    def send_far(h, c, d):
        return pltpu.make_async_remote_copy(
            src_ref=part.at[h, c, 1, pl.ds(d * 512, 512)],
            dst_ref=far.at[h, c, d],
            send_sem=r_send.at[h, 0, c, d],
            recv_sem=r_recv.at[h, 0, c, d],
            device_id=step(axes[1 - h], d),
            device_id_type=MESH,
        )

    def send_near(h, c, d):
        return pltpu.make_async_remote_copy(
            src_ref=part.at[h, c, 0 if d == 0 else 2],
            dst_ref=near.at[h, c, d],
            send_sem=r_send.at[h, 1, c, d],
            recv_sem=r_recv.at[h, 1, c, d],
            device_id=step(axes[1 - h], d),
            device_id_type=MESH,
        )

    def send_core(c):
        return pltpu.make_async_remote_copy(
            src_ref=core_out.at[c],
            dst_ref=core_in.at[c],
            send_sem=c_send.at[c],
            recv_sem=c_recv.at[c],
            device_id=partner,
            device_id_type=MESH,
        )

    def integral(pair):
        p = pair // 18
        return table[p, pair - p * 18]

    def reader(h, q):
        if h == 0:
            return ((y + q) % 4) * 4 + x
        return y * 4 + (x + q) % 4

    def signed_hot(row):
        s = lax.broadcasted_iota(jnp.int32, (SB, SB), 0)
        return jnp.where(jnp.abs(row) - 1 == s, jnp.where(row > 0, 1.0, -1.0), 0.0)

    def build_alpha(h):
        def body(n, _):
            g = reader(h, n // 8) * 8 + n % 8
            for k in range(3):
                row = alinks[k, pl.ds(g, 1), :]
                hot[h, n * 3 + k] = signed_hot(row).T.astype(BF16)
            return 0

        lax.fori_loop(0, 32, body, 0)

    def build_beta():
        def body(n, _):
            g = (z * 2 + (core + n // 8) % 2) * 8 + n % 8
            for k in range(3):
                row = blinks[k, pl.ds(g, 1), :]
                hot_b[n * 3 + k] = signed_hot(row).astype(BF16)
            return 0

        lax.fori_loop(0, 16, body, 0)

    def pieces(v):
        hi = v.astype(BF16)
        return hi, (v - hi.astype(F32)).astype(BF16)

    def compute_alpha(h, c):
        copies = [pltpu.make_async_copy(coef.at[:, cols(h, c)], stage.at[0], l_sem.at[0])]
        for q in range(3):
            copies.append(
                pltpu.make_async_copy(bufs[h].at[q, c], stage.at[q + 1], l_sem.at[q + 1])
            )
        for cp in copies:
            cp.start()
        for cp in copies:
            cp.wait()

        def split_body(n, _):
            rows = pl.ds(pl.multiple_of((n % 8) * SB, SB), SB)
            hi, lo = pieces(stage[n // 8, rows, :])
            split[n, 0:SB, :] = hi
            split[n, SB : 2 * SB, :] = lo
            return 0

        lax.fori_loop(0, 32, split_body, 0, unroll=2)

        def target(n):
            g = reader(h, n // 8) * 8 + n % 8
            acc = jnp.zeros((SB, SB), F32)
            for k in range(3):
                src = asrc[k, g]
                sy, sx = (src >> 5) & 3, (src >> 3) & 3
                if h == 0:
                    here, q = sy == y, (sx - x) & 3
                else:
                    here, q = sx == x, (sy - y) & 3
                weight = jnp.where(here, integral(apair[k, g]), 0.0)
                w = hot[h, n * 3 + k]
                acc += weight * jnp.dot(
                    jnp.concatenate([w, w], axis=1),
                    split[q * 8 + (src & 7)],
                    preferred_element_type=F32,
                )
            return acc

        def mine(n, _):
            rows = pl.ds(pl.multiple_of(n * SB, SB), SB)
            out[rows, cols(h, c)] += target(n)
            return 0

        lax.fori_loop(0, 8, mine, 0, unroll=4)

        def others(n, _):
            rows = pl.ds(pl.multiple_of((n % 8) * SB, SB), SB)
            part[h, c, n // 8 - 1, rows, :] = target(n)
            return 0

        lax.fori_loop(8, 32, others, 0, unroll=4)

    def compute_beta(c):
        rows = pl.ds(pl.multiple_of(c * SB, SB), SB)
        copies = [pltpu.make_async_copy(coef.at[rows], stage_b.at[0], l_sem.at[4])]
        for q in range(3):
            copies.append(
                pltpu.make_async_copy(gz.at[q, rows], stage_b.at[q + 1], l_sem.at[q + 5])
            )
        for cp in copies:
            cp.start()
        for cp in copies:
            cp.wait()

        def split_body(n, _):
            hi, lo = pieces(stage_b[n // 8, :, pl.ds(pl.multiple_of((n % 8) * SB, SB), SB)])
            split_b[n, :, 0:SB] = hi
            split_b[n, :, SB : 2 * SB] = lo
            return 0

        lax.fori_loop(0, 32, split_body, 0, unroll=2)

        def target(n):
            g = (z * 2 + (core + n // 8) % 2) * 8 + n % 8
            acc = jnp.zeros((SB, SB), F32)
            for k in range(3):
                src = bsrc[k, g]
                sz, sc = (src >> 4) & 3, (src >> 3) & 1
                weight = jnp.where(sc == core, integral(bpair[k, g]), 0.0)
                w = hot_b[n * 3 + k]
                acc += weight * jnp.dot(
                    split_b[((sz - z) & 3) * 8 + (src & 7)],
                    jnp.concatenate([w, w], axis=0),
                    preferred_element_type=F32,
                )
            return acc

        def mine(n, _):
            at = pl.ds(pl.multiple_of(n * SB, SB), SB)
            out[rows, at] += target(n)
            return 0

        lax.fori_loop(0, 8, mine, 0, unroll=4)

        def others(n, _):
            at = pl.ds(pl.multiple_of((n - 8) * SB, SB), SB)
            core_out[c, :, at] = target(n)
            return 0

        lax.fori_loop(8, 16, others, 0, unroll=4)

    def pass_on(h, c):
        for d in range(2):
            send_far(h, c, d).wait_recv()
            slot = 0 if d == 0 else 2

            def body(n, _):
                rows = pl.ds(pl.multiple_of(d * 512 + n * SB, SB), SB)
                part[h, c, slot, rows, :] += far[h, c, d, pl.ds(pl.multiple_of(n * SB, SB), SB), :]
                return 0

            lax.fori_loop(0, 4, body, 0)
            send_near(h, c, d).start()

    def finish(h, c):
        for d in range(2):
            send_near(h, c, d).wait_recv()

        def body(n, _):
            rows = pl.ds(pl.multiple_of(n * SB, SB), SB)
            out[rows, cols(h, c)] += near[h, c, 0, rows, :] + near[h, c, 1, rows, :]
            return 0

        lax.fori_loop(0, 8, body, 0)

    def finish_core(c):
        send_core(c).wait_recv()
        rows = pl.ds(pl.multiple_of(c * SB, SB), SB)
        out[rows, :] += core_in[c]

    barrier = pltpu.get_barrier_semaphore()
    for axis in ("x", "y", "z"):
        for d in range(2):
            pl.semaphore_signal(barrier, inc=1, device_id=step(axis, d), device_id_type=MESH)
    pl.semaphore_signal(barrier, inc=1, device_id=partner, device_id_type=MESH)
    pl.semaphore_wait(barrier, 7)

    for c in range(2):
        for d in range(2):
            own(0, c, d).start()
            own(1, c, d).start()
            own_z(c, d).start()

    out[...] = jnp.zeros_like(out)
    build_alpha(0)

    def move_on(c):
        for h in range(2):
            for d in range(2):
                own(h, c, d).wait_recv()
                relay(h, c, d).start()

        @pl.when(c < NCH - 2)
        def _():
            for h in range(2):
                for d in range(2):
                    own(h, c + 2, d).start()

    def move_on_z(c):
        for d in range(2):
            own_z(c, d).wait_recv()
            relay_z(c, d).start()

        @pl.when(c < NZ - 2)
        def _():
            for d in range(2):
                own_z(c + 2, d).start()

    move_on(0)
    move_on_z(0)
    build_alpha(1)
    build_beta()

    def loop(t, _):
        @pl.when(t < NCH - 1)
        def _():
            move_on(t + 1)

        @pl.when(t < NZ - 1)
        def _():
            move_on_z(t + 1)

        @pl.when(t < NCH)
        def _():
            for h in range(2):
                for d in range(2):
                    relay(h, t, d).wait_recv()
                compute_alpha(h, t)

        @pl.when(t == 2)
        def _():
            for c in range(2):
                for h in range(2):
                    for d in range(2):
                        send_far(h, c, d).start()

        @pl.when((t >= 2) & (t < NCH))
        def _():
            for h in range(2):
                for d in range(2):
                    send_far(h, t, d).start()

        @pl.when((t >= 3) & (t < 7))
        def _():
            for h in range(2):
                pass_on(h, t - 3)

        for d in range(2):
            relay_z(t, d).wait_recv()
        compute_beta(t)
        send_core(t).start()

        @pl.when(t >= 6)
        def _():
            for h in range(2):
                finish(h, t - 6)

        @pl.when(t >= 1)
        def _():
            finish_core(t - 1)

        return 0

    lax.fori_loop(0, NZ, loop, 0)
    finish_core(NZ - 1)

    def last(c, _):
        for h in range(2):
            finish(h, c)
        return 0

    lax.fori_loop(2, NCH, last, 0)

    def drain(c, _):
        for h in range(2):
            for d in range(2):
                own(h, c, d).wait_send()
                relay(h, c, d).wait_send()
                send_far(h, c, d).wait_send()
                send_near(h, c, d).wait_send()
        return 0

    lax.fori_loop(0, NCH, drain, 0)

    def drain_z(c, _):
        for d in range(2):
            own_z(c, d).wait_send()
            relay_z(c, d).wait_send()
        send_core(c).wait_send()
        return 0

    lax.fori_loop(0, NZ, drain_z, 0)


def any_couplings(coef, one_body, asrc, apair, alinks, bsrc, bpair, blinks):
    hbm = pl.BlockSpec(memory_space=pl.ANY)
    vmem = pl.BlockSpec(memory_space=pltpu.VMEM)
    smem = pl.BlockSpec(memory_space=pltpu.SMEM)
    dma = pltpu.SemaphoreType.DMA
    return pl.pallas_call(
        any_kernel,
        out_shape=[
            jax.ShapeDtypeStruct((1024, 1024), F32),
            jax.ShapeDtypeStruct((3, NCH, 1024, SB), F32),
            jax.ShapeDtypeStruct((3, NCH, 1024, SB), F32),
            jax.ShapeDtypeStruct((3, 1024, 1024), F32),
        ],
        in_specs=[hbm, smem, smem, vmem, smem, smem, vmem, smem],
        out_specs=[vmem, hbm, hbm, hbm],
        scratch_shapes=[
            pltpu.VMEM((4, 1024, SB), F32),
            pltpu.VMEM((4, SB, 1024), F32),
            pltpu.VMEM((32, 2 * SB, SB), BF16),
            pltpu.VMEM((32, SB, 2 * SB), BF16),
            pltpu.VMEM((2, NCH, 3, 1024, SB), F32),
            pltpu.VMEM((2, NCH, 2, 512, SB), F32),
            pltpu.VMEM((2, NCH, 2, 1024, SB), F32),
            pltpu.VMEM((NZ, SB, 1024), F32),
            pltpu.VMEM((NZ, SB, 1024), F32),
            pltpu.VMEM((2, 96, SB, SB), BF16),
            pltpu.VMEM((48, SB, SB), BF16),
            dma((2, 2, NCH, 2)),
            dma((2, 2, NCH, 2)),
            dma((2, NZ, 2)),
            dma((2, NZ, 2)),
            dma((2, 2, NCH, 2)),
            dma((2, 2, NCH, 2)),
            dma((NZ,)),
            dma((NZ,)),
            dma((8,)),
        ],
        compiler_params=pltpu.CompilerParams(
            collective_id=len(ROOMS), has_side_effects=True, vmem_limit_bytes=109 * 2**19
        ),
        name="any_couplings",
    )(coef, asrc, apair, alinks, bsrc, bpair, blinks, one_body)[0]


def on_device(
    coefficients,
    alpha_energy,
    beta_energy,
    one_body,
    alpha_source,
    alpha_pair,
    alpha_links,
    beta_source,
    beta_pair,
    beta_links,
):
    tables = (
        alpha_source.T,
        alpha_pair.T,
        alpha_links.transpose(1, 0, 2),
        beta_source.T,
        beta_pair.T,
        beta_links.transpose(1, 0, 2),
    )
    slots, choice = message_tables(tables[0])

    def with_slots(room):
        return tuple(
            named_sigma(room, coefficients, alpha_energy, beta_energy, one_body, *tables, slots)
        )

    def without_slots():
        terms = any_couplings(coefficients, one_body, *tables)
        diagonal = (alpha_energy[:, None] + beta_energy[None, :]) * coefficients
        return diagonal + terms, jnp.zeros((4, 8, SB, SB), F32)

    branches = [functools.partial(with_slots, room) for room in ROOMS] + [without_slots]
    return finish_sigma(*lax.switch(choice[0, 0], branches))


def solution(mesh):
    in_specs = (P("alpha", "beta"), P("alpha"), P("beta"), P(), P(), P(), P(), P(), P(), P())
    out_specs = P("alpha", "beta")
    return jax.shard_map(
        on_device, mesh=mesh, in_specs=in_specs, out_specs=out_specs, check_vma=False
    )
```

```python
import functools

import jax
import jax.numpy as jnp
from jax import lax
from jax.experimental import pallas as pl
from jax.experimental.pallas import tpu as pltpu
from jax.sharding import PartitionSpec as P

MESH = pl.DeviceIdType.MESH
F32, BF16 = jnp.float32, jnp.bfloat16
SB = 128
NCH = 4
NZ = 8
ROOMS = (12, 13)

LINK = (1, 3, 4, 12)


def link_of(o, i):
    return (o + i) % 4


def spans(links):
    found = [0]
    for link in links:
        found = found + [v ^ LINK[link] for v in found]
    return found


def reader_masks(o):
    last, third = LINK[link_of(o, 3)], LINK[link_of(o, 2)]
    return (0, last, third, third ^ last)


HOT_SLOT = {m: i for i, m in enumerate(sorted({m for o in range(4) for m in reader_masks(o)}))}


def table_kernel(source, slots, choice):
    me = lax.axis_index("alpha")

    def iota(shape, axis):
        return lax.broadcasted_iota(jnp.int32, shape, axis)

    def mask_of(order, i):
        link = (order + i) % 4
        return jnp.where(link == 0, 1, jnp.where(link == 1, 3, jnp.where(link == 2, 4, 12)))

    def ones(mask):
        return jnp.where(mask, 1.0, 0.0).astype(BF16)

    def dot(left, right, axis=0):
        return lax.dot_general(left, right, (((1,), (axis,)), ((), ())), preferred_element_type=F32)

    row, lane = iota((64, 128), 0), iota((64, 128), 1)
    order, sender = row // 16, row % 16
    m1, m2, m3, m4 = (mask_of(order, i) for i in range(4))
    apart = (lane >> 3) ^ sender
    reader = apart ^ m2
    two_readers = (reader == 0) | (reader == m3) | (reader == m4) | (reader == (m3 ^ m4))
    two_sources = (apart == 0) | (apart == m1)
    device = lane ^ sender
    three_sources = (device == 0) | (device == m1) | (device == m2) | (device == (m1 ^ m2))
    three_readers = (apart == m3) | (apart == (m3 ^ m4))
    which = iota((128, 128), 0)
    named, fed = which < 0, which < 0
    for k in range(3):
        line = source[k : k + 1, :]
        named = named | (line == which)
        fed = fed | ((line >> 3) == which)
    two = two_sources & (dot(ones(two_readers), ones(named), 1) > 0.5)
    three = three_readers & (dot(ones(three_sources), ones(fed)) > 0.5)
    before = ones(which < iota((128, 128), 1))
    row, lane = iota((8, 64), 0), iota((8, 64), 1)
    order = row % 4
    at = iota((8, 128), 1)
    most = jnp.int32(0)
    for stage, messages in enumerate((two, three)):
        node = jnp.where(row < 4, me, me ^ mask_of(order, stage + 1))
        mine = dot(ones(lane == order * 16 + node), ones(messages))
        rank = dot(mine.astype(BF16), before).astype(jnp.int32)
        here = mine > 0.5
        chosen = jnp.zeros((8, 128), jnp.int32)
        for s in range(ROOMS[-1]):
            block = jnp.sum(jnp.where(here & (rank == s), at, 0), axis=1, keepdims=True)
            chosen = jnp.where(at == s, block, chosen)
        got = jnp.where(here, jnp.minimum(rank, ROOMS[-1] - 1), -1)
        slots[stage] = jnp.where(iota((8, 128), 0) < 4, chosen, got)
        count = jnp.sum(jnp.where(messages, 1, 0), axis=1, keepdims=True)
        most = jnp.maximum(most, jnp.max(count))
    choice[0, 0] = sum(jnp.where(most > room, 1, 0) for room in ROOMS)


def message_tables(source):
    vmem = pl.BlockSpec(memory_space=pltpu.VMEM)
    return pl.pallas_call(
        table_kernel,
        out_shape=[
            jax.ShapeDtypeStruct((2, 8, 128), jnp.int32),
            jax.ShapeDtypeStruct((1, 1), jnp.int32),
        ],
        in_specs=[vmem],
        out_specs=[vmem, pl.BlockSpec(memory_space=pltpu.SMEM)],
        name="message_tables",
    )(source)


def named_kernel(
    room,
    coef,
    asrc_hbm,
    apair_hbm,
    alinks_hbm,
    bsrc_hbm,
    bpair_hbm,
    blinks_hbm,
    table_hbm,
    slots_hbm,
    energy_a_hbm,
    energy_b_hbm,
    out_hbm,
    tail,
    got1,
    got2,
    gz,
    gc,
    gf,
    got_b,
    out,
    alinks,
    blinks,
    stage,
    split,
    held,
    pack,
    part3,
    *rest,
):
    got3, rest = rest[:8], rest[8:]
    part4, got4, stage_b, split_b, part_b, hot, hot_b, rows_a, *rest = rest
    at_own, weight_own, at_sent, weight_sent, hot_sent, *rest = rest
    asrc, apair, bsrc, bpair, table, slots, energy_a, energy_b, *rest = rest
    s_sem, r_sem, zs_sem, zr_sem, l_sem, t_sem = rest
    a = lax.axis_index("alpha")
    b = lax.axis_index("beta")
    y, x, z, core = a // 4, a % 4, b // 2, b % 2

    def over(place, link):
        py, px = place
        if link == 0:
            return (py, px + 1 - 2 * (px % 2))
        if link == 1:
            return (py, 3 - px)
        if link == 2:
            return (py + 1 - 2 * (py % 2), px)
        return (3 - py, px)

    def index(place):
        return place[0] * 4 + place[1]

    def peer(link):
        return (index(over((y, x), link)), b)

    def over_z(pair):
        return z + 1 - 2 * (z % 2) if pair == 0 else 3 - z

    partner = (a, z * 2 + 1 - core)

    def choose(o, values):
        return jnp.where(
            o == 0, values[0], jnp.where(o == 1, values[1], jnp.where(o == 2, values[2], values[3]))
        )

    def each(o, act):
        for k in range(4):

            @pl.when(o == k)
            def _(k=k):
                act(k)

    def columns(w, o):
        return pl.ds(pl.multiple_of((w * 4 + o) * SB, SB), SB)

    def block(n):
        return pl.ds(pl.multiple_of(n * SB, SB), SB)

    def send(i, w, o):
        ch = w * 4 + o
        src = (coef.at[:, :, columns(w, o)], pack.at[ch], part3.at[ch], part4.at[ch])[i]
        if i == 2:
            dst = got3[ch]
        elif i == 3:
            dst = (got4, tail)[w].at[o]
        else:
            dst = (got1, got2)[i].at[ch]
        return pltpu.make_async_remote_copy(
            src_ref=src,
            dst_ref=dst,
            send_sem=s_sem.at[i, ch],
            recv_sem=r_sem.at[i, ch],
            device_id=peer(link_of(o, i)),
            device_id_type=MESH,
        )

    def blocks_b(h, c):
        return pl.ds(h * 4 + c * 2, 2)

    def send_z(h, c):
        return pltpu.make_async_remote_copy(
            src_ref=coef.at[blocks_b(h, c)],
            dst_ref=gz.at[blocks_b(h, c)],
            send_sem=zs_sem.at[0, h, c],
            recv_sem=zr_sem.at[0, h, c],
            device_id=(a, over_z(h) * 2 + core),
            device_id_type=MESH,
        )

    def send_c(h, c):
        return pltpu.make_async_remote_copy(
            src_ref=coef.at[blocks_b(h, c)],
            dst_ref=gc.at[blocks_b(h, c)],
            send_sem=zs_sem.at[1, h, c],
            recv_sem=zr_sem.at[1, h, c],
            device_id=partner,
            device_id_type=MESH,
        )

    def send_f(h, c):
        return pltpu.make_async_remote_copy(
            src_ref=gz.at[blocks_b(h, c)],
            dst_ref=gf.at[blocks_b(h, c)],
            send_sem=zs_sem.at[2, h, c],
            recv_sem=zr_sem.at[2, h, c],
            device_id=partner,
            device_id_type=MESH,
        )

    def send_b(h, c):
        return pltpu.make_async_remote_copy(
            src_ref=part_b.at[h],
            dst_ref=got_b.at[blocks_b(h, c)],
            send_sem=zs_sem.at[3, h, c],
            recv_sem=zr_sem.at[3, h, c],
            device_id=(a, over_z(1 - h) * 2 + core),
            device_id_type=MESH,
        )

    def integral(pair):
        p = pair // 18
        return table[p, pair - p * 18]

    def signed_hot(row):
        s = lax.broadcasted_iota(jnp.int32, (SB, SB), 0)
        return jnp.where(jnp.abs(row) - 1 == s, jnp.where(row > 0, 1.0, -1.0), 0.0)

    def pieces(v):
        hi = v.astype(BF16)
        return hi, (v - hi.astype(F32)).astype(BF16)

    def build_alpha():
        for mask, slot in HOT_SLOT.items():
            place = (y, x)
            for link in range(4):
                if mask & 3 == LINK[link] or mask & 12 == LINK[link]:
                    place = over(place, link)
            if mask & 3 == 2:
                place = over(over(place, 0), 1)
            if mask & 12 == 8:
                place = over(over(place, 2), 3)
            reader = index(place)

            def body(n, _, slot=slot, reader=reader):
                for k in range(3):
                    row = alinks[k, pl.ds(reader * 8 + n, 1), :]
                    hot[slot, k * 8 + n] = signed_hot(row).T.astype(BF16)
                return 0

            lax.fori_loop(0, 8, body, 0, unroll=4)

    def plan():
        def body(o, _):
            m1 = choose(o, [LINK[link_of(k, 0)] for k in range(4)])
            m2 = choose(o, [LINK[link_of(k, 1)] for k in range(4)])
            m3 = choose(o, [LINK[link_of(k, 2)] for k in range(4)])
            last = choose(o, [peer(link_of(k, 3))[0] for k in range(4)])
            hots = [
                choose(o, [HOT_SLOT[reader_masks(k)[role]] for k in range(4)])
                for role in range(2, 4)
            ]

            def entry(g, k):
                src = asrc[k, g]
                apart = (src >> 3) ^ a
                inner = src & 7
                over_two = (apart == m2) | (apart == (m1 ^ m2))
                here = over_two | (apart == 0) | (apart == m1)
                arrived = 16 + jnp.maximum(slots[0, 4 + o, src], 0)
                at = jnp.where(over_two, arrived, jnp.where(apart == m1, 8 + inner, inner))
                return at, jnp.where(here, integral(apair[k, g]), 0.0)

            def own_entries(n, _):
                for role, reader in enumerate((a, last)):
                    for k in range(3):
                        at, weight = entry(reader * 8 + n, k)
                        at_own[o, role * 24 + n * 3 + k] = at
                        weight_own[o, role * 24 + n * 3 + k] = weight
                return 0

            lax.fori_loop(0, 8, own_entries, 0)

            def sent_entries(s, _):
                g = slots[1, o, s]
                hot_sent[o, s] = jnp.where(((g >> 3) ^ a) == m3, hots[0], hots[1])
                hot_sent[o, room + s] = g & 7
                for k in range(3):
                    at, weight = entry(g, k)
                    at_sent[o, s * 3 + k] = at
                    weight_sent[o, s * 3 + k] = weight
                return 0

            lax.fori_loop(0, room, sent_entries, 0)
            return 0

        lax.fori_loop(0, 4, body, 0)

    def build_beta():
        for slot in range(3):
            reader = (z if slot == 0 else over_z(slot - 1)) * 2 + core

            def body(n, _, slot=slot, reader=reader):
                for k in range(3):
                    row = blinks[k, pl.ds(reader * 8 + n, 1), :]
                    hot_b[slot, n * 3 + k] = signed_hot(row).astype(BF16)
                return 0

            lax.fori_loop(0, 8, body, 0, unroll=4)

    def load(w, o, buf, second):
        copies = [
            pltpu.make_async_copy(
                coef.at[:, :, columns(w, o)], stage.at[buf, pl.ds(0, 8)], l_sem.at[buf, 0]
            ),
            pltpu.make_async_copy(
                got1.at[w * 4 + o], stage.at[buf, pl.ds(8, 8)], l_sem.at[buf, 1]
            ),
        ]
        if second:
            copies.append(
                pltpu.make_async_copy(
                    got2.at[w * 4 + o], stage.at[buf, pl.ds(16, room)], l_sem.at[buf, 2]
                )
            )
        return copies

    def start_load(w, o, second):
        for cp in load(w, o, o % 2, second):
            cp.start()

    def wait_load(w, o, second):
        for cp in load(w, o, o % 2, second):
            cp.wait()

    def ready(w, o, i):
        def first(k):
            if k == 0:
                send(i, w, 0).wait_recv()
                start_load(w, 0, i == 1)
            if k < 3:
                send(i, w, k + 1).wait_recv()
                start_load(w, k + 1, i == 1)
            wait_load(w, k, i == 1)

        each(o, first)

    def second_exchange(w):
        def body(o, _):
            ready(w, o, 0)
            buf = o % 2

            def hold(n, _):
                held[n] = stage[buf, n]
                return 0

            lax.fori_loop(0, 16, hold, 0, unroll=4)

            def fill(s, _):
                wanted = slots[0, o, s]
                at = jnp.where((wanted >> 3) == a, 0, 8) + (wanted & 7)
                pack[w * 4 + o, s] = held[at]
                return 0

            lax.fori_loop(0, room, fill, 0)
            each(o, lambda k: send(1, w, k).start())
            return 0

        lax.fori_loop(0, 4, body, 0)

    def third_exchange(w):
        def body(o, _):
            ready(w, o, 1)
            buf = o % 2
            ch = w * 4 + o
            hots = [
                choose(o, [HOT_SLOT[reader_masks(k)[role]] for k in range(4)]) for role in range(2)
            ]

            def split_body(n, _):
                hi, lo = pieces(stage[buf, n])
                split[n, 0:SB, :] = hi
                split[n, SB : 2 * SB, :] = lo
                return 0

            lax.fori_loop(0, 16 + room, split_body, 0, unroll=8)

            def product(at, w_k):
                return jnp.dot(
                    jnp.concatenate([w_k, w_k], axis=1), split[at], preferred_element_type=F32
                )

            def others(s, _):
                acc = jnp.zeros((SB, SB), F32)
                for k in range(3):
                    w_k = hot[hot_sent[o, s], k * 8 + hot_sent[o, room + s]]
                    acc += weight_sent[o, s * 3 + k] * product(at_sent[o, s * 3 + k], w_k)
                part3[ch, s] = acc
                return 0

            lax.fori_loop(0, room, others, 0, unroll=room)
            each(o, lambda k: send(2, w, k).start())

            def target(role, n):
                acc = jnp.zeros((SB, SB), F32)
                for k in range(3):
                    e = role * 24 + n * 3 + k
                    acc += weight_own[o, e] * product(at_own[o, e], hot[hots[role], k * 8 + n])
                return acc

            def mine(n, _):
                energy = rows_a[n] + energy_b[:, columns(w, o)]
                out[block(n), columns(w, o)] += energy * stage[buf, n] + target(0, n)
                return 0

            lax.fori_loop(0, 8, mine, 0, unroll=8)

            def across(n, _):
                part4[ch, n] = target(1, n)
                return 0

            lax.fori_loop(0, 8, across, 0, unroll=8)
            return 0

        lax.fori_loop(0, 4, body, 0)

    def fourth_exchange(w):
        for o in range(4):
            ch = w * 4 + o
            send(2, w, o).wait_recv()
            last = peer(link_of(o, 3))[0]

            def came(g, o=o, ch=ch):
                at = slots[1, 4 + o, g]
                return got3[ch][jnp.maximum(at, 0)] * jnp.where(at >= 0, 1.0, 0.0)

            def across(n, _, ch=ch, last=last, came=came):
                part4[ch, n] += came(last * 8 + n)
                return 0

            lax.fori_loop(0, 8, across, 0, unroll=2)
            send(3, w, o).start()

            def mine(n, _, o=o, came=came):
                out[block(n), columns(w, o)] += came(a * 8 + n)
                return 0

            lax.fori_loop(0, 8, mine, 0, unroll=2)

    def write(w):
        at = pl.ds(w * 512, 512)
        return pltpu.make_async_copy(out.at[:, at], out_hbm.at[:, at], l_sem.at[w, 3])

    def finish():
        for o in range(4):
            send(3, 0, o).wait_recv()

            def mine(n, _, o=o):
                out[block(n), columns(0, o)] += got4[o, n]
                return 0

            lax.fori_loop(0, 8, mine, 0, unroll=2)

    def compute_b(h, c):
        rows = pl.ds(h * 512 + c * 256, 256)
        send_c(h, c).wait_recv()
        send_f(h, c).wait_recv()
        sources = (coef, gc, gz, gf)
        copies = [
            pltpu.make_async_copy(sources[q].at[blocks_b(h, c)], stage_b.at[q % 2], l_sem.at[2 + q % 2, 0])
            for q in range(4)
        ]
        copies[0].start()
        copies[1].start()
        for q in range(4):
            copies[q].wait()

            def split_body(n, _, q=q):
                hi, lo = pieces(stage_b[q % 2, :, :, block(n)].reshape(256, SB))
                split_b[q * 8 + n, :, 0:SB] = hi
                split_b[q * 8 + n, :, SB : 2 * SB] = lo
                return 0

            lax.fori_loop(0, 8, split_body, 0, unroll=2)
            if q < 2:
                copies[q + 2].start()

        def target(reader, n, slot):
            g = reader * 8 + n
            acc = jnp.zeros((256, SB), F32)
            for k in range(3):
                src = bsrc[k, g]
                sz, sc = src >> 4, (src >> 3) & 1
                away = sz ^ z
                here = (away == 0) | (away == (1 if h == 0 else 3))
                at = jnp.where(away == 0, 0, 16) + jnp.where(sc == core, 0, 8) + (src & 7)
                weight = jnp.where(here, integral(bpair[k, g]), 0.0)
                w_k = hot_b[slot, n * 3 + k]
                acc += weight * jnp.dot(
                    split_b[at], jnp.concatenate([w_k, w_k], axis=0), preferred_element_type=F32
                )
            return acc

        def others(n, _):
            part_b[h, :, :, block(n)] = target(over_z(1 - h) * 2 + core, n, 2 - h).reshape(2, SB, SB)
            return 0

        if c == 1:
            send_b(h, 0).wait_send()
        lax.fori_loop(0, 8, others, 0, unroll=4)
        send_b(h, c).start()

        def mine(n, _):
            out[rows, block(n)] += target(b, n, 0)
            return 0

        lax.fori_loop(0, 8, mine, 0, unroll=4)

    def finish_b(h, c):
        send_b(h, c).wait_recv()
        cp = pltpu.make_async_copy(got_b.at[blocks_b(h, c)], stage_b.at[c], l_sem.at[2 + c, 1])
        cp.start()
        cp.wait()
        out[pl.ds(h * 512 + c * 256, 256), :] += stage_b[c].reshape(256, 1024)

    barrier = pltpu.get_barrier_semaphore()
    everyone = [peer(link) for link in range(4)]
    everyone += [(a, over_z(0) * 2 + core), (a, over_z(1) * 2 + core), partner]
    for device in everyone:
        pl.semaphore_signal(barrier, inc=1, device_id=device, device_id_type=MESH)
    pl.semaphore_wait(barrier, len(everyone))

    small = (
        (alinks_hbm, alinks),
        (blinks_hbm, blinks),
        (asrc_hbm, asrc),
        (apair_hbm, apair),
        (bsrc_hbm, bsrc),
        (bpair_hbm, bpair),
        (table_hbm, table),
        (slots_hbm, slots),
        (energy_a_hbm, energy_a),
        (energy_b_hbm, energy_b),
    )
    links = [pltpu.make_async_copy(src, dst, t_sem.at[i]) for i, (src, dst) in enumerate(small)]
    for w in range(2):
        for o in range(4):
            send(0, w, o).start()
    for cp in links:
        cp.start()
    for c in range(2):
        for h in range(2):
            send_z(h, c).start()
            send_c(h, c).start()
    for cp in links:
        cp.wait()
    build_alpha()
    for n in range(8):
        rows_a[n] = jnp.broadcast_to(energy_a[n : n + 1, :], (SB, SB)).T
    out[...] = jnp.zeros_like(out)
    plan()
    second_exchange(0)
    build_beta()
    second_exchange(1)
    for h in range(2):
        send_z(h, 0).wait_recv()
        send_f(h, 0).start()
    for h in range(2):
        compute_b(h, 0)
    third_exchange(0)
    for h in range(2):
        send_z(h, 1).wait_recv()
        send_f(h, 1).start()
    third_exchange(1)
    for h in range(2):
        compute_b(h, 1)
    fourth_exchange(0)
    for h in range(2):
        finish_b(h, 0)
    fourth_exchange(1)
    for h in range(2):
        finish_b(h, 1)
    write(1).start()
    finish()
    write(0).start()
    for o in range(4):
        send(3, 1, o).wait_recv()
    for w in range(2):
        write(w).wait()
        for o in range(4):
            for i in range(4):
                send(i, w, o).wait_send()
    for c in range(2):
        for h in range(2):
            for copy in (send_z, send_c, send_f):
                copy(h, c).wait_send()
            if c == 1:
                send_b(h, c).wait_send()


def named_sigma(
    room, coef, energy_a, energy_b, one_body, asrc, apair, alinks, bsrc, bpair, blinks, slots
):
    hbm = pl.BlockSpec(memory_space=pl.ANY)
    dma = pltpu.SemaphoreType.DMA
    whole = jax.ShapeDtypeStruct((8, SB, 1024), F32)
    return pl.pallas_call(
        functools.partial(named_kernel, room),
        out_shape=[
            jax.ShapeDtypeStruct((1024, 1024), F32),
            jax.ShapeDtypeStruct((4, 8, SB, SB), F32),
            jax.ShapeDtypeStruct((8, 8, SB, SB), F32),
            jax.ShapeDtypeStruct((8, room, SB, SB), F32),
            whole,
            whole,
            whole,
            whole,
        ],
        in_specs=[hbm] * 11,
        out_specs=[hbm] * 8,
        scratch_shapes=[
            pltpu.VMEM((1024, 1024), F32),
            pltpu.VMEM((3, 128, SB), jnp.int32),
            pltpu.VMEM((3, 64, SB), jnp.int32),
            pltpu.VMEM((2, 16 + room, SB, SB), F32),
            pltpu.VMEM((16 + room, 2 * SB, SB), BF16),
            pltpu.VMEM((16, SB, SB), F32),
            pltpu.VMEM((8, room, SB, SB), F32),
            pltpu.VMEM((8, room, SB, SB), F32),
            *[pltpu.VMEM((room, SB, SB), F32)] * 8,
            pltpu.VMEM((8, 8, SB, SB), F32),
            pltpu.VMEM((4, 8, SB, SB), F32),
            pltpu.VMEM((2, 2, SB, 1024), F32),
            pltpu.VMEM((32, 256, 2 * SB), BF16),
            pltpu.VMEM((2, 2, SB, 1024), F32),
            pltpu.VMEM((len(HOT_SLOT), 24, SB, SB), BF16),
            pltpu.VMEM((3, 24, SB, SB), BF16),
            pltpu.VMEM((8, SB, SB), F32),
            pltpu.SMEM((4, 48), jnp.int32),
            pltpu.SMEM((4, 48), F32),
            pltpu.SMEM((4, 3 * room), jnp.int32),
            pltpu.SMEM((4, 3 * room), F32),
            pltpu.SMEM((4, 2 * room), jnp.int32),
            pltpu.SMEM((3, 128), jnp.int32),
            pltpu.SMEM((3, 128), jnp.int32),
            pltpu.SMEM((3, 64), jnp.int32),
            pltpu.SMEM((3, 64), jnp.int32),
            pltpu.SMEM((18, 18), F32),
            pltpu.SMEM((2, 8, 128), jnp.int32),
            pltpu.VMEM((8, SB), F32),
            pltpu.VMEM((1, 1024), F32),
            dma((4, 8)),
            dma((4, 8)),
            dma((4, 2, 2)),
            dma((4, 2, 2)),
            dma((4, 5)),
            dma((10,)),
        ],
        compiler_params=pltpu.CompilerParams(
            collective_id=ROOMS.index(room), has_side_effects=True, vmem_limit_bytes=109 * 2**19
        ),
        name=f"named_sigma_{room}",
    )(
        coef.reshape(8, SB, 1024),
        asrc,
        apair,
        alinks,
        bsrc,
        bpair,
        blinks,
        one_body,
        slots,
        energy_a.reshape(8, SB),
        energy_b.reshape(1, 1024),
    )[:2]


def finish_kernel(part, tail, sigma, half, sems):
    first = pl.ds(0, 512)
    copies = [pltpu.make_async_copy(part.at[:, first], sigma.at[:, first], sems.at[4])]
    copies[0].start()
    for o in range(4):
        at = pl.ds(512 + o * SB, SB)
        for n in range(8):
            rows = pl.ds(n * SB, SB)
            half[o, rows, :] = part[rows, at] + tail[o, n]
        copies.append(pltpu.make_async_copy(half.at[o], sigma.at[:, at], sems.at[o]))
        copies[-1].start()
    for copy in copies:
        copy.wait()


def finish_sigma(part, tail):
    vmem = pl.BlockSpec(memory_space=pltpu.VMEM)
    return pl.pallas_call(
        finish_kernel,
        out_shape=jax.ShapeDtypeStruct((1024, 1024), F32),
        in_specs=[vmem, vmem],
        out_specs=pl.BlockSpec(memory_space=pl.ANY),
        scratch_shapes=[pltpu.VMEM((4, 1024, SB), F32), pltpu.SemaphoreType.DMA((5,))],
        compiler_params=pltpu.CompilerParams(vmem_limit_bytes=16 * 2**20),
        name="finish_sigma",
    )(part, tail)


def any_kernel(
    coef,
    asrc,
    apair,
    alinks,
    bsrc,
    bpair,
    blinks,
    table,
    out,
    gx,
    gy,
    gz,
    stage,
    stage_b,
    split,
    split_b,
    part,
    far,
    near,
    core_out,
    core_in,
    hot,
    hot_b,
    g_send,
    g_recv,
    z_send,
    z_recv,
    r_send,
    r_recv,
    c_send,
    c_recv,
    l_sem,
):
    a = lax.axis_index("alpha")
    b = lax.axis_index("beta")
    y, x, z, core = a // 4, a % 4, b // 2, b % 2

    def step(axis, d):
        s = 1 if d == 0 else 3
        if axis == "x":
            return (y * 4 + (x + s) % 4, b)
        if axis == "y":
            return (((y + s) % 4) * 4 + x, b)
        return (a, ((z + s) % 4) * 2 + core)

    partner = (a, z * 2 + 1 - core)

    def cols(h, c):
        return pl.ds(pl.multiple_of(h * 512 + c * SB, SB), SB)

    axes = ("x", "y")
    bufs = (gx, gy)

    def own(h, c, d):
        return pltpu.make_async_remote_copy(
            src_ref=coef.at[:, cols(h, c)],
            dst_ref=bufs[h].at[2 if d == 0 else 0, c],
            send_sem=g_send.at[h, 0, c, d],
            recv_sem=g_recv.at[h, 0, c, d],
            device_id=step(axes[h], d),
            device_id_type=MESH,
        )

    def relay(h, c, d):
        rows = pl.ds(d * 512, 512)
        return pltpu.make_async_remote_copy(
            src_ref=bufs[h].at[2 if d == 0 else 0, c, rows],
            dst_ref=bufs[h].at[1, c, rows],
            send_sem=g_send.at[h, 1, c, d],
            recv_sem=g_recv.at[h, 1, c, d],
            device_id=step(axes[h], d),
            device_id_type=MESH,
        )

    def own_z(c, d):
        rows = pl.ds(pl.multiple_of(c * SB, SB), SB)
        return pltpu.make_async_remote_copy(
            src_ref=coef.at[rows],
            dst_ref=gz.at[2 if d == 0 else 0, rows],
            send_sem=z_send.at[0, c, d],
            recv_sem=z_recv.at[0, c, d],
            device_id=step("z", d),
            device_id_type=MESH,
        )

    def relay_z(c, d):
        rows = pl.ds(pl.multiple_of(c * SB + d * 64, 64), 64)
        return pltpu.make_async_remote_copy(
            src_ref=gz.at[2 if d == 0 else 0, rows],
            dst_ref=gz.at[1, rows],
            send_sem=z_send.at[1, c, d],
            recv_sem=z_recv.at[1, c, d],
            device_id=step("z", d),
            device_id_type=MESH,
        )

    def send_far(h, c, d):
        return pltpu.make_async_remote_copy(
            src_ref=part.at[h, c, 1, pl.ds(d * 512, 512)],
            dst_ref=far.at[h, c, d],
            send_sem=r_send.at[h, 0, c, d],
            recv_sem=r_recv.at[h, 0, c, d],
            device_id=step(axes[1 - h], d),
            device_id_type=MESH,
        )

    def send_near(h, c, d):
        return pltpu.make_async_remote_copy(
            src_ref=part.at[h, c, 0 if d == 0 else 2],
            dst_ref=near.at[h, c, d],
            send_sem=r_send.at[h, 1, c, d],
            recv_sem=r_recv.at[h, 1, c, d],
            device_id=step(axes[1 - h], d),
            device_id_type=MESH,
        )

    def send_core(c):
        return pltpu.make_async_remote_copy(
            src_ref=core_out.at[c],
            dst_ref=core_in.at[c],
            send_sem=c_send.at[c],
            recv_sem=c_recv.at[c],
            device_id=partner,
            device_id_type=MESH,
        )

    def integral(pair):
        p = pair // 18
        return table[p, pair - p * 18]

    def reader(h, q):
        if h == 0:
            return ((y + q) % 4) * 4 + x
        return y * 4 + (x + q) % 4

    def signed_hot(row):
        s = lax.broadcasted_iota(jnp.int32, (SB, SB), 0)
        return jnp.where(jnp.abs(row) - 1 == s, jnp.where(row > 0, 1.0, -1.0), 0.0)

    def build_alpha(h):
        def body(n, _):
            g = reader(h, n // 8) * 8 + n % 8
            for k in range(3):
                row = alinks[k, pl.ds(g, 1), :]
                hot[h, n * 3 + k] = signed_hot(row).T.astype(BF16)
            return 0

        lax.fori_loop(0, 32, body, 0)

    def build_beta():
        def body(n, _):
            g = (z * 2 + (core + n // 8) % 2) * 8 + n % 8
            for k in range(3):
                row = blinks[k, pl.ds(g, 1), :]
                hot_b[n * 3 + k] = signed_hot(row).astype(BF16)
            return 0

        lax.fori_loop(0, 16, body, 0)

    def pieces(v):
        hi = v.astype(BF16)
        return hi, (v - hi.astype(F32)).astype(BF16)

    def compute_alpha(h, c):
        copies = [pltpu.make_async_copy(coef.at[:, cols(h, c)], stage.at[0], l_sem.at[0])]
        for q in range(3):
            copies.append(
                pltpu.make_async_copy(bufs[h].at[q, c], stage.at[q + 1], l_sem.at[q + 1])
            )
        for cp in copies:
            cp.start()
        for cp in copies:
            cp.wait()

        def split_body(n, _):
            rows = pl.ds(pl.multiple_of((n % 8) * SB, SB), SB)
            hi, lo = pieces(stage[n // 8, rows, :])
            split[n, 0:SB, :] = hi
            split[n, SB : 2 * SB, :] = lo
            return 0

        lax.fori_loop(0, 32, split_body, 0, unroll=2)

        def target(n):
            g = reader(h, n // 8) * 8 + n % 8
            acc = jnp.zeros((SB, SB), F32)
            for k in range(3):
                src = asrc[k, g]
                sy, sx = (src >> 5) & 3, (src >> 3) & 3
                if h == 0:
                    here, q = sy == y, (sx - x) & 3
                else:
                    here, q = sx == x, (sy - y) & 3
                weight = jnp.where(here, integral(apair[k, g]), 0.0)
                w = hot[h, n * 3 + k]
                acc += weight * jnp.dot(
                    jnp.concatenate([w, w], axis=1),
                    split[q * 8 + (src & 7)],
                    preferred_element_type=F32,
                )
            return acc

        def mine(n, _):
            rows = pl.ds(pl.multiple_of(n * SB, SB), SB)
            out[rows, cols(h, c)] += target(n)
            return 0

        lax.fori_loop(0, 8, mine, 0, unroll=4)

        def others(n, _):
            rows = pl.ds(pl.multiple_of((n % 8) * SB, SB), SB)
            part[h, c, n // 8 - 1, rows, :] = target(n)
            return 0

        lax.fori_loop(8, 32, others, 0, unroll=4)

    def compute_beta(c):
        rows = pl.ds(pl.multiple_of(c * SB, SB), SB)
        copies = [pltpu.make_async_copy(coef.at[rows], stage_b.at[0], l_sem.at[4])]
        for q in range(3):
            copies.append(
                pltpu.make_async_copy(gz.at[q, rows], stage_b.at[q + 1], l_sem.at[q + 5])
            )
        for cp in copies:
            cp.start()
        for cp in copies:
            cp.wait()

        def split_body(n, _):
            hi, lo = pieces(stage_b[n // 8, :, pl.ds(pl.multiple_of((n % 8) * SB, SB), SB)])
            split_b[n, :, 0:SB] = hi
            split_b[n, :, SB : 2 * SB] = lo
            return 0

        lax.fori_loop(0, 32, split_body, 0, unroll=2)

        def target(n):
            g = (z * 2 + (core + n // 8) % 2) * 8 + n % 8
            acc = jnp.zeros((SB, SB), F32)
            for k in range(3):
                src = bsrc[k, g]
                sz, sc = (src >> 4) & 3, (src >> 3) & 1
                weight = jnp.where(sc == core, integral(bpair[k, g]), 0.0)
                w = hot_b[n * 3 + k]
                acc += weight * jnp.dot(
                    split_b[((sz - z) & 3) * 8 + (src & 7)],
                    jnp.concatenate([w, w], axis=0),
                    preferred_element_type=F32,
                )
            return acc

        def mine(n, _):
            at = pl.ds(pl.multiple_of(n * SB, SB), SB)
            out[rows, at] += target(n)
            return 0

        lax.fori_loop(0, 8, mine, 0, unroll=4)

        def others(n, _):
            at = pl.ds(pl.multiple_of((n - 8) * SB, SB), SB)
            core_out[c, :, at] = target(n)
            return 0

        lax.fori_loop(8, 16, others, 0, unroll=4)

    def pass_on(h, c):
        for d in range(2):
            send_far(h, c, d).wait_recv()
            slot = 0 if d == 0 else 2

            def body(n, _):
                rows = pl.ds(pl.multiple_of(d * 512 + n * SB, SB), SB)
                part[h, c, slot, rows, :] += far[h, c, d, pl.ds(pl.multiple_of(n * SB, SB), SB), :]
                return 0

            lax.fori_loop(0, 4, body, 0)
            send_near(h, c, d).start()

    def finish(h, c):
        for d in range(2):
            send_near(h, c, d).wait_recv()

        def body(n, _):
            rows = pl.ds(pl.multiple_of(n * SB, SB), SB)
            out[rows, cols(h, c)] += near[h, c, 0, rows, :] + near[h, c, 1, rows, :]
            return 0

        lax.fori_loop(0, 8, body, 0)

    def finish_core(c):
        send_core(c).wait_recv()
        rows = pl.ds(pl.multiple_of(c * SB, SB), SB)
        out[rows, :] += core_in[c]

    barrier = pltpu.get_barrier_semaphore()
    for axis in ("x", "y", "z"):
        for d in range(2):
            pl.semaphore_signal(barrier, inc=1, device_id=step(axis, d), device_id_type=MESH)
    pl.semaphore_signal(barrier, inc=1, device_id=partner, device_id_type=MESH)
    pl.semaphore_wait(barrier, 7)

    for c in range(2):
        for d in range(2):
            own(0, c, d).start()
            own(1, c, d).start()
            own_z(c, d).start()

    out[...] = jnp.zeros_like(out)
    build_alpha(0)

    def move_on(c):
        for h in range(2):
            for d in range(2):
                own(h, c, d).wait_recv()
                relay(h, c, d).start()

        @pl.when(c < NCH - 2)
        def _():
            for h in range(2):
                for d in range(2):
                    own(h, c + 2, d).start()

    def move_on_z(c):
        for d in range(2):
            own_z(c, d).wait_recv()
            relay_z(c, d).start()

        @pl.when(c < NZ - 2)
        def _():
            for d in range(2):
                own_z(c + 2, d).start()

    move_on(0)
    move_on_z(0)
    build_alpha(1)
    build_beta()

    def loop(t, _):
        @pl.when(t < NCH - 1)
        def _():
            move_on(t + 1)

        @pl.when(t < NZ - 1)
        def _():
            move_on_z(t + 1)

        @pl.when(t < NCH)
        def _():
            for h in range(2):
                for d in range(2):
                    relay(h, t, d).wait_recv()
                compute_alpha(h, t)

        @pl.when(t == 2)
        def _():
            for c in range(2):
                for h in range(2):
                    for d in range(2):
                        send_far(h, c, d).start()

        @pl.when((t >= 2) & (t < NCH))
        def _():
            for h in range(2):
                for d in range(2):
                    send_far(h, t, d).start()

        @pl.when((t >= 3) & (t < 7))
        def _():
            for h in range(2):
                pass_on(h, t - 3)

        for d in range(2):
            relay_z(t, d).wait_recv()
        compute_beta(t)
        send_core(t).start()

        @pl.when(t >= 6)
        def _():
            for h in range(2):
                finish(h, t - 6)

        @pl.when(t >= 1)
        def _():
            finish_core(t - 1)

        return 0

    lax.fori_loop(0, NZ, loop, 0)
    finish_core(NZ - 1)

    def last(c, _):
        for h in range(2):
            finish(h, c)
        return 0

    lax.fori_loop(2, NCH, last, 0)

    def drain(c, _):
        for h in range(2):
            for d in range(2):
                own(h, c, d).wait_send()
                relay(h, c, d).wait_send()
                send_far(h, c, d).wait_send()
                send_near(h, c, d).wait_send()
        return 0

    lax.fori_loop(0, NCH, drain, 0)

    def drain_z(c, _):
        for d in range(2):
            own_z(c, d).wait_send()
            relay_z(c, d).wait_send()
        send_core(c).wait_send()
        return 0

    lax.fori_loop(0, NZ, drain_z, 0)


def any_couplings(coef, one_body, asrc, apair, alinks, bsrc, bpair, blinks):
    hbm = pl.BlockSpec(memory_space=pl.ANY)
    vmem = pl.BlockSpec(memory_space=pltpu.VMEM)
    smem = pl.BlockSpec(memory_space=pltpu.SMEM)
    dma = pltpu.SemaphoreType.DMA
    return pl.pallas_call(
        any_kernel,
        out_shape=[
            jax.ShapeDtypeStruct((1024, 1024), F32),
            jax.ShapeDtypeStruct((3, NCH, 1024, SB), F32),
            jax.ShapeDtypeStruct((3, NCH, 1024, SB), F32),
            jax.ShapeDtypeStruct((3, 1024, 1024), F32),
        ],
        in_specs=[hbm, smem, smem, vmem, smem, smem, vmem, smem],
        out_specs=[vmem, hbm, hbm, hbm],
        scratch_shapes=[
            pltpu.VMEM((4, 1024, SB), F32),
            pltpu.VMEM((4, SB, 1024), F32),
            pltpu.VMEM((32, 2 * SB, SB), BF16),
            pltpu.VMEM((32, SB, 2 * SB), BF16),
            pltpu.VMEM((2, NCH, 3, 1024, SB), F32),
            pltpu.VMEM((2, NCH, 2, 512, SB), F32),
            pltpu.VMEM((2, NCH, 2, 1024, SB), F32),
            pltpu.VMEM((NZ, SB, 1024), F32),
            pltpu.VMEM((NZ, SB, 1024), F32),
            pltpu.VMEM((2, 96, SB, SB), BF16),
            pltpu.VMEM((48, SB, SB), BF16),
            dma((2, 2, NCH, 2)),
            dma((2, 2, NCH, 2)),
            dma((2, NZ, 2)),
            dma((2, NZ, 2)),
            dma((2, 2, NCH, 2)),
            dma((2, 2, NCH, 2)),
            dma((NZ,)),
            dma((NZ,)),
            dma((8,)),
        ],
        compiler_params=pltpu.CompilerParams(
            collective_id=len(ROOMS), has_side_effects=True, vmem_limit_bytes=109 * 2**19
        ),
        name="any_couplings",
    )(coef, asrc, apair, alinks, bsrc, bpair, blinks, one_body)[0]


def on_device(
    coefficients,
    alpha_energy,
    beta_energy,
    one_body,
    alpha_source,
    alpha_pair,
    alpha_links,
    beta_source,
    beta_pair,
    beta_links,
):
    tables = (
        alpha_source.T,
        alpha_pair.T,
        alpha_links.transpose(1, 0, 2),
        beta_source.T,
        beta_pair.T,
        beta_links.transpose(1, 0, 2),
    )
    slots, choice = message_tables(tables[0])

    def with_slots(room):
        return tuple(
            named_sigma(room, coefficients, alpha_energy, beta_energy, one_body, *tables, slots)
        )

    def without_slots():
        terms = any_couplings(coefficients, one_body, *tables)
        diagonal = (alpha_energy[:, None] + beta_energy[None, :]) * coefficients
        return diagonal + terms, jnp.zeros((4, 8, SB, SB), F32)

    branches = [functools.partial(with_slots, room) for room in ROOMS] + [without_slots]
    return finish_sigma(*lax.switch(choice[0, 0], branches))


def solution(mesh):
    in_specs = (P("alpha", "beta"), P("alpha"), P("beta"), P(), P(), P(), P(), P(), P(), P())
    out_specs = P("alpha", "beta")
    return jax.shard_map(
        on_device, mesh=mesh, in_specs=in_specs, out_specs=out_specs, check_vma=False
    )
```
